32 devices in a mesh: rng: 4 (over y, x), az: 8 (over z, core).
Axes of the slice: x: 2, y: 2, z: 4, core: 2. Of those that a mesh axis runs over, the one named last changes fastest.
Arguments:
- raw_echo: float32 [2, 16384, 4096], P(None, 'az', 'rng'), may hold values from -6 to 6
- chirp_spectrum: float32 [2, 4096], replicated, may hold values from -6 to 6
- azimuth_rate: float32 [4096], P(('rng', 'az')), may hold values from 100 to 400
- shift_table: int32 [16, 4096], P(None, ('rng', 'az')), may hold values from -28 to 29
- filter_index: int32 [16, 4096], P(None, ('rng', 'az')), may hold values from 0 to 15
- tap_table: float32 [16, 8], replicated, may hold values from -3 to 3
Outputs:
- image_out: float32 [2, 4096, 16384], P(None, ('rng', 'az'))
The draws below stay inside these ranges and needn't reach their ends.
All inputs are finite; a program needn't handle non-finite values.
Results may differ from the reference program's by a relative error of at most 0.0003.
Values sent between devices are 32-bit elements; how exact they have to be, the bound alone decides.
No kernel may reach another device: no remote copies, remote signals or barrier semaphores. Data moves between devices by JAX's collectives and lax.ppermute only.
A program may use at most 128 MiB of HBM per device.

```python
import math
import jax
import jax.numpy as jnp
from jax import lax

NRG = 4096
NAZ = 16384
GROUPS = 16
NFILT = 16
TAPS = 8
HALO = 32


def touch_ends(result, key, smallest, top_value):
    index_at = [jax.random.randint(jax.random.fold_in(key, axis), (), 0, length) for axis, length in enumerate(result.shape)]
    longest = result.shape.index(max(result.shape))
    next_to = index_at[:longest] + [(index_at[longest] + 1) % result.shape[longest]] + index_at[longest + 1:]
    return result.at[tuple(index_at)].set(smallest).at[tuple(next_to)].set(top_value)


def block_scale(rng, shape, shards, smallest, top_value):
    loudness = 1.0
    for position, shards_of in shards:
        steps = jax.random.uniform(jax.random.fold_in(jax.random.fold_in(rng, 6), position), (shards_of,), jnp.float32, smallest / len(shards), top_value / len(shards))
        loudness = loudness * jnp.repeat(jnp.exp(steps), shape[position] // shards_of).reshape((-1,) + (1,) * (len(shape) - 1 - position))
    return loudness


def scatter_about(key, dims, deviation, reach, cuts=(), held_as=jnp.bfloat16):
    result = jax.random.normal(key, dims, jnp.float32) * deviation
    if len(cuts) > 0:
        result = block_scale(key, dims, cuts, -0.22, 0.18) * result
    return jnp.clip(result, min=-reach, max=reach).astype(held_as)


def setup_inputs(seed: int = 0) -> dict:
    seeds = jax.random.split(jax.random.key(seed), 7)
    return {
        "raw_echo": scatter_about(seeds[0], (2, NAZ, NRG), 1.0, 6.0, ((1, 8), (2, 4)), jnp.float32),
        "chirp_spectrum": scatter_about(seeds[1], (2, NRG), 1.0, 6.0, (), jnp.float32),
        "azimuth_rate": jnp.clip(jnp.exp(math.log(400.0) - 1.3862944 * jax.random.uniform(seeds[2], (NRG,), jnp.float32) ** block_scale(seeds[2], (NRG,), ((0, 32),), -0.2, 0.2)), 100.0, 400.0),
        "shift_table": touch_ends(jax.random.randint(seeds[3], (GROUPS, NRG), 4 - HALO, HALO - 2), jax.random.fold_in(seeds[3], 1), 4 - HALO, (HALO - 2) - 1).astype(jnp.int32),
        "filter_index": touch_ends(jax.random.randint(seeds[4], (GROUPS, NRG), 0, NFILT), jax.random.fold_in(seeds[4], 1), 0, NFILT - 1).astype(jnp.int32),
        "tap_table": scatter_about(seeds[5], (NFILT, TAPS), 0.35, 3.0, (), jnp.float32),
    }


def reference(raw_echo, chirp_spectrum, azimuth_rate, shift_table, filter_index, tap_table):
    echo_data = lax.complex(raw_echo[0], raw_echo[1])
    chirp_ref = lax.complex(chirp_spectrum[0], chirp_spectrum[1])
    compressed = jnp.fft.ifft(jnp.fft.fft(echo_data, axis=1) * chirp_ref[None, :], axis=1)
    doppler = jnp.fft.fft(compressed, axis=0).T
    padded = jnp.pad(doppler, ((HALO, HALO), (0, 0)))
    band_len = NAZ // GROUPS
    weights = tap_table[filter_index]
    bin_ids = jnp.arange(NRG, dtype=jnp.int32)

    def one_band(band_id):
        band_data = lax.dynamic_slice_in_dim(padded, band_id * band_len, band_len, 1)
        band_weights = weights[band_id]
        band_shift = shift_table[band_id]
        summed = jnp.zeros((NRG, band_len), doppler.dtype)
        for tap_id in range(TAPS):
            source = bin_ids + band_shift + (tap_id - 4 + HALO)
            summed = summed + band_weights[:, tap_id][:, None] * band_data[source]
        return summed

    migrated = lax.map(one_band, jnp.arange(GROUPS, dtype=jnp.int32))
    migrated = migrated.transpose(1, 0, 2).reshape(NRG, NAZ)
    freq_ids = jnp.arange(NAZ, dtype=jnp.int32)
    centred = ((freq_ids + NAZ // 2) % NAZ - NAZ // 2).astype(jnp.float32) / NAZ
    phase_map = (jnp.pi * azimuth_rate)[:, None] * (centred * centred)[None, :]
    focused = migrated * lax.complex(jnp.cos(phase_map), -jnp.sin(phase_map))
    image_out = jnp.fft.ifft(focused, axis=1)
    return jnp.stack([jnp.real(image_out), jnp.imag(image_out)]).astype(jnp.float32)
```

```python
import functools

import jax
import jax.numpy as jnp
import ml_dtypes
import numpy as np
from jax import lax
from jax.experimental import pallas as pl
from jax.experimental.pallas import tpu as pltpu
from jax.sharding import PartitionSpec as P

NRG = 4096
NAZ = 16384
GROUPS = 16
NFILT = 16
TAPS = 8
HALO = 32
LANES = 128
RG1 = NRG // LANES
CHUNKS = 8
PER_CHUNK = LANES // CHUNKS
BF16 = jnp.bfloat16
F32 = jnp.float32


def split_np(table):
    table = np.asarray(table, np.float32)
    high = table.astype(ml_dtypes.bfloat16)
    low = (table - high.astype(np.float32)).astype(ml_dtypes.bfloat16)
    return high, low


def unit(angle_num, period, sign):
    angles = (np.asarray(angle_num, np.int64) % period) * (2.0 * np.pi / period)
    return np.cos(angles), sign * np.sin(angles)


def dft_matrix(sign):
    ids = np.arange(LANES)
    return unit(ids[:, None] * ids[None, :], LANES, sign)


def right_tables(sign, scale=1.0):
    c, s = dft_matrix(sign)
    return split_np(np.block([[c, s], [-s, c]]) * scale)


def left_table(sign, scale=1.0):
    c, s = dft_matrix(sign)
    high, low = split_np(np.block([[c, -s], [s, c]]) * scale)
    return np.concatenate([high, high, low], axis=1)


def split(x):
    high = x.astype(BF16)
    low = (x - high.astype(F32)).astype(BF16)
    return high, low


def dot(a, b):
    return jnp.dot(a, b, preferred_element_type=F32)


def scale_by(value, re, im):
    a, b = value
    eps = 1e-12
    if abs(im) < eps:
        if abs(re - 1.0) < eps:
            return value
        if abs(re + 1.0) < eps:
            return -a, -b
    if abs(re) < eps:
        if abs(im - 1.0) < eps:
            return -b, a
        if abs(im + 1.0) < eps:
            return b, -a
    if abs(abs(re) - abs(im)) < eps:
        sr, si = (1.0 if re > 0 else -1.0), (1.0 if im > 0 else -1.0)
        h = abs(re)
        total, diff = (a + b) * h, (a - b) * h
        if si == sr:
            return (diff, total) if sr > 0 else (-diff, -total)
        return (total, -diff) if sr > 0 else (-total, diff)
    re, im = float(re), float(im)
    return a * re - b * im, a * im + b * re


def dft_list(values, sign):
    count = len(values)
    if count == 1:
        return values
    even, odd = dft_list(values[0::2], sign), dft_list(values[1::2], sign)
    first, second = [], []
    for k in range(count // 2):
        re, im = unit(k, count, sign)
        a, b = even[k], scale_by(odd[k], float(re), float(im))
        first.append((a[0] + b[0], a[1] + b[1]))
        second.append((a[0] - b[0], a[1] - b[1]))
    return first + second


def dft_two_step(load, mid_ref, finish, outer, inner, sign):
    for ib in range(inner):
        column = dft_list([load(ia * inner + ib) for ia in range(outer)], sign)
        for ka in range(outer):
            re, im = unit(ib * ka, outer * inner, sign)
            a, b = scale_by(column[ka], float(re), float(im))
            mid_ref[ka * inner + ib, 0] = a
            mid_ref[ka * inner + ib, 1] = b
    for ka in range(outer):
        row = [(mid_ref[ka * inner + ib, 0], mid_ref[ka * inner + ib, 1]) for ib in range(inner)]
        for kb, value in enumerate(dft_list(row, sign)):
            finish(ka + outer * kb, value)


def pack_kernel(chunks, parts, per_part, rows_in, rank_ref, x_ref, *out_refs):
    rank = rank_ref[0]
    for j in range(parts):
        part = jnp.bitwise_xor(rank, j)
        for at, c in enumerate(chunks):
            for m in range(per_part):
                start = CHUNKS * (part * per_part + m) + c
                for ri in range(2):
                    out_refs[at * parts + j][ri, 0, m * rows_in : (m + 1) * rows_in, :] = x_ref[
                        ri, pl.ds(start, rows_in, stride=LANES), :
                    ]


def pack(raw, rank, parts, chunks):
    lines, bins = raw.shape[1], raw.shape[2]
    rows_in, tiles, per_part = lines // LANES, bins // LANES, PER_CHUNK // parts
    rows = per_part * rows_in
    count = len(chunks) * parts
    shape = jax.ShapeDtypeStruct((2, tiles, rows, LANES), F32)
    spec = pl.BlockSpec((2, 1, rows, LANES), lambda i: (0, i, 0, 0))
    flat = pl.pallas_call(
        functools.partial(pack_kernel, chunks, parts, per_part, rows_in),
        grid=(tiles,),
        in_specs=[
            pl.BlockSpec(memory_space=pltpu.SMEM),
            pl.BlockSpec((2, lines, LANES), lambda i: (0, 0, i)),
        ],
        out_specs=[spec] * count,
        out_shape=[shape] * count,
        compiler_params=pltpu.CompilerParams(vmem_limit_bytes=32 << 20),
        cost_estimate=pl.CostEstimate(flops=0, bytes_accessed=16 * lines * bins, transcendentals=0),
        name="pack",
    )(rank, raw)
    return [flat[i * parts : (i + 1) * parts] for i in range(len(chunks))]


STEP = 16


def compress_kernel(parts, rows, rank_ref, *refs):
    x_refs = refs[:parts]
    chirp_ref, tw_ref, fwd_ref, fwd_low_ref, inv_ref, inv_low_ref = refs[parts : parts + 6]
    out_ref, buf_ref, lhs_ref, y_ref, mid_ref, sems = refs[parts + 6 :]
    tiles = buf_ref.shape[3]
    rank = rank_ref[0]
    step = pl.program_id(0)
    slot = lax.rem(step, 2)

    def copies(at, to):
        return [
            pltpu.make_async_copy(
                x_refs[j].at[:, :, pl.ds(pl.multiple_of(at * rows, rows), rows), :],
                buf_ref.at[to, jnp.bitwise_xor(rank, j)],
                sems.at[to, j],
            )
            for j in range(parts)
        ]

    @pl.when(step == 0)
    def _():
        for copy in copies(step, slot):
            copy.start()

    @pl.when(step + 1 < pl.num_programs(0))
    def _():
        for copy in copies(step + 1, 1 - slot):
            copy.start()

    for copy in copies(step, slot):
        copy.wait()

    def put(at, re, im):
        for half, part in enumerate((re, im)):
            high, low = split(part)
            lhs_ref[at, half * LANES : (half + 1) * LANES] = high
            lhs_ref[at, (2 + half) * LANES : (3 + half) * LANES] = low

    def forward(i, carry):
        at = pl.ds(pl.multiple_of(i * STEP, STEP), STEP)

        def load(p):
            source = buf_ref.at[slot, p // tiles]
            return source[0, p % tiles, at, :], source[1, p % tiles, at, :]

        def finish(k, value):
            wr, wi = tw_ref[0, k : k + 1, :], tw_ref[1, k : k + 1, :]
            a, b = value
            put(
                pl.ds(pl.multiple_of(k * rows + i * STEP, STEP), STEP),
                a * wr - b * wi,
                a * wi + b * wr,
            )

        dft_two_step(load, mid_ref, finish, 4, RG1 // 4, -1.0)
        return carry

    lax.fori_loop(0, rows // STEP, forward, 0)

    group = max(1, LANES // rows)

    def middle(i, carry):
        at = pl.ds(pl.multiple_of(i * group * rows, group * rows), group * rows)
        y = dot(lhs_ref[at, :], fwd_ref[...]) + dot(lhs_ref[at, 0 : 2 * LANES], fwd_low_ref[...])
        for s in range(group):
            k = i * group + s
            cr, ci = chirp_ref[0, pl.ds(k, 1), :], chirp_ref[1, pl.ds(k, 1), :]
            a = y[s * rows : (s + 1) * rows, 0:LANES]
            b = y[s * rows : (s + 1) * rows, LANES : 2 * LANES]
            put(pl.ds(pl.multiple_of(k * rows, rows), rows), a * cr - b * ci, a * ci + b * cr)
        z = dot(lhs_ref[at, :], inv_ref[...]) + dot(lhs_ref[at, 0 : 2 * LANES], inv_low_ref[...])
        for s in range(group):
            k = i * group + s
            wr, wi = tw_ref[0, pl.ds(k, 1), :], tw_ref[1, pl.ds(k, 1), :]
            a = z[s * rows : (s + 1) * rows, 0:LANES]
            b = z[s * rows : (s + 1) * rows, LANES : 2 * LANES]
            y_ref[k, 0] = a * wr + b * wi
            y_ref[k, 1] = b * wr - a * wi
        return carry

    lax.fori_loop(0, RG1 // group, middle, 0)

    def backward(i, carry):
        at = pl.ds(pl.multiple_of(i * STEP, STEP), STEP)

        def load(k):
            return y_ref[k, 0, at, :], y_ref[k, 1, at, :]

        def finish(p, value):
            out_ref[p, 0, at, :] = value[0]
            out_ref[p, 1, at, :] = value[1]

        dft_two_step(load, mid_ref, finish, 4, RG1 // 4, 1.0)
        return carry

    lax.fori_loop(0, rows // STEP, backward, 0)


def whole_spec(array):
    zeros = (0,) * array.ndim
    return pl.BlockSpec(array.shape, lambda *_: zeros)


def compress(pieces, rank, chirp):
    parts = len(pieces)
    _, tiles, rows, _ = pieces[0].shape
    block = min(rows, 32)
    ids = np.arange(RG1)[:, None] * np.arange(LANES)[None, :]
    tw = jnp.asarray(np.stack(unit(ids, NRG, -1.0)), F32)
    fwd, fwd_low = right_tables(-1.0)
    inv, inv_low = right_tables(1.0, 1.0 / NRG)
    consts = [
        chirp,
        tw,
        jnp.asarray(np.concatenate([fwd, fwd])),
        jnp.asarray(fwd_low),
        jnp.asarray(np.concatenate([inv, inv])),
        jnp.asarray(inv_low),
    ]
    points = rows * NRG
    return pl.pallas_call(
        functools.partial(compress_kernel, parts, block),
        grid=(rows // block,),
        in_specs=[pl.BlockSpec(memory_space=pltpu.SMEM)]
        + [pl.BlockSpec(memory_space=pl.ANY)] * parts
        + [whole_spec(a) for a in consts],
        out_specs=pl.BlockSpec((RG1, 2, block, LANES), lambda i: (0, 0, i, 0)),
        out_shape=jax.ShapeDtypeStruct((RG1, 2, rows, LANES), F32),
        scratch_shapes=[
            pltpu.VMEM((2, parts, 2, tiles, block, LANES), F32),
            pltpu.VMEM((RG1 * block, 4 * LANES), BF16),
            pltpu.VMEM((RG1, 2, block, LANES), F32),
            pltpu.VMEM((RG1, 2, STEP, LANES), F32),
            pltpu.SemaphoreType.DMA((2, parts)),
        ],
        compiler_params=pltpu.CompilerParams(vmem_limit_bytes=40 << 20),
        cost_estimate=pl.CostEstimate(
            flops=points * 8 * LANES * 6, bytes_accessed=16 * points, transcendentals=0
        ),
        name="compress",
    )(rank, *pieces, *consts)


def azimuth_kernel(chunk, x_ref, tw_ref, fwd_ref, fwd_low_ref, out_ref, up_ref, down_ref, t_ref, mid_ref):
    part = pl.program_id(0)
    pieces, per_part, bins = x_ref.shape[1], x_ref.shape[3], x_ref.shape[5]

    def stage(m, carry):
        sides = []
        for ri in range(2):
            column = jnp.concatenate([x_ref[0, a, ri, m] for a in range(pieces)], axis=0)
            sides.append(split(jnp.transpose(column)))
        high = jnp.concatenate([sides[0][0], sides[1][0]], axis=1)
        low = jnp.concatenate([sides[0][1], sides[1][1]], axis=1)
        y = dot(high, fwd_ref[...]) + dot(low, fwd_ref[...]) + dot(high, fwd_low_ref[...])
        index = part * per_part + m
        at = pl.ds(CHUNKS * index + chunk, 1)
        wr, wi = tw_ref[0, at, :], tw_ref[1, at, :]
        a, b = y[:, 0:LANES], y[:, LANES : 2 * LANES]
        t_ref[index, 0] = a * wr - b * wi
        t_ref[index, 1] = a * wi + b * wr
        return carry

    lax.fori_loop(0, per_part, stage, 0)

    @pl.when(part == pl.num_programs(0) - 1)
    def _():
        def rest(i, carry):
            at = pl.ds(pl.multiple_of(i * STEP, STEP), STEP)

            def load(m):
                return t_ref[m, 0, at, :], t_ref[m, 1, at, :]

            def finish(k, value):
                re, im = unit(chunk * k, LANES, -1.0)
                a, b = scale_by(value, float(re), float(im))
                out_ref[k, 0, at, :] = a
                out_ref[k, 1, at, :] = b

            dft_two_step(load, mid_ref, finish, 4, PER_CHUNK // 4, -1.0)
            return carry

        lax.fori_loop(0, bins // STEP, rest, 0)

        def edges(k, carry):
            for ri in range(2):
                up_ref[k, ri] = out_ref[k, ri, bins - HALO : bins, :]
                down_ref[k, ri] = out_ref[k, ri, 0:HALO, :]
            return carry

        lax.fori_loop(0, PER_CHUNK, edges, 0)


def azimuth(x, chunk):
    parts, pieces, _, per_part, rows_in, bins = x.shape
    ids = np.arange(LANES)
    tw = jnp.asarray(np.stack(unit(ids[:, None] * ids[None, :], NAZ, -1.0)), F32)
    fwd, fwd_low = right_tables(-1.0)
    consts = [tw, jnp.asarray(fwd), jnp.asarray(fwd_low)]
    points = PER_CHUNK * LANES * bins
    shape = (PER_CHUNK, 2, bins, LANES)
    edge = (PER_CHUNK, 2, HALO, LANES)
    return pl.pallas_call(
        functools.partial(azimuth_kernel, chunk),
        grid=(parts,),
        in_specs=[
            pl.BlockSpec(
                (1, pieces, 2, per_part, rows_in, bins), lambda i: (i, 0, 0, 0, 0, 0)
            )
        ]
        + [whole_spec(a) for a in consts],
        out_specs=[pl.BlockSpec(s, lambda i: (0, 0, 0, 0)) for s in (shape, edge, edge)],
        out_shape=[jax.ShapeDtypeStruct(s, F32) for s in (shape, edge, edge)],
        scratch_shapes=[pltpu.VMEM(shape, F32), pltpu.VMEM((PER_CHUNK, 2, STEP, LANES), F32)],
        compiler_params=pltpu.CompilerParams(vmem_limit_bytes=32 << 20),
        cost_estimate=pl.CostEstimate(
            flops=points * 8 * LANES * 3, bytes_accessed=16 * points, transcendentals=0
        ),
        name=f"azimuth{chunk}",
    )(x, *consts)


KB = 4
BB = 8
QUAD = 4


def fit(fn, even):
    nodes = np.cos((2 * np.arange(64) + 1) * np.pi / 128) * 0.25
    z2 = (nodes + 0.25) / 2
    z = np.sqrt(z2)
    goal = fn(np.pi * z) if even else fn(np.pi * z) / z
    return [float(v) for v in np.polynomial.polynomial.polyfit(z2, goal, 4)]


SIN_FIT, COS_FIT = fit(np.sin, False), fit(np.cos, True)


def horner(coefficients, x):
    total = coefficients[-1]
    for c in reversed(coefficients[:-1]):
        total = total * x + c
    return total


def turn(t):
    z = t - jnp.round(t)
    z2 = z * z
    s = horner(SIN_FIT, z2) * z
    c = horner(COS_FIT, z2)
    twice = s + s
    return 1.0 - twice * s, twice * c


def final_kernel(steps, wide, *refs):
    d_refs, refs = refs[:CHUNKS], refs[CHUNKS:]
    low_refs, high_refs = (), ()
    if wide:
        low_refs, high_refs, refs = refs[:CHUNKS], refs[CHUNKS : 2 * CHUNKS], refs[2 * CHUNKS :]
    g_ref, rate_ref, inv1_ref, inv2_ref, tw_ref = refs[:5]
    out_ref, zr_ref, zi_ref, x_ref, s_ref = refs[-5:]
    own = d_refs[0].shape[2]
    ext = x_ref.shape[1] // 3
    bins = rate_ref.shape[0]
    step = pl.program_id(0)

    @pl.when(step < steps)
    def _():
        def one(kk, buf):
            k = step * KB + kk

            def combine(sources, start, to):
                at = slice(start, start + STEP)
                values = [(ref[kk, 0, at, :], ref[kk, 1, at, :]) for ref in sources]
                for q, (a, b) in enumerate(dft_list(values, -1.0)):
                    for half, part in enumerate((a, b)):
                        hi, lo = split(part)
                        cols = slice(half * LANES, (half + 1) * LANES)
                        x_ref[buf * CHUNKS + q, to : to + STEP, cols] = hi
                        x_ref[buf * CHUNKS + q, ext + to : ext + to + STEP, cols] = lo
                        x_ref[buf * CHUNKS + q, 2 * ext + to : 2 * ext + to + STEP, cols] = hi

            for start in range(0, own, STEP):
                combine(d_refs, start, start)
            if wide:
                for start in range(0, HALO, STEP):
                    combine(low_refs, start, own + start)
                    combine(high_refs, start, own + HALO + start)
            for q in range(CHUNKS):
                k2 = k + PER_CHUNK * q
                moved = dot(g_ref[lax.div(k2, LANES // GROUPS)], x_ref[buf * CHUNKS + q])
                f = k2 * LANES + lax.broadcasted_iota(jnp.int32, (1, LANES), 1)
                centred = jnp.where(f >= NAZ // 2, f - NAZ, f).astype(F32) * (1.0 / NAZ)
                square = centred * centred
                block = min(bins, 32)
                for start in range(0, bins, block):
                    at = slice(start, start + block)
                    c, s = turn(rate_ref[at, :] * square)
                    a, b = moved[at, 0:LANES], moved[at, LANES : 2 * LANES]
                    to = pl.ds(pl.multiple_of(k2 * bins + start, block), block)
                    zr_ref[to, :] = a * c + b * s
                    zi_ref[to, :] = b * c - a * s

        def first(i, carry):
            one(2 * i, 0)
            one(2 * i + 1, 1)
            return carry

        lax.fori_loop(0, KB // 2, first, 0)

    @pl.when(step >= steps)
    def _():
        base = (step - steps) * BB

        def some(j, carry):
            cols = []
            for t in range(QUAD):
                at = pl.ds(base + QUAD * j + t, LANES, stride=bins)
                cols.append(jnp.concatenate([zr_ref[at, :], zi_ref[at, :]], axis=0))
            hi, lo = split(jnp.concatenate(cols, axis=1))
            w = dot(inv1_ref[...], jnp.concatenate([hi, lo, hi], axis=0))
            rows = []
            for t in range(QUAD):
                a = w[0:LANES, t * LANES : (t + 1) * LANES]
                b = w[LANES : 2 * LANES, t * LANES : (t + 1) * LANES]
                wr, wi = tw_ref[0], tw_ref[1]
                rows.append(jnp.concatenate([a * wr - b * wi, a * wi + b * wr], axis=1))
            hi, lo = split(jnp.concatenate(rows, axis=0))
            image = lax.dot_general(
                inv2_ref[...],
                jnp.concatenate([hi, lo, hi], axis=1),
                (((1,), (1,)), ((), ())),
                preferred_element_type=F32,
            )
            for t in range(QUAD):
                for ri in range(2):
                    s_ref[ri, pl.ds(QUAD * j + t, LANES, stride=BB), :] = image[
                        ri * LANES : (ri + 1) * LANES, t * LANES : (t + 1) * LANES
                    ]
            return carry

        lax.fori_loop(0, BB // QUAD, some, 0)
        for ri in range(2):
            for n in range(LANES):
                out_ref[ri, :, n * LANES : (n + 1) * LANES] = s_ref[ri, n * BB : (n + 1) * BB, :]


def final(bins, mains, lows, highs, mover, rate, places, image=None):
    own, rows = mains[0].shape[2], rate.shape[0]
    wide = len(lows) > 0
    ext = own + (2 * HALO if wide else 0)
    steps = PER_CHUNK // KB
    ids = np.arange(LANES)
    tw = jnp.asarray(np.stack(unit(ids[:, None] * ids[None, :], NAZ, 1.0)), F32)
    consts = [
        mover,
        rate,
        jnp.asarray(left_table(1.0)),
        jnp.asarray(left_table(1.0, 1.0 / NAZ)),
        tw,
    ]
    start, gap_at = places[0], len(places)
    for i, place in enumerate(places):
        if place != start + i:
            gap_at = i
            break
    gap = places[-1] - start - len(places) + 1

    def early(i):
        return (jnp.minimum(i, steps - 1), 0, 0, 0)

    def late(i):
        at = jnp.maximum(i - steps, 0)
        return (0, start + at + jnp.where(at >= gap_at, gap, 0), 0)

    points = NAZ * rows
    given = [*mains, *lows, *highs, *consts]
    specs = [pl.BlockSpec((KB, 2, own, LANES), early)] * CHUNKS
    specs += [pl.BlockSpec((KB, 2, HALO, LANES), early)] * (2 * CHUNKS if wide else 0)
    specs += [whole_spec(a) for a in consts]
    aliases = {}
    if image is not None:
        aliases = {len(given): 0}
        given.append(image)
        specs.append(pl.BlockSpec(memory_space=pl.ANY))
    return pl.pallas_call(
        functools.partial(final_kernel, steps, wide),
        grid=(steps + len(places),),
        in_specs=specs,
        out_specs=pl.BlockSpec((2, BB, NAZ), late),
        out_shape=jax.ShapeDtypeStruct((2, bins, NAZ), F32),
        scratch_shapes=[
            pltpu.VMEM((LANES * rows, LANES), F32),
            pltpu.VMEM((LANES * rows, LANES), F32),
            pltpu.VMEM((2 * CHUNKS, 3 * ext, 2 * LANES), BF16),
            pltpu.VMEM((2, LANES * BB, LANES), F32),
        ],
        input_output_aliases=aliases,
        compiler_params=pltpu.CompilerParams(vmem_limit_bytes=56 << 20),
        cost_estimate=pl.CostEstimate(
            flops=points * 8 * LANES * 9, bytes_accessed=28 * points, transcendentals=0
        ),
        name="final_wide" if wide else "final_inner",
    )(*given)


def mover_table(bins, rows, wide, shift_table, filter_index, tap_table):
    ext = bins + (2 * HALO if wide else 0)
    shift_table, filter_index = shift_table[:, rows], filter_index[:, rows]
    onehot = (filter_index[:, :, None] == jnp.arange(NFILT, dtype=jnp.int32)).astype(F32)
    weights = jnp.einsum("gbf,ft->gbt", onehot, tap_table, precision=lax.Precision.HIGHEST)
    first = rows[None, :].astype(np.int32) + shift_table + (HALO - 4)
    column = np.arange(3 * ext) % ext
    natural = np.where(
        column < bins, column + HALO, np.where(column < bins + HALO, column - bins, column)
    ).astype(np.int32)
    offset = natural[None, None, :] - first[:, :, None]
    table = jnp.zeros(offset.shape, F32)
    for t in range(TAPS):
        table = table + jnp.where(offset == t, weights[:, :, t : t + 1], 0.0)
    high = lax.reduce_precision(table, 8, 7)
    return jnp.where(np.arange(3 * ext) < 2 * ext, high, table - high).astype(BF16)


def neighbours(axes, size, step):
    return [(i, i + step) for i in range(size) if 0 <= i + step < size]


def local(nrng, naz, raw_echo, chirp_spectrum, azimuth_rate, shift_table, filter_index, tap_table):
    axes = ("rng", "az")
    devices = nrng * naz
    bins = NRG // devices
    rows_in = raw_echo.shape[1] // LANES
    per_part = PER_CHUNK // nrng
    rows = per_part * rows_in
    chirp = chirp_spectrum.reshape(2, LANES, RG1).transpose(0, 2, 1)
    rate = jnp.broadcast_to((azimuth_rate * 0.5)[:, None], (bins, LANES))
    rank = lax.axis_index("rng").astype(jnp.int32).reshape(1)
    packed = pack(raw_echo, rank, nrng, [0]) + pack(raw_echo, rank, nrng, list(range(1, CHUNKS)))
    mains, lows, highs = [], [], []

    def finish(lines, c):
        if bins < LANES:
            cut = lines.reshape(RG1, 2, rows, LANES // bins, bins)
            lines = cut.transpose(0, 3, 1, 2, 4).reshape(devices, 2, rows, bins)
        turned = lax.all_to_all(lines, axes, split_axis=0, concat_axis=0, tiled=True)
        turned = turned.reshape(nrng, naz, 2, per_part, rows_in, bins)
        main, up, down = azimuth(turned, c)
        mains.append(main)
        lows.append(lax.ppermute(up, axes, neighbours(axes, devices, 1)))
        highs.append(lax.ppermute(down, axes, neighbours(axes, devices, -1)))

    arrived = None
    for c in range(CHUNKS):
        sent = packed[c]
        if arrived is not None:
            sent, arrived = lax.optimization_barrier((sent, arrived))
            lines = compress(arrived, rank, chirp)
            if c >= 3:
                lines, mains[c - 3] = lax.optimization_barrier((lines, mains[c - 3]))
            finish(lines, c - 1)
        arrived = [sent[0]] + [
            lax.ppermute(sent[j], "rng", [(i, i ^ j) for i in range(nrng)]) for j in range(1, nrng)
        ]
    finish(compress(arrived, rank, chirp), CHUNKS - 1)
    tables = (shift_table, filter_index, tap_table)
    blocks = np.arange(bins // BB)
    inner = (blocks >= HALO // BB) & (blocks < (bins - HALO) // BB)
    image = None
    for chosen, wide in ((inner, False), (~inner, True)):
        places = blocks[chosen].tolist()
        if not places:
            continue
        ids = np.concatenate([np.arange(BB) + BB * place for place in places])
        mover = mover_table(bins, ids, wide, *tables)
        halos = (lows, highs) if wide else ([], [])
        image = final(bins, mains, *halos, mover, rate[ids], places, image)
    return image
def solution(mesh):
    return jax.shard_map(
        functools.partial(local, mesh.shape["rng"], mesh.shape["az"]),
        mesh=mesh,
        in_specs=(
            P(None, "az", "rng"),
            P(),
            P(("rng", "az")),
            P(None, ("rng", "az")),
            P(None, ("rng", "az")),
            P(),
        ),
        out_specs=P(None, ("rng", "az"), None),
        check_vma=False,
    )
```

```python
import functools

import jax
import jax.numpy as jnp
import ml_dtypes
import numpy as np
from jax import lax
from jax.experimental import pallas as pl
from jax.experimental.pallas import tpu as pltpu
from jax.sharding import PartitionSpec as P

NRG = 4096
NAZ = 16384
GROUPS = 16
NFILT = 16
TAPS = 8
HALO = 32
LANES = 128
RG1 = NRG // LANES
CHUNKS = 8
PER_CHUNK = LANES // CHUNKS
VMEM_LIMIT = 60 << 20
BF16 = jnp.bfloat16
F32 = jnp.float32


def split_np(table):
    table = np.asarray(table, np.float32)
    high = table.astype(ml_dtypes.bfloat16)
    low = (table - high.astype(np.float32)).astype(ml_dtypes.bfloat16)
    return high, low


def unit(angle_num, period, sign):
    angles = (np.asarray(angle_num, np.int64) % period) * (2.0 * np.pi / period)
    return np.cos(angles), sign * np.sin(angles)


def dft_matrix(sign):
    ids = np.arange(LANES)
    return unit(ids[:, None] * ids[None, :], LANES, sign)


def right_tables(sign, scale=1.0):
    c, s = dft_matrix(sign)
    return split_np(np.block([[c, s], [-s, c]]) * scale)


def left_table(sign, scale=1.0):
    c, s = dft_matrix(sign)
    high, low = split_np(np.block([[c, -s], [s, c]]) * scale)
    return np.concatenate([high, high, low], axis=1)


def split(x):
    high = x.astype(BF16)
    low = (x - high.astype(F32)).astype(BF16)
    return high, low


def dot(a, b):
    return jnp.dot(a, b, preferred_element_type=F32)


def scale_by(value, re, im):
    a, b = value
    eps = 1e-12
    if abs(im) < eps:
        if abs(re - 1.0) < eps:
            return value
        if abs(re + 1.0) < eps:
            return -a, -b
    if abs(re) < eps:
        if abs(im - 1.0) < eps:
            return -b, a
        if abs(im + 1.0) < eps:
            return b, -a
    if abs(abs(re) - abs(im)) < eps:
        sr, si = (1.0 if re > 0 else -1.0), (1.0 if im > 0 else -1.0)
        h = abs(re)
        total, diff = (a + b) * h, (a - b) * h
        if si == sr:
            return (diff, total) if sr > 0 else (-diff, -total)
        return (total, -diff) if sr > 0 else (-total, diff)
    re, im = float(re), float(im)
    return a * re - b * im, a * im + b * re


def dft_list(values, sign):
    count = len(values)
    if count == 1:
        return values
    even, odd = dft_list(values[0::2], sign), dft_list(values[1::2], sign)
    first, second = [], []
    for k in range(count // 2):
        re, im = unit(k, count, sign)
        a, b = even[k], scale_by(odd[k], float(re), float(im))
        first.append((a[0] + b[0], a[1] + b[1]))
        second.append((a[0] - b[0], a[1] - b[1]))
    return first + second


def dft_two_step(load, mid_ref, finish, outer, inner, sign):
    for ib in range(inner):
        column = dft_list([load(ia * inner + ib) for ia in range(outer)], sign)
        for ka in range(outer):
            re, im = unit(ib * ka, outer * inner, sign)
            a, b = scale_by(column[ka], float(re), float(im))
            mid_ref[ka * inner + ib, 0] = a
            mid_ref[ka * inner + ib, 1] = b
    for ka in range(outer):
        row = [(mid_ref[ka * inner + ib, 0], mid_ref[ka * inner + ib, 1]) for ib in range(inner)]
        for kb, value in enumerate(dft_list(row, sign)):
            finish(ka + outer * kb, value)


def pack_kernel(chunks, parts, per_part, rows_in, rank_ref, x_ref, *out_refs):
    rank = rank_ref[0]
    for j in range(parts):
        part = jnp.bitwise_xor(rank, j)
        for at, c in enumerate(chunks):
            for m in range(per_part):
                start = CHUNKS * (part * per_part + m) + c
                for ri in range(2):
                    out_refs[at * parts + j][ri, 0, m * rows_in : (m + 1) * rows_in, :] = x_ref[
                        ri, pl.ds(start, rows_in, stride=LANES), :
                    ]


def pack(raw, rank, parts, chunks):
    lines, bins = raw.shape[1], raw.shape[2]
    rows_in, tiles, per_part = lines // LANES, bins // LANES, PER_CHUNK // parts
    rows = per_part * rows_in
    count = len(chunks) * parts
    shape = jax.ShapeDtypeStruct((2, tiles, rows, LANES), F32)
    spec = pl.BlockSpec((2, 1, rows, LANES), lambda i: (0, i, 0, 0))
    flat = pl.pallas_call(
        functools.partial(pack_kernel, chunks, parts, per_part, rows_in),
        grid=(tiles,),
        in_specs=[
            pl.BlockSpec(memory_space=pltpu.SMEM),
            pl.BlockSpec((2, lines, LANES), lambda i: (0, 0, i)),
        ],
        out_specs=[spec] * count,
        out_shape=[shape] * count,
        compiler_params=pltpu.CompilerParams(vmem_limit_bytes=VMEM_LIMIT),
        cost_estimate=pl.CostEstimate(flops=0, bytes_accessed=16 * lines * bins, transcendentals=0),
        name="pack",
    )(rank, raw)
    return [flat[i * parts : (i + 1) * parts] for i in range(len(chunks))]


STEP = 16


def compress_kernel(parts, rows, rank_ref, *refs):
    x_refs = refs[:parts]
    chirp_ref, tw_ref, fwd_ref, fwd_low_ref, inv_ref, inv_low_ref = refs[parts : parts + 6]
    out_ref, buf_ref, lhs_ref, y_ref, mid_ref, sems = refs[parts + 6 :]
    tiles = buf_ref.shape[3]
    rank = rank_ref[0]
    step = pl.program_id(0)
    slot = lax.rem(step, 2)

    def copies(at, to):
        return [
            pltpu.make_async_copy(
                x_refs[j].at[:, :, pl.ds(pl.multiple_of(at * rows, rows), rows), :],
                buf_ref.at[to, jnp.bitwise_xor(rank, j)],
                sems.at[to, j],
            )
            for j in range(parts)
        ]

    @pl.when(step == 0)
    def _():
        for copy in copies(step, slot):
            copy.start()

    @pl.when(step + 1 < pl.num_programs(0))
    def _():
        for copy in copies(step + 1, 1 - slot):
            copy.start()

    for copy in copies(step, slot):
        copy.wait()

    def put(at, re, im):
        for half, part in enumerate((re, im)):
            high, low = split(part)
            lhs_ref[at, half * LANES : (half + 1) * LANES] = high
            lhs_ref[at, (2 + half) * LANES : (3 + half) * LANES] = low

    def forward(i, carry):
        at = pl.ds(pl.multiple_of(i * STEP, STEP), STEP)

        def load(p):
            source = buf_ref.at[slot, p // tiles]
            return source[0, p % tiles, at, :], source[1, p % tiles, at, :]

        def finish(k, value):
            wr, wi = tw_ref[0, k : k + 1, :], tw_ref[1, k : k + 1, :]
            a, b = value
            put(
                pl.ds(pl.multiple_of(k * rows + i * STEP, STEP), STEP),
                a * wr - b * wi,
                a * wi + b * wr,
            )

        dft_two_step(load, mid_ref, finish, 4, RG1 // 4, -1.0)
        return carry

    lax.fori_loop(0, rows // STEP, forward, 0)

    group = max(1, LANES // rows)

    def middle(i, carry):
        at = pl.ds(pl.multiple_of(i * group * rows, group * rows), group * rows)
        y = dot(lhs_ref[at, :], fwd_ref[...]) + dot(lhs_ref[at, 0 : 2 * LANES], fwd_low_ref[...])
        for s in range(group):
            k = i * group + s
            cr, ci = chirp_ref[0, pl.ds(k, 1), :], chirp_ref[1, pl.ds(k, 1), :]
            a = y[s * rows : (s + 1) * rows, 0:LANES]
            b = y[s * rows : (s + 1) * rows, LANES : 2 * LANES]
            put(pl.ds(pl.multiple_of(k * rows, rows), rows), a * cr - b * ci, a * ci + b * cr)
        z = dot(lhs_ref[at, :], inv_ref[...]) + dot(lhs_ref[at, 0 : 2 * LANES], inv_low_ref[...])
        for s in range(group):
            k = i * group + s
            wr, wi = tw_ref[0, pl.ds(k, 1), :], tw_ref[1, pl.ds(k, 1), :]
            a = z[s * rows : (s + 1) * rows, 0:LANES]
            b = z[s * rows : (s + 1) * rows, LANES : 2 * LANES]
            y_ref[k, 0] = a * wr + b * wi
            y_ref[k, 1] = b * wr - a * wi
        return carry

    lax.fori_loop(0, RG1 // group, middle, 0)

    def backward(i, carry):
        at = pl.ds(pl.multiple_of(i * STEP, STEP), STEP)

        def load(k):
            return y_ref[k, 0, at, :], y_ref[k, 1, at, :]

        def finish(p, value):
            out_ref[p, 0, at, :] = value[0]
            out_ref[p, 1, at, :] = value[1]

        dft_two_step(load, mid_ref, finish, 4, RG1 // 4, 1.0)
        return carry

    lax.fori_loop(0, rows // STEP, backward, 0)


def whole_spec(array):
    zeros = (0,) * array.ndim
    return pl.BlockSpec(array.shape, lambda *_: zeros)


def compress(pieces, rank, chirp):
    parts = len(pieces)
    _, tiles, rows, _ = pieces[0].shape
    block = min(rows, 32)
    ids = np.arange(RG1)[:, None] * np.arange(LANES)[None, :]
    tw = jnp.asarray(np.stack(unit(ids, NRG, -1.0)), F32)
    fwd, fwd_low = right_tables(-1.0)
    inv, inv_low = right_tables(1.0, 1.0 / NRG)
    consts = [
        chirp,
        tw,
        jnp.asarray(np.concatenate([fwd, fwd])),
        jnp.asarray(fwd_low),
        jnp.asarray(np.concatenate([inv, inv])),
        jnp.asarray(inv_low),
    ]
    points = rows * NRG
    return pl.pallas_call(
        functools.partial(compress_kernel, parts, block),
        grid=(rows // block,),
        in_specs=[pl.BlockSpec(memory_space=pltpu.SMEM)]
        + [pl.BlockSpec(memory_space=pl.ANY)] * parts
        + [whole_spec(a) for a in consts],
        out_specs=pl.BlockSpec((RG1, 2, block, LANES), lambda i: (0, 0, i, 0)),
        out_shape=jax.ShapeDtypeStruct((RG1, 2, rows, LANES), F32),
        scratch_shapes=[
            pltpu.VMEM((2, parts, 2, tiles, block, LANES), F32),
            pltpu.VMEM((RG1 * block, 4 * LANES), BF16),
            pltpu.VMEM((RG1, 2, block, LANES), F32),
            pltpu.VMEM((RG1, 2, STEP, LANES), F32),
            pltpu.SemaphoreType.DMA((2, parts)),
        ],
        compiler_params=pltpu.CompilerParams(vmem_limit_bytes=VMEM_LIMIT),
        cost_estimate=pl.CostEstimate(
            flops=points * 8 * LANES * 6, bytes_accessed=16 * points, transcendentals=0
        ),
        name="compress",
    )(rank, *pieces, *consts)


def azimuth_kernel(chunk, x_ref, tw_ref, fwd_ref, fwd_low_ref, out_ref, up_ref, down_ref, t_ref, mid_ref):
    part = pl.program_id(0)
    pieces, per_part, bins = x_ref.shape[1], x_ref.shape[3], x_ref.shape[5]

    def stage(m, carry):
        sides = []
        for ri in range(2):
            column = jnp.concatenate([x_ref[0, a, ri, m] for a in range(pieces)], axis=0)
            sides.append(split(jnp.transpose(column)))
        high = jnp.concatenate([sides[0][0], sides[1][0]], axis=1)
        low = jnp.concatenate([sides[0][1], sides[1][1]], axis=1)
        y = dot(high, fwd_ref[...]) + dot(low, fwd_ref[...]) + dot(high, fwd_low_ref[...])
        index = part * per_part + m
        at = pl.ds(CHUNKS * index + chunk, 1)
        wr, wi = tw_ref[0, at, :], tw_ref[1, at, :]
        a, b = y[:, 0:LANES], y[:, LANES : 2 * LANES]
        t_ref[index, 0] = a * wr - b * wi
        t_ref[index, 1] = a * wi + b * wr
        return carry

    lax.fori_loop(0, per_part, stage, 0)

    @pl.when(part == pl.num_programs(0) - 1)
    def _():
        def rest(i, carry):
            at = pl.ds(pl.multiple_of(i * STEP, STEP), STEP)

            def load(m):
                return t_ref[m, 0, at, :], t_ref[m, 1, at, :]

            def finish(k, value):
                re, im = unit(chunk * k, LANES, -1.0)
                a, b = scale_by(value, float(re), float(im))
                out_ref[k, 0, at, :] = a
                out_ref[k, 1, at, :] = b

            dft_two_step(load, mid_ref, finish, 4, PER_CHUNK // 4, -1.0)
            return carry

        lax.fori_loop(0, bins // STEP, rest, 0)

        def edges(k, carry):
            for ri in range(2):
                up_ref[k, ri] = out_ref[k, ri, bins - HALO : bins, :]
                down_ref[k, ri] = out_ref[k, ri, 0:HALO, :]
            return carry

        lax.fori_loop(0, PER_CHUNK, edges, 0)


def azimuth(x, chunk):
    parts, pieces, _, per_part, rows_in, bins = x.shape
    ids = np.arange(LANES)
    tw = jnp.asarray(np.stack(unit(ids[:, None] * ids[None, :], NAZ, -1.0)), F32)
    fwd, fwd_low = right_tables(-1.0)
    consts = [tw, jnp.asarray(fwd), jnp.asarray(fwd_low)]
    points = PER_CHUNK * LANES * bins
    shape = (PER_CHUNK, 2, bins, LANES)
    edge = (PER_CHUNK, 2, HALO, LANES)
    return pl.pallas_call(
        functools.partial(azimuth_kernel, chunk),
        grid=(parts,),
        in_specs=[
            pl.BlockSpec(
                (1, pieces, 2, per_part, rows_in, bins), lambda i: (i, 0, 0, 0, 0, 0)
            )
        ]
        + [whole_spec(a) for a in consts],
        out_specs=[pl.BlockSpec(s, lambda i: (0, 0, 0, 0)) for s in (shape, edge, edge)],
        out_shape=[jax.ShapeDtypeStruct(s, F32) for s in (shape, edge, edge)],
        scratch_shapes=[pltpu.VMEM(shape, F32), pltpu.VMEM((PER_CHUNK, 2, STEP, LANES), F32)],
        compiler_params=pltpu.CompilerParams(vmem_limit_bytes=VMEM_LIMIT),
        cost_estimate=pl.CostEstimate(
            flops=points * 8 * LANES * 3, bytes_accessed=16 * points, transcendentals=0
        ),
        name=f"azimuth{chunk}",
    )(x, *consts)


KB = 4
BB = 8
QUAD = 4


def fit(fn, even):
    nodes = np.cos((2 * np.arange(64) + 1) * np.pi / 128) * 0.25
    z2 = (nodes + 0.25) / 2
    z = np.sqrt(z2)
    goal = fn(np.pi * z) if even else fn(np.pi * z) / z
    return [float(v) for v in np.polynomial.polynomial.polyfit(z2, goal, 4)]


SIN_FIT, COS_FIT = fit(np.sin, False), fit(np.cos, True)


def horner(coefficients, x):
    total = coefficients[-1]
    for c in reversed(coefficients[:-1]):
        total = total * x + c
    return total


def turn(t):
    z = t - jnp.round(t)
    z2 = z * z
    s = horner(SIN_FIT, z2) * z
    c = horner(COS_FIT, z2)
    twice = s + s
    return 1.0 - twice * s, twice * c


def final_kernel(steps, wide, *refs):
    d_refs, refs = refs[:CHUNKS], refs[CHUNKS:]
    low_refs, high_refs = (), ()
    if wide:
        low_refs, high_refs, refs = refs[:CHUNKS], refs[CHUNKS : 2 * CHUNKS], refs[2 * CHUNKS :]
    g_ref, rate_ref, inv1_ref, inv2_ref, tw_ref = refs[:5]
    out_ref, zr_ref, zi_ref, x_ref, s_ref = refs[-5:]
    own = d_refs[0].shape[2]
    ext = x_ref.shape[1] // 2
    bins = rate_ref.shape[0]
    step = pl.program_id(0)

    @pl.when(step < steps)
    def _():
        def one(kk, buf):
            k = step * KB + kk

            def combine(sources, start, to):
                at = slice(start, start + STEP)
                values = [(ref[kk, 0, at, :], ref[kk, 1, at, :]) for ref in sources]
                for q, (a, b) in enumerate(dft_list(values, -1.0)):
                    for half, part in enumerate((a, b)):
                        hi, lo = split(part)
                        cols = slice(half * LANES, (half + 1) * LANES)
                        x_ref[buf * CHUNKS + q, to : to + STEP, cols] = hi
                        x_ref[buf * CHUNKS + q, ext + to : ext + to + STEP, cols] = lo

            for start in range(0, own, STEP):
                combine(d_refs, start, start)
            if wide:
                for start in range(0, HALO, STEP):
                    combine(low_refs, start, own + start)
                    combine(high_refs, start, own + HALO + start)
            for q in range(CHUNKS):
                k2 = k + PER_CHUNK * q
                moved = dot(g_ref[lax.div(k2, LANES // GROUPS)], x_ref[buf * CHUNKS + q])
                f = k2 * LANES + lax.broadcasted_iota(jnp.int32, (1, LANES), 1)
                centred = jnp.where(f >= NAZ // 2, f - NAZ, f).astype(F32) * (1.0 / NAZ)
                square = centred * centred
                block = min(bins, 32)
                for start in range(0, bins, block):
                    at = slice(start, start + block)
                    c, s = turn(rate_ref[at, :] * square)
                    both = moved[at, :] + moved[bins + start : bins + start + block, :]
                    a, b = both[:, 0:LANES], both[:, LANES : 2 * LANES]
                    to = pl.ds(pl.multiple_of(k2 * bins + start, block), block)
                    zr_ref[to, :] = a * c + b * s
                    zi_ref[to, :] = b * c - a * s

        def first(i, carry):
            one(2 * i, 0)
            one(2 * i + 1, 1)
            return carry

        lax.fori_loop(0, KB // 2, first, 0)

    @pl.when(step >= steps)
    def _():
        base = (step - steps) * BB

        def some(j, carry):
            cols = []
            for t in range(QUAD):
                at = pl.ds(base + QUAD * j + t, LANES, stride=bins)
                cols.append(jnp.concatenate([zr_ref[at, :], zi_ref[at, :]], axis=0))
            hi, lo = split(jnp.concatenate(cols, axis=1))
            w = dot(inv1_ref[...], jnp.concatenate([hi, lo, hi], axis=0))
            rows = []
            for t in range(QUAD):
                a = w[0:LANES, t * LANES : (t + 1) * LANES]
                b = w[LANES : 2 * LANES, t * LANES : (t + 1) * LANES]
                wr, wi = tw_ref[0], tw_ref[1]
                rows.append(jnp.concatenate([a * wr - b * wi, a * wi + b * wr], axis=1))
            hi, lo = split(jnp.concatenate(rows, axis=0))
            image = lax.dot_general(
                inv2_ref[...],
                jnp.concatenate([hi, lo, hi], axis=1),
                (((1,), (1,)), ((), ())),
                preferred_element_type=F32,
            )
            for t in range(QUAD):
                for ri in range(2):
                    s_ref[ri, pl.ds(QUAD * j + t, LANES, stride=BB), :] = image[
                        ri * LANES : (ri + 1) * LANES, t * LANES : (t + 1) * LANES
                    ]
            return carry

        lax.fori_loop(0, BB // QUAD, some, 0)
        for ri in range(2):
            for n in range(LANES):
                out_ref[ri, :, n * LANES : (n + 1) * LANES] = s_ref[ri, n * BB : (n + 1) * BB, :]


def final(bins, mains, lows, highs, mover, rate, places, image=None):
    own, rows = mains[0].shape[2], rate.shape[0]
    wide = len(lows) > 0
    ext = own + (2 * HALO if wide else 0)
    steps = PER_CHUNK // KB
    ids = np.arange(LANES)
    tw = jnp.asarray(np.stack(unit(ids[:, None] * ids[None, :], NAZ, 1.0)), F32)
    consts = [
        mover,
        rate,
        jnp.asarray(left_table(1.0)),
        jnp.asarray(left_table(1.0, 1.0 / NAZ)),
        tw,
    ]
    start, gap_at = places[0], len(places)
    for i, place in enumerate(places):
        if place != start + i:
            gap_at = i
            break
    gap = places[-1] - start - len(places) + 1

    def early(i):
        return (jnp.minimum(i, steps - 1), 0, 0, 0)

    def late(i):
        at = jnp.maximum(i - steps, 0)
        return (0, start + at + jnp.where(at >= gap_at, gap, 0), 0)

    points = NAZ * rows
    given = [*mains, *lows, *highs, *consts]
    specs = [pl.BlockSpec((KB, 2, own, LANES), early)] * CHUNKS
    specs += [pl.BlockSpec((KB, 2, HALO, LANES), early)] * (2 * CHUNKS if wide else 0)
    specs += [whole_spec(a) for a in consts]
    aliases = {}
    if image is not None:
        aliases = {len(given): 0}
        given.append(image)
        specs.append(pl.BlockSpec(memory_space=pl.ANY))
    return pl.pallas_call(
        functools.partial(final_kernel, steps, wide),
        grid=(steps + len(places),),
        in_specs=specs,
        out_specs=pl.BlockSpec((2, BB, NAZ), late),
        out_shape=jax.ShapeDtypeStruct((2, bins, NAZ), F32),
        scratch_shapes=[
            pltpu.VMEM((LANES * rows, LANES), F32),
            pltpu.VMEM((LANES * rows, LANES), F32),
            pltpu.VMEM((2 * CHUNKS, 2 * ext, 2 * LANES), BF16),
            pltpu.VMEM((2, LANES * BB, LANES), F32),
        ],
        input_output_aliases=aliases,
        compiler_params=pltpu.CompilerParams(vmem_limit_bytes=VMEM_LIMIT),
        cost_estimate=pl.CostEstimate(
            flops=points * 8 * LANES * 9, bytes_accessed=28 * points, transcendentals=0
        ),
        name="final_wide" if wide else "final_inner",
    )(*given)


def mover_table(bins, rows, wide, shift_table, filter_index, tap_table):
    ext = bins + (2 * HALO if wide else 0)
    shift_table, filter_index = shift_table[:, rows], filter_index[:, rows]
    onehot = (filter_index[:, :, None] == jnp.arange(NFILT, dtype=jnp.int32)).astype(F32)
    weights = jnp.einsum("gbf,ft->gbt", onehot, tap_table, precision=lax.Precision.HIGHEST)
    first = rows[None, :].astype(np.int32) + shift_table + (HALO - 4)
    column = np.arange(ext)
    natural = np.where(
        column < bins, column + HALO, np.where(column < bins + HALO, column - bins, column)
    ).astype(np.int32)
    offset = natural[None, None, :] - first[:, :, None]
    table = jnp.zeros(offset.shape, F32)
    for t in range(TAPS):
        table = table + jnp.where(offset == t, weights[:, :, t : t + 1], 0.0)
    high = lax.reduce_precision(table, 8, 7)
    low = table - high
    top = jnp.concatenate([high, high], axis=2)
    bottom = jnp.concatenate([low, jnp.zeros_like(low)], axis=2)
    return jnp.concatenate([top, bottom], axis=1).astype(BF16)


def neighbours(axes, size, step):
    return [(i, i + step) for i in range(size) if 0 <= i + step < size]


def local(nrng, naz, raw_echo, chirp_spectrum, azimuth_rate, shift_table, filter_index, tap_table):
    axes = ("rng", "az")
    devices = nrng * naz
    bins = NRG // devices
    rows_in = raw_echo.shape[1] // LANES
    per_part = PER_CHUNK // nrng
    rows = per_part * rows_in
    chirp = chirp_spectrum.reshape(2, LANES, RG1).transpose(0, 2, 1)
    rate = jnp.broadcast_to((azimuth_rate * 0.5)[:, None], (bins, LANES))
    rank = lax.axis_index("rng").astype(jnp.int32).reshape(1)
    packed = pack(raw_echo, rank, nrng, [0]) + pack(raw_echo, rank, nrng, list(range(1, CHUNKS)))
    mains, lows, highs = [], [], []
    turned = []

    def gather(c):
        return [packed[c][0]] + [
            lax.ppermute(packed[c][j], "rng", [(i, i ^ j) for i in range(nrng)])
            for j in range(1, nrng)
        ]

    def transform(c):
        if c > 0:
            turned[c], mains[c - 1] = lax.optimization_barrier((turned[c], mains[c - 1]))
        main, up, down = azimuth(turned[c], c)
        mains.append(main)
        lows.append(lax.ppermute(up, axes, neighbours(axes, devices, 1)))
        highs.append(lax.ppermute(down, axes, neighbours(axes, devices, -1)))

    got = [gather(0)]
    packed[1], got[0] = lax.optimization_barrier((packed[1], got[0]))
    got.append(gather(1))
    for c in range(CHUNKS):
        lines = compress(got[c], rank, chirp)
        if c + 2 < CHUNKS:
            packed[c + 2], lines = lax.optimization_barrier((packed[c + 2], lines))
            packed[c + 2], got[c + 1] = lax.optimization_barrier((packed[c + 2], got[c + 1]))
            if c >= 1:
                held = (packed[c + 2], turned[c - 1])
                packed[c + 2], turned[c - 1] = lax.optimization_barrier(held)
            got.append(gather(c + 2))
        if c >= 2:
            transform(c - 2)
            lines, mains[c - 2] = lax.optimization_barrier((lines, mains[c - 2]))
        if c >= 3:
            held = (lines, lows[c - 3], highs[c - 3])
            lines, lows[c - 3], highs[c - 3] = lax.optimization_barrier(held)
        if bins < LANES:
            cut = lines.reshape(RG1, 2, rows, LANES // bins, bins)
            lines = cut.transpose(0, 3, 1, 2, 4).reshape(devices, 2, rows, bins)
        moved = lax.all_to_all(lines, axes, split_axis=0, concat_axis=0, tiled=True)
        turned.append(moved.reshape(nrng, naz, 2, per_part, rows_in, bins))
    transform(CHUNKS - 2)
    transform(CHUNKS - 1)
    tables = (shift_table, filter_index, tap_table)
    blocks = np.arange(bins // BB)
    inner = (blocks >= HALO // BB) & (blocks < (bins - HALO) // BB)
    image = None
    for chosen, wide in ((inner, False), (~inner, True)):
        places = blocks[chosen].tolist()
        if not places:
            continue
        ids = np.concatenate([np.arange(BB) + BB * place for place in places])
        mover = mover_table(bins, ids, wide, *tables)
        halos = (lows, highs) if wide else ([], [])
        image = final(bins, mains, *halos, mover, rate[ids], places, image)
    return image
def solution(mesh):
    return jax.shard_map(
        functools.partial(local, mesh.shape["rng"], mesh.shape["az"]),
        mesh=mesh,
        in_specs=(
            P(None, "az", "rng"),
            P(),
            P(("rng", "az")),
            P(None, ("rng", "az")),
            P(None, ("rng", "az")),
            P(),
        ),
        out_specs=P(None, ("rng", "az"), None),
        check_vma=False,
    )
```

```python
import functools

import jax
import jax.numpy as jnp
import ml_dtypes
import numpy as np
from jax import lax
from jax.experimental import pallas as pl
from jax.experimental.pallas import tpu as pltpu
from jax.sharding import PartitionSpec as P

NRG = 4096
NAZ = 16384
GROUPS = 16
NFILT = 16
TAPS = 8
HALO = 32
LANES = 128
RG1 = NRG // LANES
CHUNKS = 8
PER_CHUNK = LANES // CHUNKS
VMEM_LIMIT = 60 << 20
BF16 = jnp.bfloat16
F32 = jnp.float32


def split_np(table):
    table = np.asarray(table, np.float32)
    high = table.astype(ml_dtypes.bfloat16)
    low = (table - high.astype(np.float32)).astype(ml_dtypes.bfloat16)
    return high, low


def unit(angle_num, period, sign):
    angles = (np.asarray(angle_num, np.int64) % period) * (2.0 * np.pi / period)
    return np.cos(angles), sign * np.sin(angles)


def dft_matrix(sign):
    ids = np.arange(LANES)
    return unit(ids[:, None] * ids[None, :], LANES, sign)


def right_tables(sign, scale=1.0):
    c, s = dft_matrix(sign)
    return split_np(np.block([[c, s], [-s, c]]) * scale)


def left_table(sign, scale=1.0, order=np.arange(LANES)):
    c, s = (part[:, order] for part in dft_matrix(sign))
    high, low = split_np(np.block([[c, -s], [s, c]]) * scale)
    return np.concatenate([high, high, low], axis=1)


def split(x):
    high = x.astype(BF16)
    low = (x - high.astype(F32)).astype(BF16)
    return high, low


def dot(a, b):
    return jnp.dot(a, b, preferred_element_type=F32)


def scale_by(value, re, im):
    a, b = value
    eps = 1e-12
    if abs(im) < eps:
        if abs(re - 1.0) < eps:
            return value
        if abs(re + 1.0) < eps:
            return -a, -b
    if abs(re) < eps:
        if abs(im - 1.0) < eps:
            return -b, a
        if abs(im + 1.0) < eps:
            return b, -a
    if abs(abs(re) - abs(im)) < eps:
        sr, si = (1.0 if re > 0 else -1.0), (1.0 if im > 0 else -1.0)
        h = abs(re)
        total, diff = (a + b) * h, (a - b) * h
        if si == sr:
            return (diff, total) if sr > 0 else (-diff, -total)
        return (total, -diff) if sr > 0 else (-total, diff)
    re, im = float(re), float(im)
    return a * re - b * im, a * im + b * re


def dft_list(values, sign):
    count = len(values)
    if count == 1:
        return values
    even, odd = dft_list(values[0::2], sign), dft_list(values[1::2], sign)
    first, second = [], []
    for k in range(count // 2):
        re, im = unit(k, count, sign)
        a, b = even[k], scale_by(odd[k], float(re), float(im))
        first.append((a[0] + b[0], a[1] + b[1]))
        second.append((a[0] - b[0], a[1] - b[1]))
    return first + second


def dft_two_step(load, mid_ref, finish, outer, inner, sign):
    for ib in range(inner):
        column = dft_list([load(ia * inner + ib) for ia in range(outer)], sign)
        for ka in range(outer):
            re, im = unit(ib * ka, outer * inner, sign)
            a, b = scale_by(column[ka], float(re), float(im))
            mid_ref[ka * inner + ib, 0] = a
            mid_ref[ka * inner + ib, 1] = b
    for ka in range(outer):
        row = [(mid_ref[ka * inner + ib, 0], mid_ref[ka * inner + ib, 1]) for ib in range(inner)]
        for kb, value in enumerate(dft_list(row, sign)):
            finish(ka + outer * kb, value)


def pack_kernel(chunks, parts, per_part, rows_in, rank_ref, x_ref, *out_refs):
    rank = rank_ref[0]
    for j in range(parts):
        part = jnp.bitwise_xor(rank, j)
        for at, c in enumerate(chunks):
            for m in range(per_part):
                start = CHUNKS * (part * per_part + m) + c
                for ri in range(2):
                    out_refs[at * parts + j][ri, 0, m * rows_in : (m + 1) * rows_in, :] = x_ref[
                        ri, pl.ds(start, rows_in, stride=LANES), :
                    ]


def pack(raw, rank, parts, chunks):
    lines, bins = raw.shape[1], raw.shape[2]
    rows_in, tiles, per_part = lines // LANES, bins // LANES, PER_CHUNK // parts
    rows = per_part * rows_in
    count = len(chunks) * parts
    shape = jax.ShapeDtypeStruct((2, tiles, rows, LANES), F32)
    spec = pl.BlockSpec((2, 1, rows, LANES), lambda i: (0, i, 0, 0))
    flat = pl.pallas_call(
        functools.partial(pack_kernel, chunks, parts, per_part, rows_in),
        grid=(tiles,),
        in_specs=[
            pl.BlockSpec(memory_space=pltpu.SMEM),
            pl.BlockSpec((2, lines, LANES), lambda i: (0, 0, i)),
        ],
        out_specs=[spec] * count,
        out_shape=[shape] * count,
        compiler_params=pltpu.CompilerParams(vmem_limit_bytes=VMEM_LIMIT),
        cost_estimate=pl.CostEstimate(flops=0, bytes_accessed=16 * lines * bins, transcendentals=0),
        name="pack",
    )(rank, raw)
    return [flat[i * parts : (i + 1) * parts] for i in range(len(chunks))]


STEP = 16


def compress_kernel(parts, rows, rank_ref, *refs):
    x_refs = refs[:parts]
    chirp_ref, tw_ref, fwd_ref, fwd_low_ref, inv_ref, inv_low_ref = refs[parts : parts + 6]
    out_ref, buf_ref, lhs_ref, y_ref, mid_ref, sems = refs[parts + 6 :]
    tiles = buf_ref.shape[3]
    rank = rank_ref[0]
    step = pl.program_id(0)
    slot = lax.rem(step, 2)

    def copies(at, to):
        return [
            pltpu.make_async_copy(
                x_refs[j].at[:, :, pl.ds(pl.multiple_of(at * rows, rows), rows), :],
                buf_ref.at[to, jnp.bitwise_xor(rank, j)],
                sems.at[to, j],
            )
            for j in range(parts)
        ]

    @pl.when(step == 0)
    def _():
        for copy in copies(step, slot):
            copy.start()

    @pl.when(step + 1 < pl.num_programs(0))
    def _():
        for copy in copies(step + 1, 1 - slot):
            copy.start()

    for copy in copies(step, slot):
        copy.wait()

    def put(at, re, im):
        for half, part in enumerate((re, im)):
            high, low = split(part)
            lhs_ref[at, half * LANES : (half + 1) * LANES] = high
            lhs_ref[at, (2 + half) * LANES : (3 + half) * LANES] = low

    def forward(i, carry):
        at = pl.ds(pl.multiple_of(i * STEP, STEP), STEP)

        def load(p):
            source = buf_ref.at[slot, p // tiles]
            return source[0, p % tiles, at, :], source[1, p % tiles, at, :]

        def finish(k, value):
            wr, wi = tw_ref[0, k : k + 1, :], tw_ref[1, k : k + 1, :]
            a, b = value
            put(
                pl.ds(pl.multiple_of(k * rows + i * STEP, STEP), STEP),
                a * wr - b * wi,
                a * wi + b * wr,
            )

        dft_two_step(load, mid_ref, finish, 4, RG1 // 4, -1.0)
        return carry

    lax.fori_loop(0, rows // STEP, forward, 0)

    group = max(1, LANES // rows)

    def middle(i, carry):
        at = pl.ds(pl.multiple_of(i * group * rows, group * rows), group * rows)
        y = dot(lhs_ref[at, :], fwd_ref[...]) + dot(lhs_ref[at, 0 : 2 * LANES], fwd_low_ref[...])
        for s in range(group):
            k = i * group + s
            cr, ci = chirp_ref[0, pl.ds(k, 1), :], chirp_ref[1, pl.ds(k, 1), :]
            a = y[s * rows : (s + 1) * rows, 0:LANES]
            b = y[s * rows : (s + 1) * rows, LANES : 2 * LANES]
            put(pl.ds(pl.multiple_of(k * rows, rows), rows), a * cr - b * ci, a * ci + b * cr)
        z = dot(lhs_ref[at, :], inv_ref[...]) + dot(lhs_ref[at, 0 : 2 * LANES], inv_low_ref[...])
        for s in range(group):
            k = i * group + s
            wr, wi = tw_ref[0, pl.ds(k, 1), :], tw_ref[1, pl.ds(k, 1), :]
            a = z[s * rows : (s + 1) * rows, 0:LANES]
            b = z[s * rows : (s + 1) * rows, LANES : 2 * LANES]
            y_ref[k, 0] = a * wr + b * wi
            y_ref[k, 1] = b * wr - a * wi
        return carry

    lax.fori_loop(0, RG1 // group, middle, 0)

    def backward(i, carry):
        at = pl.ds(pl.multiple_of(i * STEP, STEP), STEP)

        def load(k):
            return y_ref[k, 0, at, :], y_ref[k, 1, at, :]

        def finish(p, value):
            out_ref[p, 0, at, :] = value[0]
            out_ref[p, 1, at, :] = value[1]

        dft_two_step(load, mid_ref, finish, 4, RG1 // 4, 1.0)
        return carry

    lax.fori_loop(0, rows // STEP, backward, 0)


def whole_spec(array):
    zeros = (0,) * array.ndim
    return pl.BlockSpec(array.shape, lambda *_: zeros)


def compress(pieces, rank, chirp):
    parts = len(pieces)
    _, tiles, rows, _ = pieces[0].shape
    block = min(rows, 32)
    ids = np.arange(RG1)[:, None] * np.arange(LANES)[None, :]
    tw = jnp.asarray(np.stack(unit(ids, NRG, -1.0)), F32)
    fwd, fwd_low = right_tables(-1.0)
    inv, inv_low = right_tables(1.0, 1.0 / NRG)
    consts = [
        chirp,
        tw,
        jnp.asarray(np.concatenate([fwd, fwd])),
        jnp.asarray(fwd_low),
        jnp.asarray(np.concatenate([inv, inv])),
        jnp.asarray(inv_low),
    ]
    points = rows * NRG
    return pl.pallas_call(
        functools.partial(compress_kernel, parts, block),
        grid=(rows // block,),
        in_specs=[pl.BlockSpec(memory_space=pltpu.SMEM)]
        + [pl.BlockSpec(memory_space=pl.ANY)] * parts
        + [whole_spec(a) for a in consts],
        out_specs=pl.BlockSpec((RG1, 2, block, LANES), lambda i: (0, 0, i, 0)),
        out_shape=jax.ShapeDtypeStruct((RG1, 2, rows, LANES), F32),
        scratch_shapes=[
            pltpu.VMEM((2, parts, 2, tiles, block, LANES), F32),
            pltpu.VMEM((RG1 * block, 4 * LANES), BF16),
            pltpu.VMEM((RG1, 2, block, LANES), F32),
            pltpu.VMEM((RG1, 2, STEP, LANES), F32),
            pltpu.SemaphoreType.DMA((2, parts)),
        ],
        compiler_params=pltpu.CompilerParams(vmem_limit_bytes=VMEM_LIMIT),
        cost_estimate=pl.CostEstimate(
            flops=points * 8 * LANES * 6, bytes_accessed=16 * points, transcendentals=0
        ),
        name="compress",
    )(rank, *pieces, *consts)


def azimuth_kernel(chunk, x_ref, tw_ref, fwd_ref, fwd_low_ref, out_ref, up_ref, down_ref, t_ref, mid_ref):
    part = pl.program_id(0)
    pieces, per_part, bins = x_ref.shape[1], x_ref.shape[3], x_ref.shape[5]

    def stage(m, carry):
        sides = []
        for ri in range(2):
            column = jnp.concatenate([x_ref[0, a, ri, m] for a in range(pieces)], axis=0)
            sides.append(split(jnp.transpose(column)))
        high = jnp.concatenate([sides[0][0], sides[1][0]], axis=1)
        low = jnp.concatenate([sides[0][1], sides[1][1]], axis=1)
        y = dot(high, fwd_ref[...]) + dot(low, fwd_ref[...]) + dot(high, fwd_low_ref[...])
        index = part * per_part + m
        at = pl.ds(CHUNKS * index + chunk, 1)
        wr, wi = tw_ref[0, at, :], tw_ref[1, at, :]
        a, b = y[:, 0:LANES], y[:, LANES : 2 * LANES]
        t_ref[index, 0] = a * wr - b * wi
        t_ref[index, 1] = a * wi + b * wr
        return carry

    lax.fori_loop(0, per_part, stage, 0)

    @pl.when(part == pl.num_programs(0) - 1)
    def _():
        def rest(i, carry):
            at = pl.ds(pl.multiple_of(i * STEP, STEP), STEP)

            def load(m):
                return t_ref[m, 0, at, :], t_ref[m, 1, at, :]

            def finish(k, value):
                re, im = unit(chunk * k, LANES, -1.0)
                a, b = scale_by(value, float(re), float(im))
                out_ref[k, 0, at, :] = a
                out_ref[k, 1, at, :] = b

            dft_two_step(load, mid_ref, finish, 4, PER_CHUNK // 4, -1.0)
            return carry

        lax.fori_loop(0, bins // STEP, rest, 0)

        def edges(k, carry):
            for ri in range(2):
                up_ref[k, ri] = out_ref[k, ri, bins - HALO : bins, :]
                down_ref[k, ri] = out_ref[k, ri, 0:HALO, :]
            return carry

        lax.fori_loop(0, PER_CHUNK, edges, 0)


def azimuth(x, chunk):
    parts, pieces, _, per_part, rows_in, bins = x.shape
    ids = np.arange(LANES)
    tw = jnp.asarray(np.stack(unit(ids[:, None] * ids[None, :], NAZ, -1.0)), F32)
    fwd, fwd_low = right_tables(-1.0)
    consts = [tw, jnp.asarray(fwd), jnp.asarray(fwd_low)]
    points = PER_CHUNK * LANES * bins
    shape = (PER_CHUNK, 2, bins, LANES)
    edge = (PER_CHUNK, 2, HALO, LANES)
    return pl.pallas_call(
        functools.partial(azimuth_kernel, chunk),
        grid=(parts,),
        in_specs=[
            pl.BlockSpec(
                (1, pieces, 2, per_part, rows_in, bins), lambda i: (i, 0, 0, 0, 0, 0)
            )
        ]
        + [whole_spec(a) for a in consts],
        out_specs=[pl.BlockSpec(s, lambda i: (0, 0, 0, 0)) for s in (shape, edge, edge)],
        out_shape=[jax.ShapeDtypeStruct(s, F32) for s in (shape, edge, edge)],
        scratch_shapes=[pltpu.VMEM(shape, F32), pltpu.VMEM((PER_CHUNK, 2, STEP, LANES), F32)],
        compiler_params=pltpu.CompilerParams(vmem_limit_bytes=VMEM_LIMIT),
        cost_estimate=pl.CostEstimate(
            flops=points * 8 * LANES * 3, bytes_accessed=16 * points, transcendentals=0
        ),
        name=f"azimuth{chunk}",
    )(x, *consts)


KB = 4
BB = 8
QUAD = 4


def fit(fn, even):
    nodes = np.cos((2 * np.arange(64) + 1) * np.pi / 128) * 0.25
    z2 = (nodes + 0.25) / 2
    z = np.sqrt(z2)
    goal = fn(np.pi * z) if even else fn(np.pi * z) / z
    return [float(v) for v in np.polynomial.polynomial.polyfit(z2, goal, 4)]


SIN_FIT, COS_FIT = fit(np.sin, False), fit(np.cos, True)


def horner(coefficients, x):
    total = coefficients[-1]
    for c in reversed(coefficients[:-1]):
        total = total * x + c
    return total


def turn(t):
    z = t - jnp.round(t)
    z2 = z * z
    s = horner(SIN_FIT, z2) * z
    c = horner(COS_FIT, z2)
    twice = s + s
    return 1.0 - twice * s, twice * c


def phase_kernel(part, sets, *refs):
    k = pl.program_id(0)
    for rate_ref, out_ref in zip(refs[:sets], refs[sets:]):
        for half in range(2):
            k2 = k + PER_CHUNK * (2 * part + half)
            f = k2 * LANES + lax.broadcasted_iota(jnp.int32, (1, LANES), 1)
            centred = jnp.where(f >= NAZ // 2, f - NAZ, f).astype(F32) * (1.0 / NAZ)
            c, s = turn(rate_ref[...] * (centred * centred))
            out_ref[half, 0, 0] = c
            out_ref[half, 0, 1] = s


def phase_tables(rates, part):
    shapes = [(2, PER_CHUNK, 2, rate.shape[0], LANES) for rate in rates]
    points = sum(2 * PER_CHUNK * rate.size for rate in rates)
    return pl.pallas_call(
        functools.partial(phase_kernel, part, len(rates)),
        grid=(PER_CHUNK,),
        in_specs=[whole_spec(rate) for rate in rates],
        out_specs=[
            pl.BlockSpec((2, 1) + shape[2:], lambda i: (0, i, 0, 0, 0)) for shape in shapes
        ],
        out_shape=[jax.ShapeDtypeStruct(shape, F32) for shape in shapes],
        compiler_params=pltpu.CompilerParams(vmem_limit_bytes=VMEM_LIMIT),
        cost_estimate=pl.CostEstimate(
            flops=40 * points, bytes_accessed=8 * points, transcendentals=0
        ),
        name="phase",
    )(*rates)


def combine(sources, kk, start, put):
    at = slice(start, start + STEP)
    values = [(ref[kk, 0, at, :], ref[kk, 1, at, :]) for ref in sources]
    for q, value in enumerate(dft_list(values, -1.0)):
        for half, part in enumerate(value):
            high, low = split(part)
            put(q, slice(half * LANES, (half + 1) * LANES), high, low)


def final_kernel(steps, joins, wide, *refs):
    refs = list(refs)

    def take(count):
        taken = refs[:count]
        del refs[:count]
        return taken

    sources = take(CHUNKS) if joins else take(1)
    low_refs, high_refs = (take(CHUNKS), take(CHUNKS)) if wide else ((), ())
    phase_refs = take(CHUNKS // 2)
    mover_refs = take(2 if wide else 1)
    inv1_ref, inv2_ref, tw_ref = take(3)
    out_ref, own_ref, zr_ref, zi_ref, s_ref, swap_ref = refs[-7:-1] if wide else refs[-6:]
    halo_ref = refs[-1]
    if not joins:
        own_ref = sources[0]
    own = own_ref.shape[2] // 2
    rows = phase_refs[0].shape[3]
    step = pl.program_id(0)

    @pl.when(step < steps)
    def _():
        def one(kk, buf):
            k = step * KB + kk
            if joins:
                for start in range(0, own, STEP):

                    def put_own(q, cols, high, low, start=start):
                        own_ref[q, kk, start : start + STEP, cols] = high
                        own_ref[q, kk, own + start : own + start + STEP, cols] = low

                    combine(sources, kk, start, put_own)
            if wide:
                for side, halo_refs in enumerate((low_refs, high_refs)):
                    for start in range(0, HALO, STEP):

                        def put_halo(q, cols, high, low, at=side * HALO + start):
                            halo_ref[buf, q, at : at + STEP, cols] = high
                            halo_ref[buf, q, 2 * HALO + at : 2 * HALO + at + STEP, cols] = low

                        combine(halo_refs, kk, start, put_halo)
            for q in range(CHUNKS):
                k2 = k + PER_CHUNK * q
                band = lax.div(k2, LANES // GROUPS)
                moved = dot(mover_refs[0][band], own_ref[q, kk])
                if wide:
                    moved = moved + dot(mover_refs[1][band], halo_ref[buf, q])
                both = moved[0:rows, :] + moved[rows : 2 * rows, :]
                c, s = phase_refs[q // 2][q % 2, kk, 0], phase_refs[q // 2][q % 2, kk, 1]
                a, b = both[:, 0:LANES], both[:, LANES : 2 * LANES]
                swap_ref[buf, 0, q] = a * c + b * s
                swap_ref[buf, 1, q] = b * c - a * s
            to = pl.ds(pl.multiple_of(k * CHUNKS, CHUNKS), CHUNKS)
            for start in range(0, rows, BB):
                at = slice(start, start + BB)
                zr_ref[at, to, :] = jnp.swapaxes(swap_ref[buf, 0, :, at, :], 0, 1)
                zi_ref[at, to, :] = jnp.swapaxes(swap_ref[buf, 1, :, at, :], 0, 1)

        def first(i, carry):
            one(2 * i, 0)
            one(2 * i + 1, 1)
            return carry

        lax.fori_loop(0, KB // 2, first, 0)

    @pl.when(step >= steps)
    def _():
        base = (step - steps) * BB

        def some(j, carry):
            cols = []
            for t in range(QUAD):
                at = base + QUAD * j + t
                cols.append(jnp.concatenate([zr_ref[at], zi_ref[at]], axis=0))
            hi, lo = split(jnp.concatenate(cols, axis=1))
            w = dot(inv1_ref[...], jnp.concatenate([hi, lo, hi], axis=0))
            turned = []
            for t in range(QUAD):
                a = w[0:LANES, t * LANES : (t + 1) * LANES]
                b = w[LANES : 2 * LANES, t * LANES : (t + 1) * LANES]
                wr, wi = tw_ref[0], tw_ref[1]
                turned.append(jnp.concatenate([a * wr - b * wi, a * wi + b * wr], axis=1))
            hi, lo = split(jnp.concatenate(turned, axis=0))
            image = lax.dot_general(
                inv2_ref[...],
                jnp.concatenate([hi, lo, hi], axis=1),
                (((1,), (1,)), ((), ())),
                preferred_element_type=F32,
            )
            for t in range(QUAD):
                for ri in range(2):
                    s_ref[ri, QUAD * j + t] = image[
                        ri * LANES : (ri + 1) * LANES, t * LANES : (t + 1) * LANES
                    ]
            return carry

        lax.fori_loop(0, BB // QUAD, some, 0)
        for ri in range(2):
            for start in range(0, LANES, 8):
                lines = jnp.swapaxes(s_ref[ri, :, start : start + 8, :], 0, 1)
                for n in range(8):
                    at = (start + n) * LANES
                    out_ref[ri, :, at : at + LANES] = lines[n]


def final(bins, places, sources, lows, highs, phases, movers, image=None):
    joins, wide = len(sources) > 1, len(lows) > 0
    rows = len(places) * BB
    steps = PER_CHUNK // KB
    ids = np.arange(LANES)
    tw = jnp.asarray(np.stack(unit(ids[:, None] * ids[None, :], NAZ, 1.0)), F32)
    consts = [
        *movers,
        jnp.asarray(left_table(1.0, 1.0, ids // CHUNKS + PER_CHUNK * (ids % CHUNKS))),
        jnp.asarray(left_table(1.0, 1.0 / NAZ)),
        tw,
    ]
    start, gap_at = places[0], len(places)
    for i, place in enumerate(places):
        if place != start + i:
            gap_at = i
            break
    gap = places[-1] - start - len(places) + 1

    def early(i):
        return (jnp.minimum(i, steps - 1), 0, 0, 0)

    def early_second(i):
        return (0, jnp.minimum(i, steps - 1), 0, 0)

    def late(i):
        at = jnp.maximum(i - steps, 0)
        return (0, start + at + jnp.where(at >= gap_at, gap, 0), 0)

    joined = (CHUNKS, PER_CHUNK, 2 * bins, 2 * LANES)
    joined_spec = pl.BlockSpec((CHUNKS, KB, 2 * bins, 2 * LANES), early_second)
    given = [*sources, *lows, *highs, *phases, *consts]
    specs = [pl.BlockSpec((KB, 2, bins, LANES), early)] * CHUNKS if joins else [joined_spec]
    specs += [pl.BlockSpec((KB, 2, HALO, LANES), early)] * (2 * CHUNKS if wide else 0)
    specs += [
        pl.BlockSpec((2, KB, 2, rows, LANES), lambda i: (0, jnp.minimum(i, steps - 1), 0, 0, 0))
    ] * len(phases)
    specs += [whole_spec(a) for a in consts]
    aliases = {}
    if image is not None:
        aliases = {len(given): 0}
        given.append(image)
        specs.append(pl.BlockSpec(memory_space=pl.ANY))
    shapes = [jax.ShapeDtypeStruct((2, bins, NAZ), F32)]
    out_specs = [pl.BlockSpec((2, BB, NAZ), late)]
    scratch = []
    if joins and wide:
        scratch.append(pltpu.VMEM((CHUNKS, KB, 2 * bins, 2 * LANES), BF16))
    elif joins:
        shapes.append(jax.ShapeDtypeStruct(joined, BF16))
        out_specs.append(joined_spec)
    else:
        scratch.append(pltpu.VMEM((16, LANES), BF16))
    scratch += [
        pltpu.VMEM((rows, LANES, LANES), F32),
        pltpu.VMEM((rows, LANES, LANES), F32),
        pltpu.VMEM((2, BB, LANES, LANES), F32),
        pltpu.VMEM((2, 2, CHUNKS, rows, LANES), F32),
    ]
    if wide:
        scratch.append(pltpu.VMEM((2, CHUNKS, 4 * HALO, 2 * LANES), BF16))
    points = NAZ * rows
    return pl.pallas_call(
        functools.partial(final_kernel, steps, joins, wide),
        grid=(steps + len(places),),
        in_specs=specs,
        out_specs=out_specs,
        out_shape=shapes,
        scratch_shapes=scratch,
        input_output_aliases=aliases,
        compiler_params=pltpu.CompilerParams(vmem_limit_bytes=VMEM_LIMIT),
        cost_estimate=pl.CostEstimate(
            flops=points * 8 * LANES * 9, bytes_accessed=28 * points, transcendentals=0
        ),
        name="final_wide" if wide else "final_inner",
    )(*given)


def mover_table(rows, columns, shift_table, filter_index, tap_table):
    shift_table, filter_index = shift_table[:, rows], filter_index[:, rows]
    onehot = (filter_index[:, :, None] == jnp.arange(NFILT, dtype=jnp.int32)).astype(F32)
    weights = jnp.einsum("gbf,ft->gbt", onehot, tap_table, precision=lax.Precision.HIGHEST)
    first = rows[None, :].astype(np.int32) + shift_table + (HALO - 4)
    offset = columns.astype(np.int32)[None, None, :] - first[:, :, None]
    table = jnp.zeros(offset.shape, F32)
    for t in range(TAPS):
        table = table + jnp.where(offset == t, weights[:, :, t : t + 1], 0.0)
    high = lax.reduce_precision(table, 8, 7)
    low = table - high
    top = jnp.concatenate([high, high], axis=2)
    bottom = jnp.concatenate([low, jnp.zeros_like(low)], axis=2)
    return jnp.concatenate([top, bottom], axis=1).astype(BF16)


def own_columns(bins):
    return np.arange(HALO, HALO + bins)


def halo_columns(bins):
    return np.concatenate([np.arange(HALO), np.arange(bins + HALO, bins + 2 * HALO)])


def row_sets(bins):
    blocks = np.arange(bins // BB)
    inner = (blocks >= HALO // BB) & (blocks < (bins - HALO) // BB)
    return [blocks[chosen].tolist() for chosen in (inner, ~inner) if chosen.any()]


def bins_of(places):
    return np.concatenate([np.arange(BB) + BB * place for place in places])


def neighbours(axes, size, step):
    return [(i, i + step) for i in range(size) if 0 <= i + step < size]


def local(nrng, naz, raw_echo, chirp_spectrum, azimuth_rate, shift_table, filter_index, tap_table):
    axes = ("rng", "az")
    devices = nrng * naz
    bins = NRG // devices
    rows_in = raw_echo.shape[1] // LANES
    per_part = PER_CHUNK // nrng
    rows = per_part * rows_in
    chirp = chirp_spectrum.reshape(2, LANES, RG1).transpose(0, 2, 1)
    rate = jnp.broadcast_to((azimuth_rate * 0.5)[:, None], (bins, LANES))
    rank = lax.axis_index("rng").astype(jnp.int32).reshape(1)
    packed = pack(raw_echo, rank, nrng, [0]) + pack(raw_echo, rank, nrng, list(range(1, CHUNKS)))
    mains, lows, highs = [], [], []
    turned = []

    def gather(c):
        return [packed[c][0]] + [
            lax.ppermute(packed[c][j], "rng", [(i, i ^ j) for i in range(nrng)])
            for j in range(1, nrng)
        ]

    def transform(c):
        if c > 0:
            turned[c], mains[c - 1] = lax.optimization_barrier((turned[c], mains[c - 1]))
        main, up, down = azimuth(turned[c], c)
        mains.append(main)
        lows.append(lax.ppermute(up, axes, neighbours(axes, devices, 1)))
        highs.append(lax.ppermute(down, axes, neighbours(axes, devices, -1)))

    places = row_sets(bins)
    rates = [rate[bins_of(p)] for p in places]
    phases = []
    got = [gather(0)]
    packed[1], got[0] = lax.optimization_barrier((packed[1], got[0]))
    got.append(gather(1))
    for c in range(CHUNKS):
        lines = compress(got[c], rank, chirp)
        if c + 1 < CHUNKS:
            lines, got[c + 1] = lax.optimization_barrier((lines, got[c + 1]))
        if c + 2 < CHUNKS:
            packed[c + 2], got[c + 1] = lax.optimization_barrier((packed[c + 2], got[c + 1]))
            if c >= 1:
                held = (packed[c + 2], turned[c - 1])
                packed[c + 2], turned[c - 1] = lax.optimization_barrier(held)
            got.append(gather(c + 2))
        if c >= 2:
            transform(c - 2)
            lines, mains[c - 2] = lax.optimization_barrier((lines, mains[c - 2]))
            if c - 2 < CHUNKS // 2:
                rates, turned[c - 2] = lax.optimization_barrier((rates, turned[c - 2]))
                table = phase_tables(rates, c - 2)
                lines, table = lax.optimization_barrier((lines, table))
                phases.append(table)
        if c >= 3:
            held = (lines, lows[c - 3], highs[c - 3])
            lines, lows[c - 3], highs[c - 3] = lax.optimization_barrier(held)
        if bins < LANES:
            cut = lines.reshape(RG1, 2, rows, LANES // bins, bins)
            lines = cut.transpose(0, 3, 1, 2, 4).reshape(devices, 2, rows, bins)
        moved = lax.all_to_all(lines, axes, split_axis=0, concat_axis=0, tiled=True)
        turned.append(moved.reshape(nrng, naz, 2, per_part, rows_in, bins))
    transform(CHUNKS - 2)
    transform(CHUNKS - 1)
    tables = (shift_table, filter_index, tap_table)
    image, sources = None, mains
    for i, places_of in enumerate(places):
        ids = bins_of(places_of)
        wide = i == len(places) - 1
        halos = (lows, highs) if wide else ([], [])
        columns = [own_columns(bins), halo_columns(bins)] if wide else [own_columns(bins)]
        movers = [mover_table(ids, cols, *tables) for cols in columns]
        result = final(
            bins, places_of, sources, *halos, [table[i] for table in phases], movers, image
        )
        image, sources = result[0], result[1:]
    return image


def solution(mesh):
    return jax.shard_map(
        functools.partial(local, mesh.shape["rng"], mesh.shape["az"]),
        mesh=mesh,
        in_specs=(
            P(None, "az", "rng"),
            P(),
            P(("rng", "az")),
            P(None, ("rng", "az")),
            P(None, ("rng", "az")),
            P(),
        ),
        out_specs=P(None, ("rng", "az"), None),
        check_vma=False,
    )
```

```python
import functools

import jax
import jax.numpy as jnp
import ml_dtypes
import numpy as np
from jax import lax
from jax.experimental import pallas as pl
from jax.experimental.pallas import tpu as pltpu
from jax.sharding import PartitionSpec as P

NRG = 4096
NAZ = 16384
GROUPS = 16
NFILT = 16
TAPS = 8
HALO = 32
LANES = 128
RG1 = NRG // LANES
CHUNKS = 8
PER_CHUNK = LANES // CHUNKS
GROUPED = ((0,), (1,), (2, 3), (4, 5), (6,), (7,))
VMEM_LIMIT = 60 << 20
BF16 = jnp.bfloat16
F32 = jnp.float32


def split_np(table):
    table = np.asarray(table, np.float32)
    high = table.astype(ml_dtypes.bfloat16)
    low = (table - high.astype(np.float32)).astype(ml_dtypes.bfloat16)
    return high, low


def unit(angle_num, period, sign):
    angles = (np.asarray(angle_num, np.int64) % period) * (2.0 * np.pi / period)
    return np.cos(angles), sign * np.sin(angles)


def dft_matrix(sign):
    ids = np.arange(LANES)
    return unit(ids[:, None] * ids[None, :], LANES, sign)


def right_tables(sign, scale=1.0):
    c, s = dft_matrix(sign)
    return split_np(np.block([[c, s], [-s, c]]) * scale)


def left_table(sign, scale=1.0, order=np.arange(LANES)):
    c, s = (part[:, order] for part in dft_matrix(sign))
    high, low = split_np(np.block([[c, -s], [s, c]]) * scale)
    return np.concatenate([high, high, low], axis=1)


def split(x):
    high = x.astype(BF16)
    low = (x - high.astype(F32)).astype(BF16)
    return high, low


def dot(a, b):
    return jnp.dot(a, b, preferred_element_type=F32)


def scale_by(value, re, im):
    a, b = value
    eps = 1e-12
    if abs(im) < eps:
        if abs(re - 1.0) < eps:
            return value
        if abs(re + 1.0) < eps:
            return -a, -b
    if abs(re) < eps:
        if abs(im - 1.0) < eps:
            return -b, a
        if abs(im + 1.0) < eps:
            return b, -a
    if abs(abs(re) - abs(im)) < eps:
        sr, si = (1.0 if re > 0 else -1.0), (1.0 if im > 0 else -1.0)
        h = abs(re)
        total, diff = (a + b) * h, (a - b) * h
        if si == sr:
            return (diff, total) if sr > 0 else (-diff, -total)
        return (total, -diff) if sr > 0 else (-total, diff)
    re, im = float(re), float(im)
    return a * re - b * im, a * im + b * re


def dft_list(values, sign):
    count = len(values)
    if count == 1:
        return values
    even, odd = dft_list(values[0::2], sign), dft_list(values[1::2], sign)
    first, second = [], []
    for k in range(count // 2):
        re, im = unit(k, count, sign)
        a, b = even[k], scale_by(odd[k], float(re), float(im))
        first.append((a[0] + b[0], a[1] + b[1]))
        second.append((a[0] - b[0], a[1] - b[1]))
    return first + second


def dft_two_step(load, mid_ref, finish, outer, inner, sign):
    for ib in range(inner):
        column = dft_list([load(ia * inner + ib) for ia in range(outer)], sign)
        for ka in range(outer):
            re, im = unit(ib * ka, outer * inner, sign)
            a, b = scale_by(column[ka], float(re), float(im))
            mid_ref[ka * inner + ib, 0] = a
            mid_ref[ka * inner + ib, 1] = b
    for ka in range(outer):
        row = [(mid_ref[ka * inner + ib, 0], mid_ref[ka * inner + ib, 1]) for ib in range(inner)]
        for kb, value in enumerate(dft_list(row, sign)):
            finish(ka + outer * kb, value)


def pack_kernel(groups, parts, per_part, rows_in, rank_ref, x_ref, *out_refs):
    rank = rank_ref[0]
    for j in range(parts):
        part = jnp.bitwise_xor(rank, j)
        for g, chunks in enumerate(groups):
            for at, c in enumerate(chunks):
                for m in range(per_part):
                    start = CHUNKS * (part * per_part + m) + c
                    to = (at * per_part + m) * rows_in
                    for ri in range(2):
                        out_refs[g * parts + j][ri, 0, to : to + rows_in, :] = x_ref[
                            ri, pl.ds(start, rows_in, stride=LANES), :
                        ]


def pack(raw, rank, parts, groups):
    lines, bins = raw.shape[1], raw.shape[2]
    rows_in, tiles, per_part = lines // LANES, bins // LANES, PER_CHUNK // parts
    heights = [len(chunks) * per_part * rows_in for chunks in groups for _ in range(parts)]
    flat = pl.pallas_call(
        functools.partial(pack_kernel, groups, parts, per_part, rows_in),
        grid=(tiles,),
        in_specs=[
            pl.BlockSpec(memory_space=pltpu.SMEM),
            pl.BlockSpec((2, lines, LANES), lambda i: (0, 0, i)),
        ],
        out_specs=[pl.BlockSpec((2, 1, rows, LANES), lambda i: (0, i, 0, 0)) for rows in heights],
        out_shape=[jax.ShapeDtypeStruct((2, tiles, rows, LANES), F32) for rows in heights],
        compiler_params=pltpu.CompilerParams(vmem_limit_bytes=VMEM_LIMIT),
        cost_estimate=pl.CostEstimate(flops=0, bytes_accessed=16 * lines * bins, transcendentals=0),
        name="pack",
    )(rank, raw)
    return [flat[i * parts : (i + 1) * parts] for i in range(len(groups))]


STEP = 16


def compress_kernel(parts, rows, rank_ref, *refs):
    x_refs = refs[:parts]
    chirp_ref, tw_ref, fwd_ref, fwd_low_ref, inv_ref, inv_low_ref = refs[parts : parts + 6]
    out_ref, buf_ref, lhs_ref, y_ref, mid_ref, sems = refs[parts + 6 :]
    tiles = buf_ref.shape[3]
    rank = rank_ref[0]
    step = pl.program_id(0)
    slot = lax.rem(step, 2)

    def copies(at, to):
        return [
            pltpu.make_async_copy(
                x_refs[j].at[:, :, pl.ds(pl.multiple_of(at * rows, rows), rows), :],
                buf_ref.at[to, jnp.bitwise_xor(rank, j)],
                sems.at[to, j],
            )
            for j in range(parts)
        ]

    @pl.when(step == 0)
    def _():
        for copy in copies(step, slot):
            copy.start()

    @pl.when(step + 1 < pl.num_programs(0))
    def _():
        for copy in copies(step + 1, 1 - slot):
            copy.start()

    for copy in copies(step, slot):
        copy.wait()

    def put(at, re, im):
        for half, part in enumerate((re, im)):
            high, low = split(part)
            lhs_ref[at, half * LANES : (half + 1) * LANES] = high
            lhs_ref[at, (2 + half) * LANES : (3 + half) * LANES] = low

    def forward(i, carry):
        at = pl.ds(pl.multiple_of(i * STEP, STEP), STEP)

        def load(p):
            source = buf_ref.at[slot, p // tiles]
            return source[0, p % tiles, at, :], source[1, p % tiles, at, :]

        def finish(k, value):
            wr, wi = tw_ref[0, k : k + 1, :], tw_ref[1, k : k + 1, :]
            a, b = value
            put(
                pl.ds(pl.multiple_of(k * rows + i * STEP, STEP), STEP),
                a * wr - b * wi,
                a * wi + b * wr,
            )

        dft_two_step(load, mid_ref, finish, 4, RG1 // 4, -1.0)
        return carry

    lax.fori_loop(0, rows // STEP, forward, 0)

    group = max(1, 2 * LANES // rows)

    def middle(i, carry):
        at = pl.ds(pl.multiple_of(i * group * rows, group * rows), group * rows)
        y = dot(lhs_ref[at, :], fwd_ref[...]) + dot(lhs_ref[at, 0 : 2 * LANES], fwd_low_ref[...])
        for s in range(group):
            k = i * group + s
            cr, ci = chirp_ref[0, pl.ds(k, 1), :], chirp_ref[1, pl.ds(k, 1), :]
            a = y[s * rows : (s + 1) * rows, 0:LANES]
            b = y[s * rows : (s + 1) * rows, LANES : 2 * LANES]
            put(pl.ds(pl.multiple_of(k * rows, rows), rows), a * cr - b * ci, a * ci + b * cr)
        z = dot(lhs_ref[at, :], inv_ref[...]) + dot(lhs_ref[at, 0 : 2 * LANES], inv_low_ref[...])
        for s in range(group):
            k = i * group + s
            wr, wi = tw_ref[0, pl.ds(k, 1), :], tw_ref[1, pl.ds(k, 1), :]
            a = z[s * rows : (s + 1) * rows, 0:LANES]
            b = z[s * rows : (s + 1) * rows, LANES : 2 * LANES]
            y_ref[k, 0] = a * wr + b * wi
            y_ref[k, 1] = b * wr - a * wi
        return carry

    lax.fori_loop(0, RG1 // group, middle, 0)

    def backward(i, carry):
        at = pl.ds(pl.multiple_of(i * STEP, STEP), STEP)

        def load(k):
            return y_ref[k, 0, at, :], y_ref[k, 1, at, :]

        def finish(p, value):
            out_ref[p, 0, at, :] = value[0]
            out_ref[p, 1, at, :] = value[1]

        dft_two_step(load, mid_ref, finish, 4, RG1 // 4, 1.0)
        return carry

    lax.fori_loop(0, rows // STEP, backward, 0)


def whole_spec(array):
    zeros = (0,) * array.ndim
    return pl.BlockSpec(array.shape, lambda *_: zeros)


def compress(pieces, rank, chirp):
    parts = len(pieces)
    _, tiles, rows, _ = pieces[0].shape
    block = min(rows, 64)
    ids = np.arange(RG1)[:, None] * np.arange(LANES)[None, :]
    tw = jnp.asarray(np.stack(unit(ids, NRG, -1.0)), F32)
    fwd, fwd_low = right_tables(-1.0)
    inv, inv_low = right_tables(1.0, 1.0 / NRG)
    consts = [
        chirp,
        tw,
        jnp.asarray(np.concatenate([fwd, fwd])),
        jnp.asarray(fwd_low),
        jnp.asarray(np.concatenate([inv, inv])),
        jnp.asarray(inv_low),
    ]
    points = rows * NRG
    return pl.pallas_call(
        functools.partial(compress_kernel, parts, block),
        grid=(rows // block,),
        in_specs=[pl.BlockSpec(memory_space=pltpu.SMEM)]
        + [pl.BlockSpec(memory_space=pl.ANY)] * parts
        + [whole_spec(a) for a in consts],
        out_specs=pl.BlockSpec((RG1, 2, block, LANES), lambda i: (0, 0, i, 0)),
        out_shape=jax.ShapeDtypeStruct((RG1, 2, rows, LANES), F32),
        scratch_shapes=[
            pltpu.VMEM((2, parts, 2, tiles, block, LANES), F32),
            pltpu.VMEM((RG1 * block, 4 * LANES), BF16),
            pltpu.VMEM((RG1, 2, block, LANES), F32),
            pltpu.VMEM((RG1, 2, STEP, LANES), F32),
            pltpu.SemaphoreType.DMA((2, parts)),
        ],
        compiler_params=pltpu.CompilerParams(vmem_limit_bytes=VMEM_LIMIT),
        cost_estimate=pl.CostEstimate(
            flops=points * 8 * LANES * 6, bytes_accessed=16 * points, transcendentals=0
        ),
        name="compress",
    )(rank, *pieces, *consts)


def azimuth_kernel(chunk, x_ref, tw_ref, fwd_ref, fwd_low_ref, out_ref, up_ref, down_ref, t_ref, mid_ref):
    part = pl.program_id(0)
    pieces, per_part, bins = x_ref.shape[1], x_ref.shape[4], x_ref.shape[6]

    def stage(m):
        sides = []
        for ri in range(2):
            column = jnp.concatenate([x_ref[0, a, ri, 0, m] for a in range(pieces)], axis=0)
            sides.append(split(jnp.transpose(column)))
        high = jnp.concatenate([sides[0][0], sides[1][0]], axis=1)
        low = jnp.concatenate([sides[0][1], sides[1][1]], axis=1)
        y = dot(high, fwd_ref[...]) + dot(low, fwd_ref[...]) + dot(high, fwd_low_ref[...])
        index = part * per_part + m
        at = pl.ds(CHUNKS * index + chunk, 1)
        wr, wi = tw_ref[0, at, :], tw_ref[1, at, :]
        a, b = y[:, 0:LANES], y[:, LANES : 2 * LANES]
        t_ref[index, 0] = a * wr - b * wi
        t_ref[index, 1] = a * wi + b * wr

    for m in range(per_part):
        stage(m)

    @pl.when(part == pl.num_programs(0) - 1)
    def _():
        def rest(i, carry):
            at = pl.ds(pl.multiple_of(i * STEP, STEP), STEP)

            def load(m):
                return t_ref[m, 0, at, :], t_ref[m, 1, at, :]

            def finish(k, value):
                re, im = unit(chunk * k, LANES, -1.0)
                a, b = scale_by(value, float(re), float(im))
                out_ref[k, 0, at, :] = a
                out_ref[k, 1, at, :] = b

            dft_two_step(load, mid_ref, finish, 4, PER_CHUNK // 4, -1.0)
            return carry

        lax.fori_loop(0, bins // STEP, rest, 0)

        def edges(k, carry):
            for ri in range(2):
                up_ref[k, ri] = out_ref[k, ri, bins - HALO : bins, :]
                down_ref[k, ri] = out_ref[k, ri, 0:HALO, :]
            return carry

        lax.fori_loop(0, PER_CHUNK, edges, 0)


def azimuth(x, chunk, place):
    parts, pieces, _, _, per_part, rows_in, bins = x.shape
    ids = np.arange(LANES)
    tw = jnp.asarray(np.stack(unit(ids[:, None] * ids[None, :], NAZ, -1.0)), F32)
    fwd, fwd_low = right_tables(-1.0)
    consts = [tw, jnp.asarray(fwd), jnp.asarray(fwd_low)]
    points = PER_CHUNK * LANES * bins
    shape = (PER_CHUNK, 2, bins, LANES)
    edge = (PER_CHUNK, 2, HALO, LANES)
    return pl.pallas_call(
        functools.partial(azimuth_kernel, chunk),
        grid=(parts,),
        in_specs=[
            pl.BlockSpec(
                (1, pieces, 2, 1, per_part, rows_in, bins),
                lambda i: (i, 0, 0, place, 0, 0, 0),
            )
        ]
        + [whole_spec(a) for a in consts],
        out_specs=[pl.BlockSpec(s, lambda i: (0, 0, 0, 0)) for s in (shape, edge, edge)],
        out_shape=[jax.ShapeDtypeStruct(s, F32) for s in (shape, edge, edge)],
        scratch_shapes=[pltpu.VMEM(shape, F32), pltpu.VMEM((PER_CHUNK, 2, STEP, LANES), F32)],
        compiler_params=pltpu.CompilerParams(vmem_limit_bytes=VMEM_LIMIT),
        cost_estimate=pl.CostEstimate(
            flops=points * 8 * LANES * 3, bytes_accessed=16 * points, transcendentals=0
        ),
        name=f"azimuth{chunk}",
    )(x, *consts)


KB = 4
BB = 8
QUAD = 4


def fit(fn, even):
    nodes = np.cos((2 * np.arange(64) + 1) * np.pi / 128) * 0.25
    z2 = (nodes + 0.25) / 2
    z = np.sqrt(z2)
    goal = fn(np.pi * z) if even else fn(np.pi * z) / z
    return [float(v) for v in np.polynomial.polynomial.polyfit(z2, goal, 4)]


SIN_FIT, COS_FIT = fit(np.sin, False), fit(np.cos, True)


def horner(coefficients, x):
    total = coefficients[-1]
    for c in reversed(coefficients[:-1]):
        total = total * x + c
    return total


def turn(t):
    z = t - jnp.round(t)
    z2 = z * z
    s = horner(SIN_FIT, z2) * z
    c = horner(COS_FIT, z2)
    twice = s + s
    return 1.0 - twice * s, twice * c


def phase_kernel(part, sets, *refs):
    k = pl.program_id(0)
    for rate_ref, out_ref in zip(refs[:sets], refs[sets:]):
        for half in range(2):
            k2 = k + PER_CHUNK * (2 * part + half)
            f = k2 * LANES + lax.broadcasted_iota(jnp.int32, (1, LANES), 1)
            centred = jnp.where(f >= NAZ // 2, f - NAZ, f).astype(F32) * (1.0 / NAZ)
            c, s = turn(rate_ref[...] * (centred * centred))
            out_ref[half, 0, 0] = c
            out_ref[half, 0, 1] = s


def phase_tables(rates, part):
    shapes = [(2, PER_CHUNK, 2, rate.shape[0], LANES) for rate in rates]
    points = sum(2 * PER_CHUNK * rate.size for rate in rates)
    return pl.pallas_call(
        functools.partial(phase_kernel, part, len(rates)),
        grid=(PER_CHUNK,),
        in_specs=[whole_spec(rate) for rate in rates],
        out_specs=[
            pl.BlockSpec((2, 1) + shape[2:], lambda i: (0, i, 0, 0, 0)) for shape in shapes
        ],
        out_shape=[jax.ShapeDtypeStruct(shape, F32) for shape in shapes],
        compiler_params=pltpu.CompilerParams(vmem_limit_bytes=VMEM_LIMIT),
        cost_estimate=pl.CostEstimate(
            flops=40 * points, bytes_accessed=8 * points, transcendentals=0
        ),
        name="phase",
    )(*rates)


def combine(sources, kk, start, put):
    at = slice(start, start + STEP)
    values = [(ref[kk, 0, at, :], ref[kk, 1, at, :]) for ref in sources]
    for q, value in enumerate(dft_list(values, -1.0)):
        for half, part in enumerate(value):
            high, low = split(part)
            put(q, slice(half * LANES, (half + 1) * LANES), high, low)


def final_kernel(steps, joins, wide, *refs):
    refs = list(refs)

    def take(count):
        taken = refs[:count]
        del refs[:count]
        return taken

    sources = take(CHUNKS) if joins else take(1)
    low_refs, high_refs = (take(CHUNKS), take(CHUNKS)) if wide else ((), ())
    phase_refs = take(CHUNKS // 2)
    mover_refs = take(2 if wide else 1)
    inv1_ref, inv2_ref, tw_ref = take(3)
    out_ref, own_ref, zr_ref, zi_ref, s_ref, swap_ref, half_ref = (
        refs[-8:-1] if wide else refs[-7:]
    )
    halo_ref = refs[-1]
    if not joins:
        own_ref = sources[0]
    own = own_ref.shape[2] // 2
    rows = phase_refs[0].shape[3]
    step = pl.program_id(0)

    def first_half(block):
        base = jnp.minimum(block * BB, rows - BB)
        for j in range(BB // QUAD):
            cols = []
            for t in range(QUAD):
                at = base + QUAD * j + t
                cols.append(jnp.concatenate([zr_ref[at], zi_ref[at]], axis=0))
            hi, lo = split(jnp.concatenate(cols, axis=1))
            w = dot(inv1_ref[...], jnp.concatenate([hi, lo, hi], axis=0))
            turned = []
            for t in range(QUAD):
                a = w[0:LANES, t * LANES : (t + 1) * LANES]
                b = w[LANES : 2 * LANES, t * LANES : (t + 1) * LANES]
                wr, wi = tw_ref[0], tw_ref[1]
                turned.append(jnp.concatenate([a * wr - b * wi, a * wi + b * wr], axis=1))
            hi, lo = split(jnp.concatenate(turned, axis=0))
            half_ref[j] = jnp.concatenate([hi, lo, hi], axis=1)

    @pl.when(step < steps)
    def _():
        def one(kk, buf):
            k = step * KB + kk
            if joins:
                for start in range(0, own, STEP):

                    def put_own(q, cols, high, low, start=start):
                        own_ref[q, kk, start : start + STEP, cols] = high
                        own_ref[q, kk, own + start : own + start + STEP, cols] = low

                    combine(sources, kk, start, put_own)
            if wide:
                for side, halo_refs in enumerate((low_refs, high_refs)):
                    for start in range(0, HALO, STEP):

                        def put_halo(q, cols, high, low, at=side * HALO + start):
                            halo_ref[buf, q, at : at + STEP, cols] = high
                            halo_ref[buf, q, 2 * HALO + at : 2 * HALO + at + STEP, cols] = low

                        combine(halo_refs, kk, start, put_halo)
            for q in range(CHUNKS):
                k2 = k + PER_CHUNK * q
                band = lax.div(k2, LANES // GROUPS)
                moved = dot(mover_refs[0][band], own_ref[q, kk])
                if wide:
                    moved = moved + dot(mover_refs[1][band], halo_ref[buf, q])
                both = moved[0:rows, :] + moved[rows : 2 * rows, :]
                c, s = phase_refs[q // 2][q % 2, kk, 0], phase_refs[q // 2][q % 2, kk, 1]
                a, b = both[:, 0:LANES], both[:, LANES : 2 * LANES]
                swap_ref[buf, 0, q] = a * c + b * s
                swap_ref[buf, 1, q] = b * c - a * s
            to = pl.ds(pl.multiple_of(k * CHUNKS, CHUNKS), CHUNKS)
            for start in range(0, rows, BB):
                at = slice(start, start + BB)
                zr_ref[at, to, :] = jnp.swapaxes(swap_ref[buf, 0, :, at, :], 0, 1)
                zi_ref[at, to, :] = jnp.swapaxes(swap_ref[buf, 1, :, at, :], 0, 1)

        for kk in range(KB):
            one(kk, kk % 2)

    @pl.when(step > steps)
    def _():
        for j in range(BB // QUAD):
            image = lax.dot_general(
                inv2_ref[...], half_ref[j], (((1,), (1,)), ((), ())), preferred_element_type=F32
            )
            for t in range(QUAD):
                for ri in range(2):
                    s_ref[ri, QUAD * j + t] = image[
                        ri * LANES : (ri + 1) * LANES, t * LANES : (t + 1) * LANES
                    ]
        first_half(step - steps)
        for ri in range(2):
            for start in range(0, LANES, 8):
                lines = jnp.swapaxes(s_ref[ri, :, start : start + 8, :], 0, 1)
                for n in range(8):
                    at = (start + n) * LANES
                    out_ref[ri, :, at : at + LANES] = lines[n]

    @pl.when(step == steps)
    def _():
        first_half(0)


def final(bins, places, sources, lows, highs, phases, movers, image=None):
    joins, wide = len(sources) > 1, len(lows) > 0
    rows = len(places) * BB
    steps = PER_CHUNK // KB
    ids = np.arange(LANES)
    tw = jnp.asarray(np.stack(unit(ids[:, None] * ids[None, :], NAZ, 1.0)), F32)
    consts = [
        *movers,
        jnp.asarray(left_table(1.0, 1.0, ids // CHUNKS + PER_CHUNK * (ids % CHUNKS))),
        jnp.asarray(left_table(1.0, 1.0 / NAZ)),
        tw,
    ]
    start, gap_at = places[0], len(places)
    for i, place in enumerate(places):
        if place != start + i:
            gap_at = i
            break
    gap = places[-1] - start - len(places) + 1

    def early(i):
        return (jnp.minimum(i, steps - 1), 0, 0, 0)

    def early_second(i):
        return (0, jnp.minimum(i, steps - 1), 0, 0)

    def late(i):
        at = jnp.maximum(i - steps - 1, 0)
        return (0, start + at + jnp.where(at >= gap_at, gap, 0), 0)

    joined = (CHUNKS, PER_CHUNK, 2 * bins, 2 * LANES)
    joined_spec = pl.BlockSpec((CHUNKS, KB, 2 * bins, 2 * LANES), early_second)
    given = [*sources, *lows, *highs, *phases, *consts]
    specs = [pl.BlockSpec((KB, 2, bins, LANES), early)] * CHUNKS if joins else [joined_spec]
    specs += [pl.BlockSpec((KB, 2, HALO, LANES), early)] * (2 * CHUNKS if wide else 0)
    specs += [
        pl.BlockSpec((2, KB, 2, rows, LANES), lambda i: (0, jnp.minimum(i, steps - 1), 0, 0, 0))
    ] * len(phases)
    specs += [whole_spec(a) for a in consts]
    aliases = {}
    if image is not None:
        aliases = {len(given): 0}
        given.append(image)
        specs.append(pl.BlockSpec(memory_space=pl.ANY))
    shapes = [jax.ShapeDtypeStruct((2, bins, NAZ), F32)]
    out_specs = [pl.BlockSpec((2, BB, NAZ), late)]
    scratch = []
    if joins and wide:
        scratch.append(pltpu.VMEM((CHUNKS, KB, 2 * bins, 2 * LANES), BF16))
    elif joins:
        shapes.append(jax.ShapeDtypeStruct(joined, BF16))
        out_specs.append(joined_spec)
    else:
        scratch.append(pltpu.VMEM((16, LANES), BF16))
    scratch += [
        pltpu.VMEM((rows, LANES, LANES), F32),
        pltpu.VMEM((rows, LANES, LANES), F32),
        pltpu.VMEM((2, BB, LANES, LANES), F32),
        pltpu.VMEM((2, 2, CHUNKS, rows, LANES), F32),
        pltpu.VMEM((BB // QUAD, QUAD * LANES, 6 * LANES), BF16),
    ]
    if wide:
        scratch.append(pltpu.VMEM((2, CHUNKS, 4 * HALO, 2 * LANES), BF16))
    points = NAZ * rows
    return pl.pallas_call(
        functools.partial(final_kernel, steps, joins, wide),
        grid=(steps + 1 + len(places),),
        in_specs=specs,
        out_specs=out_specs,
        out_shape=shapes,
        scratch_shapes=scratch,
        input_output_aliases=aliases,
        compiler_params=pltpu.CompilerParams(vmem_limit_bytes=VMEM_LIMIT),
        cost_estimate=pl.CostEstimate(
            flops=points * 8 * LANES * 9, bytes_accessed=28 * points, transcendentals=0
        ),
        name="final_wide" if wide else "final_inner",
    )(*given)


def mover_table(rows, columns, shift_table, filter_index, tap_table):
    shift_table, filter_index = shift_table[:, rows], filter_index[:, rows]
    onehot = (filter_index[:, :, None] == jnp.arange(NFILT, dtype=jnp.int32)).astype(F32)
    weights = jnp.einsum("gbf,ft->gbt", onehot, tap_table, precision=lax.Precision.HIGHEST)
    first = rows[None, :].astype(np.int32) + shift_table + (HALO - 4)
    offset = columns.astype(np.int32)[None, None, :] - first[:, :, None]
    table = jnp.zeros(offset.shape, F32)
    for t in range(TAPS):
        table = table + jnp.where(offset == t, weights[:, :, t : t + 1], 0.0)
    high = lax.reduce_precision(table, 8, 7)
    low = table - high
    top = jnp.concatenate([high, high], axis=2)
    bottom = jnp.concatenate([low, jnp.zeros_like(low)], axis=2)
    return jnp.concatenate([top, bottom], axis=1).astype(BF16)


def own_columns(bins):
    return np.arange(HALO, HALO + bins)


def halo_columns(bins):
    return np.concatenate([np.arange(HALO), np.arange(bins + HALO, bins + 2 * HALO)])


def row_sets(bins):
    blocks = np.arange(bins // BB)
    inner = (blocks >= HALO // BB) & (blocks < (bins - HALO) // BB)
    return [blocks[chosen].tolist() for chosen in (inner, ~inner) if chosen.any()]


def bins_of(places):
    return np.concatenate([np.arange(BB) + BB * place for place in places])


def neighbours(axes, size, step):
    return [(i, i + step) for i in range(size) if 0 <= i + step < size]


def local(nrng, naz, raw_echo, chirp_spectrum, azimuth_rate, shift_table, filter_index, tap_table):
    axes = ("rng", "az")
    devices = nrng * naz
    bins = NRG // devices
    rows_in = raw_echo.shape[1] // LANES
    per_part = PER_CHUNK // nrng
    chirp = chirp_spectrum.reshape(2, LANES, RG1).transpose(0, 2, 1)
    rate = jnp.broadcast_to((azimuth_rate * 0.5)[:, None], (bins, LANES))
    rank = lax.axis_index("rng").astype(jnp.int32).reshape(1)
    packed = pack(raw_echo, rank, nrng, GROUPED[:1]) + pack(raw_echo, rank, nrng, GROUPED[1:])
    mains, lows, highs = [None] * CHUNKS, [None] * CHUNKS, [None] * CHUNKS
    turned = []

    def gather(g):
        return [packed[g][0]] + [
            lax.ppermute(packed[g][j], "rng", [(i, i ^ j) for i in range(nrng)])
            for j in range(1, nrng)
        ]

    def transform(g):
        for place, c in enumerate(GROUPED[g]):
            if c > 0:
                turned[g], mains[c - 1] = lax.optimization_barrier((turned[g], mains[c - 1]))
            main, up, down = azimuth(turned[g], c, place)
            mains[c] = main
            lows[c] = lax.ppermute(up, axes, neighbours(axes, devices, 1))
            highs[c] = lax.ppermute(down, axes, neighbours(axes, devices, -1))

    places = row_sets(bins)
    rates = [rate[bins_of(p)] for p in places]
    phases = []
    got = [gather(0)]
    packed[1], got[0] = lax.optimization_barrier((packed[1], got[0]))
    got.append(gather(1))
    count = len(GROUPED)
    for g, chunks in enumerate(GROUPED):
        lines = compress(got[g], rank, chirp)
        if g + 1 < count:
            lines, got[g + 1] = lax.optimization_barrier((lines, got[g + 1]))
        if g + 2 < count:
            packed[g + 2], got[g + 1] = lax.optimization_barrier((packed[g + 2], got[g + 1]))
            if g >= 1:
                held = (packed[g + 2], turned[g - 1])
                packed[g + 2], turned[g - 1] = lax.optimization_barrier(held)
            got.append(gather(g + 2))
        if g >= 2:
            transform(g - 2)
            for c in GROUPED[g - 2]:
                lines, mains[c] = lax.optimization_barrier((lines, mains[c]))
        if g >= 3:
            for c in GROUPED[g - 3]:
                held = (lines, lows[c], highs[c])
                lines, lows[c], highs[c] = lax.optimization_barrier(held)
            for _ in range(2 if len(phases) < CHUNKS // 2 else 0):
                rates, turned[g - 2] = lax.optimization_barrier((rates, turned[g - 2]))
                table = phase_tables(rates, len(phases))
                lines, table = lax.optimization_barrier((lines, table))
                phases.append(table)
        if bins < LANES:
            cut = lines.reshape(RG1, 2, -1, LANES // bins, bins)
            lines = cut.transpose(0, 3, 1, 2, 4).reshape(devices, 2, -1, bins)
        moved = lax.all_to_all(lines, axes, split_axis=0, concat_axis=0, tiled=True)
        turned.append(moved.reshape(nrng, naz, 2, len(chunks), per_part, rows_in, bins))
    transform(count - 2)
    transform(count - 1)
    tables = (shift_table, filter_index, tap_table)
    image, sources = None, mains
    for i, places_of in enumerate(places):
        ids = bins_of(places_of)
        wide = i == len(places) - 1
        halos = (lows, highs) if wide else ([], [])
        columns = [own_columns(bins), halo_columns(bins)] if wide else [own_columns(bins)]
        movers = [mover_table(ids, cols, *tables) for cols in columns]
        result = final(
            bins, places_of, sources, *halos, [table[i] for table in phases], movers, image
        )
        image, sources = result[0], result[1:]
    return image


def solution(mesh):
    return jax.shard_map(
        functools.partial(local, mesh.shape["rng"], mesh.shape["az"]),
        mesh=mesh,
        in_specs=(
            P(None, "az", "rng"),
            P(),
            P(("rng", "az")),
            P(None, ("rng", "az")),
            P(None, ("rng", "az")),
            P(),
        ),
        out_specs=P(None, ("rng", "az"), None),
        check_vma=False,
    )
```

```python
import functools

import jax
import jax.numpy as jnp
import ml_dtypes
import numpy as np
from jax import lax
from jax.experimental import pallas as pl
from jax.experimental.pallas import tpu as pltpu
from jax.sharding import PartitionSpec as P

NRG = 4096
NAZ = 16384
GROUPS = 16
NFILT = 16
TAPS = 8
HALO = 32
LANES = 128
RG1 = NRG // LANES
CHUNKS = 8
PER_CHUNK = LANES // CHUNKS
GROUPED = tuple((c,) for c in range(CHUNKS))
VMEM_LIMIT = 60 << 20
BF16 = jnp.bfloat16
F32 = jnp.float32


def split_np(table):
    table = np.asarray(table, np.float32)
    high = table.astype(ml_dtypes.bfloat16)
    low = (table - high.astype(np.float32)).astype(ml_dtypes.bfloat16)
    return high, low


def unit(angle_num, period, sign):
    angles = (np.asarray(angle_num, np.int64) % period) * (2.0 * np.pi / period)
    return np.cos(angles), sign * np.sin(angles)


def dft_matrix(sign):
    ids = np.arange(LANES)
    return unit(ids[:, None] * ids[None, :], LANES, sign)


def right_tables(sign, scale=1.0):
    c, s = dft_matrix(sign)
    return split_np(np.block([[c, s], [-s, c]]) * scale)


def left_table(sign, scale=1.0, order=np.arange(LANES)):
    c, s = (part[:, order] for part in dft_matrix(sign))
    high, low = split_np(np.block([[c, -s], [s, c]]) * scale)
    return np.concatenate([high, high, low], axis=1)


def split(x):
    high = x.astype(BF16)
    low = (x - high.astype(F32)).astype(BF16)
    return high, low


def dot(a, b):
    return jnp.dot(a, b, preferred_element_type=F32)


def scale_by(value, re, im):
    a, b = value
    eps = 1e-12
    if abs(im) < eps:
        if abs(re - 1.0) < eps:
            return value
        if abs(re + 1.0) < eps:
            return -a, -b
    if abs(re) < eps:
        if abs(im - 1.0) < eps:
            return -b, a
        if abs(im + 1.0) < eps:
            return b, -a
    if abs(abs(re) - abs(im)) < eps:
        sr, si = (1.0 if re > 0 else -1.0), (1.0 if im > 0 else -1.0)
        h = abs(re)
        total, diff = (a + b) * h, (a - b) * h
        if si == sr:
            return (diff, total) if sr > 0 else (-diff, -total)
        return (total, -diff) if sr > 0 else (-total, diff)
    re, im = float(re), float(im)
    return a * re - b * im, a * im + b * re


def dft_list(values, sign):
    count = len(values)
    if count == 1:
        return values
    even, odd = dft_list(values[0::2], sign), dft_list(values[1::2], sign)
    first, second = [], []
    for k in range(count // 2):
        re, im = unit(k, count, sign)
        a, b = even[k], scale_by(odd[k], float(re), float(im))
        first.append((a[0] + b[0], a[1] + b[1]))
        second.append((a[0] - b[0], a[1] - b[1]))
    return first + second


def dft_two_step(load, mid_ref, finish, outer, inner, sign):
    for ib in range(inner):
        column = dft_list([load(ia * inner + ib) for ia in range(outer)], sign)
        for ka in range(outer):
            re, im = unit(ib * ka, outer * inner, sign)
            a, b = scale_by(column[ka], float(re), float(im))
            mid_ref[ka * inner + ib, 0] = a
            mid_ref[ka * inner + ib, 1] = b
    for ka in range(outer):
        row = [(mid_ref[ka * inner + ib, 0], mid_ref[ka * inner + ib, 1]) for ib in range(inner)]
        for kb, value in enumerate(dft_list(row, sign)):
            finish(ka + outer * kb, value)


def pack_kernel(groups, parts, per_part, rows_in, rank_ref, x_ref, *out_refs):
    rank = rank_ref[0]
    for j in range(parts):
        part = jnp.bitwise_xor(rank, j)
        for g, chunks in enumerate(groups):
            for at, c in enumerate(chunks):
                for m in range(per_part):
                    start = CHUNKS * (part * per_part + m) + c
                    to = (at * per_part + m) * rows_in
                    for ri in range(2):
                        out_refs[g * parts + j][ri, 0, to : to + rows_in, :] = x_ref[
                            ri, pl.ds(start, rows_in, stride=LANES), :
                        ]


def pack(raw, rank, parts, groups):
    lines, bins = raw.shape[1], raw.shape[2]
    rows_in, tiles, per_part = lines // LANES, bins // LANES, PER_CHUNK // parts
    heights = [len(chunks) * per_part * rows_in for chunks in groups for _ in range(parts)]
    flat = pl.pallas_call(
        functools.partial(pack_kernel, groups, parts, per_part, rows_in),
        grid=(tiles,),
        in_specs=[
            pl.BlockSpec(memory_space=pltpu.SMEM),
            pl.BlockSpec((2, lines, LANES), lambda i: (0, 0, i)),
        ],
        out_specs=[pl.BlockSpec((2, 1, rows, LANES), lambda i: (0, i, 0, 0)) for rows in heights],
        out_shape=[jax.ShapeDtypeStruct((2, tiles, rows, LANES), F32) for rows in heights],
        compiler_params=pltpu.CompilerParams(vmem_limit_bytes=VMEM_LIMIT),
        cost_estimate=pl.CostEstimate(flops=0, bytes_accessed=16 * lines * bins, transcendentals=0),
        name="pack",
    )(rank, raw)
    return [flat[i * parts : (i + 1) * parts] for i in range(len(groups))]


STEP = 16


def compress_kernel(parts, rows, rank_ref, *refs):
    x_refs = refs[:parts]
    chirp_ref, tw_ref, fwd_ref, fwd_low_ref, inv_ref, inv_low_ref = refs[parts : parts + 6]
    out_ref, buf_ref, lhs_ref, y_ref, mid_ref, sems = refs[parts + 6 :]
    tiles = buf_ref.shape[3]
    rank = rank_ref[0]
    step = pl.program_id(0)
    slot = lax.rem(step, 2)

    def copies(at, to):
        return [
            pltpu.make_async_copy(
                x_refs[j].at[:, :, pl.ds(pl.multiple_of(at * rows, rows), rows), :],
                buf_ref.at[to, jnp.bitwise_xor(rank, j)],
                sems.at[to, j],
            )
            for j in range(parts)
        ]

    @pl.when(step == 0)
    def _():
        for copy in copies(step, slot):
            copy.start()

    @pl.when(step + 1 < pl.num_programs(0))
    def _():
        for copy in copies(step + 1, 1 - slot):
            copy.start()

    for copy in copies(step, slot):
        copy.wait()

    def put(at, re, im):
        for half, part in enumerate((re, im)):
            high, low = split(part)
            lhs_ref[at, half * LANES : (half + 1) * LANES] = high
            lhs_ref[at, (2 + half) * LANES : (3 + half) * LANES] = low

    def forward(i, carry):
        at = pl.ds(pl.multiple_of(i * STEP, STEP), STEP)

        def load(p):
            source = buf_ref.at[slot, p // tiles]
            return source[0, p % tiles, at, :], source[1, p % tiles, at, :]

        def finish(k, value):
            wr, wi = tw_ref[0, k : k + 1, :], tw_ref[1, k : k + 1, :]
            a, b = value
            put(
                pl.ds(pl.multiple_of(k * rows + i * STEP, STEP), STEP),
                a * wr - b * wi,
                a * wi + b * wr,
            )

        dft_two_step(load, mid_ref, finish, 4, RG1 // 4, -1.0)
        return carry

    lax.fori_loop(0, rows // STEP, forward, 0)

    group = max(1, 2 * LANES // rows)

    def middle(i, carry):
        at = pl.ds(pl.multiple_of(i * group * rows, group * rows), group * rows)
        y = dot(lhs_ref[at, :], fwd_ref[...]) + dot(lhs_ref[at, 0 : 2 * LANES], fwd_low_ref[...])
        for s in range(group):
            k = i * group + s
            cr, ci = chirp_ref[0, pl.ds(k, 1), :], chirp_ref[1, pl.ds(k, 1), :]
            a = y[s * rows : (s + 1) * rows, 0:LANES]
            b = y[s * rows : (s + 1) * rows, LANES : 2 * LANES]
            put(pl.ds(pl.multiple_of(k * rows, rows), rows), a * cr - b * ci, a * ci + b * cr)
        z = dot(lhs_ref[at, :], inv_ref[...]) + dot(lhs_ref[at, 0 : 2 * LANES], inv_low_ref[...])
        for s in range(group):
            k = i * group + s
            wr, wi = tw_ref[0, pl.ds(k, 1), :], tw_ref[1, pl.ds(k, 1), :]
            a = z[s * rows : (s + 1) * rows, 0:LANES]
            b = z[s * rows : (s + 1) * rows, LANES : 2 * LANES]
            y_ref[k, 0] = a * wr + b * wi
            y_ref[k, 1] = b * wr - a * wi
        return carry

    lax.fori_loop(0, RG1 // group, middle, 0)

    def backward(i, carry):
        at = pl.ds(pl.multiple_of(i * STEP, STEP), STEP)

        def load(k):
            return y_ref[k, 0, at, :], y_ref[k, 1, at, :]

        def finish(p, value):
            out_ref[p, 0, at, :] = value[0]
            out_ref[p, 1, at, :] = value[1]

        dft_two_step(load, mid_ref, finish, 4, RG1 // 4, 1.0)
        return carry

    lax.fori_loop(0, rows // STEP, backward, 0)


def whole_spec(array):
    zeros = (0,) * array.ndim
    return pl.BlockSpec(array.shape, lambda *_: zeros)


def compress(pieces, rank, chirp):
    parts = len(pieces)
    _, tiles, rows, _ = pieces[0].shape
    block = min(rows, 64)
    ids = np.arange(RG1)[:, None] * np.arange(LANES)[None, :]
    tw = jnp.asarray(np.stack(unit(ids, NRG, -1.0)), F32)
    fwd, fwd_low = right_tables(-1.0)
    inv, inv_low = right_tables(1.0, 1.0 / NRG)
    consts = [
        chirp,
        tw,
        jnp.asarray(np.concatenate([fwd, fwd])),
        jnp.asarray(fwd_low),
        jnp.asarray(np.concatenate([inv, inv])),
        jnp.asarray(inv_low),
    ]
    points = rows * NRG
    return pl.pallas_call(
        functools.partial(compress_kernel, parts, block),
        grid=(rows // block,),
        in_specs=[pl.BlockSpec(memory_space=pltpu.SMEM)]
        + [pl.BlockSpec(memory_space=pl.ANY)] * parts
        + [whole_spec(a) for a in consts],
        out_specs=pl.BlockSpec((RG1, 2, block, LANES), lambda i: (0, 0, i, 0)),
        out_shape=jax.ShapeDtypeStruct((RG1, 2, rows, LANES), F32),
        scratch_shapes=[
            pltpu.VMEM((2, parts, 2, tiles, block, LANES), F32),
            pltpu.VMEM((RG1 * block, 4 * LANES), BF16),
            pltpu.VMEM((RG1, 2, block, LANES), F32),
            pltpu.VMEM((RG1, 2, STEP, LANES), F32),
            pltpu.SemaphoreType.DMA((2, parts)),
        ],
        compiler_params=pltpu.CompilerParams(vmem_limit_bytes=VMEM_LIMIT),
        cost_estimate=pl.CostEstimate(
            flops=points * 8 * LANES * 6, bytes_accessed=16 * points, transcendentals=0
        ),
        name="compress",
    )(rank, *pieces, *consts)


def azimuth_kernel(chunk, x_ref, tw_ref, fwd_ref, fwd_low_ref, out_ref, up_ref, down_ref, t_ref, mid_ref):
    part = pl.program_id(0)
    pieces, per_part, bins = x_ref.shape[1], x_ref.shape[4], x_ref.shape[6]

    def stage(m):
        sides = []
        for ri in range(2):
            column = jnp.concatenate([x_ref[0, a, ri, 0, m] for a in range(pieces)], axis=0)
            sides.append(split(jnp.transpose(column)))
        high = jnp.concatenate([sides[0][0], sides[1][0]], axis=1)
        low = jnp.concatenate([sides[0][1], sides[1][1]], axis=1)
        y = dot(high, fwd_ref[...]) + dot(low, fwd_ref[...]) + dot(high, fwd_low_ref[...])
        index = part * per_part + m
        at = pl.ds(CHUNKS * index + chunk, 1)
        wr, wi = tw_ref[0, at, :], tw_ref[1, at, :]
        a, b = y[:, 0:LANES], y[:, LANES : 2 * LANES]
        t_ref[index, 0] = a * wr - b * wi
        t_ref[index, 1] = a * wi + b * wr

    for m in range(per_part):
        stage(m)

    @pl.when(part == pl.num_programs(0) - 1)
    def _():
        def rest(i, carry):
            at = pl.ds(pl.multiple_of(i * STEP, STEP), STEP)

            def load(m):
                return t_ref[m, 0, at, :], t_ref[m, 1, at, :]

            def finish(k, value):
                re, im = unit(chunk * k, LANES, -1.0)
                a, b = scale_by(value, float(re), float(im))
                out_ref[k, 0, at, :] = a
                out_ref[k, 1, at, :] = b

            dft_two_step(load, mid_ref, finish, 4, PER_CHUNK // 4, -1.0)
            return carry

        lax.fori_loop(0, bins // STEP, rest, 0)

        def edges(k, carry):
            for ri in range(2):
                up_ref[k, ri] = out_ref[k, ri, bins - HALO : bins, :]
                down_ref[k, ri] = out_ref[k, ri, 0:HALO, :]
            return carry

        lax.fori_loop(0, PER_CHUNK, edges, 0)


def azimuth(x, chunk, place):
    parts, pieces, _, _, per_part, rows_in, bins = x.shape
    ids = np.arange(LANES)
    tw = jnp.asarray(np.stack(unit(ids[:, None] * ids[None, :], NAZ, -1.0)), F32)
    fwd, fwd_low = right_tables(-1.0)
    consts = [tw, jnp.asarray(fwd), jnp.asarray(fwd_low)]
    points = PER_CHUNK * LANES * bins
    shape = (PER_CHUNK, 2, bins, LANES)
    edge = (PER_CHUNK, 2, HALO, LANES)
    return pl.pallas_call(
        functools.partial(azimuth_kernel, chunk),
        grid=(parts,),
        in_specs=[
            pl.BlockSpec(
                (1, pieces, 2, 1, per_part, rows_in, bins),
                lambda i: (i, 0, 0, place, 0, 0, 0),
            )
        ]
        + [whole_spec(a) for a in consts],
        out_specs=[pl.BlockSpec(s, lambda i: (0, 0, 0, 0)) for s in (shape, edge, edge)],
        out_shape=[jax.ShapeDtypeStruct(s, F32) for s in (shape, edge, edge)],
        scratch_shapes=[pltpu.VMEM(shape, F32), pltpu.VMEM((PER_CHUNK, 2, STEP, LANES), F32)],
        compiler_params=pltpu.CompilerParams(vmem_limit_bytes=VMEM_LIMIT),
        cost_estimate=pl.CostEstimate(
            flops=points * 8 * LANES * 3, bytes_accessed=16 * points, transcendentals=0
        ),
        name=f"azimuth{chunk}",
    )(x, *consts)


KB = 4
BB = 8
QUAD = 4


def fit(fn, even):
    nodes = np.cos((2 * np.arange(64) + 1) * np.pi / 128) * 0.25
    z2 = (nodes + 0.25) / 2
    z = np.sqrt(z2)
    goal = fn(np.pi * z) if even else fn(np.pi * z) / z
    return [float(v) for v in np.polynomial.polynomial.polyfit(z2, goal, 4)]


SIN_FIT, COS_FIT = fit(np.sin, False), fit(np.cos, True)


def horner(coefficients, x):
    total = coefficients[-1]
    for c in reversed(coefficients[:-1]):
        total = total * x + c
    return total


def square_of(k2):
    f = k2 * LANES + lax.broadcasted_iota(jnp.int32, (1, LANES), 1)
    centred = jnp.where(f >= NAZ // 2, f - NAZ, f).astype(F32) * (1.0 / NAZ)
    return centred * centred


def turn(t):
    z = t - jnp.round(t)
    z2 = z * z
    s = horner(SIN_FIT, z2) * z
    c = horner(COS_FIT, z2)
    twice = s + s
    return 1.0 - twice * s, twice * c


def phase_kernel(part, rate_ref, out_ref):
    k = pl.program_id(0)
    for half in range(2):
        c, s = turn(rate_ref[...] * square_of(k + PER_CHUNK * (2 * part + half)))
        out_ref[half, 0, 0] = c
        out_ref[half, 0, 1] = s


def phase_table(rate, part):
    shape = (2, PER_CHUNK, 2, rate.shape[0], LANES)
    points = 2 * PER_CHUNK * rate.size
    return pl.pallas_call(
        functools.partial(phase_kernel, part),
        grid=(PER_CHUNK,),
        in_specs=[whole_spec(rate)],
        out_specs=pl.BlockSpec((2, 1) + shape[2:], lambda i: (0, i, 0, 0, 0)),
        out_shape=jax.ShapeDtypeStruct(shape, F32),
        compiler_params=pltpu.CompilerParams(vmem_limit_bytes=VMEM_LIMIT),
        cost_estimate=pl.CostEstimate(
            flops=40 * points, bytes_accessed=8 * points, transcendentals=0
        ),
        name="phase",
    )(rate)


def combine(sources, kk, start, put):
    at = slice(start, start + STEP)
    values = [(ref[kk, 0, at, :], ref[kk, 1, at, :]) for ref in sources]
    for q, value in enumerate(dft_list(values, -1.0)):
        for half, part in enumerate(value):
            high, low = split(part)
            put(q, slice(half * LANES, (half + 1) * LANES), high, low)


def final_kernel(steps, joins, wide, *refs):
    refs = list(refs)

    def take(count):
        taken = refs[:count]
        del refs[:count]
        return taken

    sources = take(CHUNKS) if joins else take(1)
    low_refs, high_refs = (take(CHUNKS), take(CHUNKS)) if wide else ((), ())
    phase_refs = take(1 if wide else CHUNKS // 2)
    mover_refs = take(2 if wide else 1)
    inv1_ref, inv2_ref, tw_ref = take(3)
    if not joins or wide:
        out_ref, own_ref, zr_ref, zi_ref, s_ref, swap_ref, half_ref, halo_ref = refs[-8:]
        if not joins:
            own_ref = sources[0]
    else:
        out_ref, joined_ref, own_ref, zr_ref, zi_ref, s_ref, swap_ref, half_ref, sems = refs[-9:]
    step = pl.program_id(0)
    own = own_ref.shape[2] // 2
    rows = zr_ref.shape[0]
    keeps = joins and not wide
    copies = []
    if keeps:
        copies = [
            pltpu.make_async_copy(own_ref.at[q], joined_ref.at[q], sems.at[q])
            for q in range(CHUNKS)
        ]

    def own_at(kk):
        return step * KB + kk if keeps else kk

    def first_half(block):
        base = jnp.minimum(block * BB, rows - BB)
        for j in range(BB // QUAD):
            cols = []
            for t in range(QUAD):
                at = base + QUAD * j + t
                cols.append(jnp.concatenate([zr_ref[at], zi_ref[at]], axis=0))
            hi, lo = split(jnp.concatenate(cols, axis=1))
            w = dot(inv1_ref[...], jnp.concatenate([hi, lo, hi], axis=0))
            turned = []
            for t in range(QUAD):
                a = w[0:LANES, t * LANES : (t + 1) * LANES]
                b = w[LANES : 2 * LANES, t * LANES : (t + 1) * LANES]
                wr, wi = tw_ref[0], tw_ref[1]
                turned.append(jnp.concatenate([a * wr - b * wi, a * wi + b * wr], axis=1))
            hi, lo = split(jnp.concatenate(turned, axis=0))
            half_ref[j] = jnp.concatenate([hi, lo, hi], axis=1)

    @pl.when(step < steps)
    def _():
        def one(kk, buf):
            k = step * KB + kk
            if joins:
                for start in range(0, own, STEP):

                    def put_own(q, cols, high, low, start=start):
                        own_ref[q, own_at(kk), start : start + STEP, cols] = high
                        own_ref[q, own_at(kk), own + start : own + start + STEP, cols] = low

                    combine(sources, kk, start, put_own)
            if wide:
                for side, halo_refs in enumerate((low_refs, high_refs)):
                    for start in range(0, HALO, STEP):

                        def put_halo(q, cols, high, low, at=side * HALO + start):
                            halo_ref[buf, q, at : at + STEP, cols] = high
                            halo_ref[buf, q, 2 * HALO + at : 2 * HALO + at + STEP, cols] = low

                        combine(halo_refs, kk, start, put_halo)
            for q in range(CHUNKS):
                k2 = k + PER_CHUNK * q
                band = lax.div(k2, LANES // GROUPS)
                moved = dot(mover_refs[0][band], own_ref[q, own_at(kk)])
                if wide:
                    moved = moved + dot(mover_refs[1][band], halo_ref[buf, q])
                both = moved[0:rows, :] + moved[rows : 2 * rows, :]
                if wide:
                    c, s = turn(phase_refs[0][...] * square_of(k2))
                else:
                    c, s = phase_refs[q // 2][q % 2, kk, 0], phase_refs[q // 2][q % 2, kk, 1]
                a, b = both[:, 0:LANES], both[:, LANES : 2 * LANES]
                swap_ref[buf, 0, q] = a * c + b * s
                swap_ref[buf, 1, q] = b * c - a * s
            to = pl.ds(pl.multiple_of(k * CHUNKS, CHUNKS), CHUNKS)
            for start in range(0, rows, BB):
                at = slice(start, start + BB)
                zr_ref[at, to, :] = jnp.swapaxes(swap_ref[buf, 0, :, at, :], 0, 1)
                zi_ref[at, to, :] = jnp.swapaxes(swap_ref[buf, 1, :, at, :], 0, 1)

        for kk in range(KB):
            one(kk, kk % 2)

    @pl.when(step > steps)
    def _():
        for j in range(BB // QUAD):
            image = lax.dot_general(
                inv2_ref[...], half_ref[j], (((1,), (1,)), ((), ())), preferred_element_type=F32
            )
            for t in range(QUAD):
                for ri in range(2):
                    s_ref[ri, QUAD * j + t] = image[
                        ri * LANES : (ri + 1) * LANES, t * LANES : (t + 1) * LANES
                    ]
        first_half(step - steps)
        for ri in range(2):
            for start in range(0, LANES, 8):
                lines = jnp.swapaxes(s_ref[ri, :, start : start + 8, :], 0, 1)
                for n in range(8):
                    at = (start + n) * LANES
                    out_ref[ri, :, at : at + LANES] = lines[n]

    @pl.when(step == steps)
    def _():
        for copy in copies:
            copy.start()
        first_half(0)

    @pl.when(step == pl.num_programs(0) - 1)
    def _():
        for copy in copies:
            copy.wait()


def final(bins, places, sources, lows, highs, phases, movers, image=None):
    joins, wide = len(sources) > 1, len(lows) > 0
    rows = len(places) * BB
    steps = PER_CHUNK // KB
    ids = np.arange(LANES)
    tw = jnp.asarray(np.stack(unit(ids[:, None] * ids[None, :], NAZ, 1.0)), F32)
    consts = [
        *movers,
        jnp.asarray(left_table(1.0, 1.0, ids // CHUNKS + PER_CHUNK * (ids % CHUNKS))),
        jnp.asarray(left_table(1.0, 1.0 / NAZ)),
        tw,
    ]
    start, gap_at = places[0], len(places)
    for i, place in enumerate(places):
        if place != start + i:
            gap_at = i
            break
    gap = places[-1] - start - len(places) + 1

    def early(i):
        return (jnp.minimum(i, steps - 1), 0, 0, 0)

    def early_second(i):
        return (0, jnp.minimum(i, steps - 1), 0, 0)

    def late(i):
        at = jnp.maximum(i - steps - 1, 0)
        return (0, start + at + jnp.where(at >= gap_at, gap, 0), 0)

    joined = (CHUNKS, PER_CHUNK, 2 * bins, 2 * LANES)
    joined_spec = pl.BlockSpec((CHUNKS, KB, 2 * bins, 2 * LANES), early_second)
    given = [*sources, *lows, *highs, *phases, *consts]
    specs = [pl.BlockSpec((KB, 2, bins, LANES), early)] * CHUNKS if joins else [joined_spec]
    specs += [pl.BlockSpec((KB, 2, HALO, LANES), early)] * (2 * CHUNKS if wide else 0)
    if wide:
        specs += [whole_spec(a) for a in phases]
    else:
        specs += [
            pl.BlockSpec((2, KB, 2, rows, LANES), lambda i: (0, jnp.minimum(i, steps - 1), 0, 0, 0))
        ] * len(phases)
    specs += [whole_spec(a) for a in consts]
    aliases = {}
    if image is not None:
        aliases = {len(given): 0}
        given.append(image)
        specs.append(pl.BlockSpec(memory_space=pl.ANY))
    shapes = [jax.ShapeDtypeStruct((2, bins, NAZ), F32)]
    out_specs = [pl.BlockSpec((2, BB, NAZ), late)]
    scratch = []
    if joins and wide:
        scratch.append(pltpu.VMEM((CHUNKS, KB, 2 * bins, 2 * LANES), BF16))
    elif joins:
        shapes.append(jax.ShapeDtypeStruct(joined, BF16))
        out_specs.append(pl.BlockSpec(memory_space=pl.ANY))
        scratch.append(pltpu.VMEM(joined, BF16))
    else:
        scratch.append(pltpu.VMEM((16, LANES), BF16))
    scratch += [
        pltpu.VMEM((rows, LANES, LANES), F32),
        pltpu.VMEM((rows, LANES, LANES), F32),
        pltpu.VMEM((2, BB, LANES, LANES), F32),
        pltpu.VMEM((2, 2, CHUNKS, rows, LANES), F32),
        pltpu.VMEM((BB // QUAD, QUAD * LANES, 6 * LANES), BF16),
    ]
    if wide:
        scratch.append(pltpu.VMEM((2, CHUNKS, 4 * HALO, 2 * LANES), BF16))
    else:
        scratch.append(pltpu.SemaphoreType.DMA((CHUNKS,)))
    points = NAZ * rows
    return pl.pallas_call(
        functools.partial(final_kernel, steps, joins, wide),
        grid=(steps + 1 + len(places),),
        in_specs=specs,
        out_specs=out_specs,
        out_shape=shapes,
        scratch_shapes=scratch,
        input_output_aliases=aliases,
        compiler_params=pltpu.CompilerParams(vmem_limit_bytes=VMEM_LIMIT),
        cost_estimate=pl.CostEstimate(
            flops=points * 8 * LANES * 9, bytes_accessed=28 * points, transcendentals=0
        ),
        name="final_wide" if wide else "final_inner",
    )(*given)


def mover_table(rows, columns, shift_table, filter_index, tap_table):
    shift_table, filter_index = shift_table[:, rows], filter_index[:, rows]
    onehot = (filter_index[:, :, None] == jnp.arange(NFILT, dtype=jnp.int32)).astype(F32)
    weights = jnp.einsum("gbf,ft->gbt", onehot, tap_table, precision=lax.Precision.HIGHEST)
    first = rows[None, :].astype(np.int32) + shift_table + (HALO - 4)
    offset = columns.astype(np.int32)[None, None, :] - first[:, :, None]
    table = jnp.zeros(offset.shape, F32)
    for t in range(TAPS):
        table = table + jnp.where(offset == t, weights[:, :, t : t + 1], 0.0)
    high = lax.reduce_precision(table, 8, 7)
    low = table - high
    top = jnp.concatenate([high, high], axis=2)
    bottom = jnp.concatenate([low, jnp.zeros_like(low)], axis=2)
    return jnp.concatenate([top, bottom], axis=1).astype(BF16)


def own_columns(bins):
    return np.arange(HALO, HALO + bins)


def halo_columns(bins):
    return np.concatenate([np.arange(HALO), np.arange(bins + HALO, bins + 2 * HALO)])


def row_sets(bins):
    blocks = np.arange(bins // BB)
    inner = (blocks >= HALO // BB) & (blocks < (bins - HALO) // BB)
    return [blocks[chosen].tolist() for chosen in (inner, ~inner) if chosen.any()]


def bins_of(places):
    return np.concatenate([np.arange(BB) + BB * place for place in places])


def neighbours(axes, size, step):
    return [(i, i + step) for i in range(size) if 0 <= i + step < size]


def local(nrng, naz, raw_echo, chirp_spectrum, azimuth_rate, shift_table, filter_index, tap_table):
    axes = ("rng", "az")
    devices = nrng * naz
    bins = NRG // devices
    rows_in = raw_echo.shape[1] // LANES
    per_part = PER_CHUNK // nrng
    chirp = chirp_spectrum.reshape(2, LANES, RG1).transpose(0, 2, 1)
    rate = jnp.broadcast_to((azimuth_rate * 0.5)[:, None], (bins, LANES))
    rank = lax.axis_index("rng").astype(jnp.int32).reshape(1)
    packed = pack(raw_echo, rank, nrng, GROUPED[:1]) + pack(raw_echo, rank, nrng, GROUPED[1:])
    mains, lows, highs = [None] * CHUNKS, [None] * CHUNKS, [None] * CHUNKS
    turned = []

    def gather(g):
        return [packed[g][0]] + [
            lax.ppermute(packed[g][j], "rng", [(i, i ^ j) for i in range(nrng)])
            for j in range(1, nrng)
        ]

    def transform(g):
        for place, c in enumerate(GROUPED[g]):
            if c > 0:
                turned[g], mains[c - 1] = lax.optimization_barrier((turned[g], mains[c - 1]))
            main, up, down = azimuth(turned[g], c, place)
            mains[c] = main
            lows[c] = lax.ppermute(up, axes, neighbours(axes, devices, 1))
            highs[c] = lax.ppermute(down, axes, neighbours(axes, devices, -1))

    places = row_sets(bins)
    rates = [rate[bins_of(p)] for p in places]
    inner_rate = rates[0]
    phases = []
    got = [gather(0)]
    packed[1], got[0] = lax.optimization_barrier((packed[1], got[0]))
    got.append(gather(1))
    count = len(GROUPED)
    for g, chunks in enumerate(GROUPED):
        lines = compress(got[g], rank, chirp)
        if g + 1 < count:
            held = got[g + 1][1 : (3 if g < 2 else nrng)]
            lines, held = lax.optimization_barrier((lines, held))
            got[g + 1][1 : 1 + len(held)] = held
        if g + 2 < count:
            packed[g + 2], got[g + 1] = lax.optimization_barrier((packed[g + 2], got[g + 1]))
            if g >= 1:
                held = (packed[g + 2], turned[g - 1])
                packed[g + 2], turned[g - 1] = lax.optimization_barrier(held)
            got.append(gather(g + 2))
        if g >= 2:
            transform(g - 2)
            for c in GROUPED[g - 2]:
                lines, mains[c] = lax.optimization_barrier((lines, mains[c]))
        if g >= 3:
            for c in GROUPED[g - 3]:
                held = (lines, lows[c], highs[c])
                lines, lows[c], highs[c] = lax.optimization_barrier(held)
        if 2 <= g and len(places) > 1 and len(phases) < CHUNKS // 2:
            inner_rate, turned[g - 2] = lax.optimization_barrier((inner_rate, turned[g - 2]))
            table = phase_table(inner_rate, len(phases))
            lines, table = lax.optimization_barrier((lines, table))
            phases.append(table)
        if bins < LANES:
            cut = lines.reshape(RG1, 2, -1, LANES // bins, bins)
            lines = cut.transpose(0, 3, 1, 2, 4).reshape(devices, 2, -1, bins)
        moved = lax.all_to_all(lines, axes, split_axis=0, concat_axis=0, tiled=True)
        turned.append(moved.reshape(nrng, naz, 2, len(chunks), per_part, rows_in, bins))
    transform(count - 2)
    transform(count - 1)
    tables = (shift_table, filter_index, tap_table)
    image, sources = None, mains
    for i, places_of in enumerate(places):
        ids = bins_of(places_of)
        wide = i == len(places) - 1
        halos = (lows, highs) if wide else ([], [])
        columns = [own_columns(bins), halo_columns(bins)] if wide else [own_columns(bins)]
        movers = [mover_table(ids, cols, *tables) for cols in columns]
        result = final(
            bins, places_of, sources, *halos, [rates[i]] if wide else phases, movers, image
        )
        image, sources = result[0], result[1:]
    return image


def solution(mesh):
    return jax.shard_map(
        functools.partial(local, mesh.shape["rng"], mesh.shape["az"]),
        mesh=mesh,
        in_specs=(
            P(None, "az", "rng"),
            P(),
            P(("rng", "az")),
            P(None, ("rng", "az")),
            P(None, ("rng", "az")),
            P(),
        ),
        out_specs=P(None, ("rng", "az"), None),
        check_vma=False,
    )
```

```python
import functools

import jax
import jax.numpy as jnp
import ml_dtypes
import numpy as np
from jax import lax
from jax.experimental import pallas as pl
from jax.experimental.pallas import tpu as pltpu
from jax.sharding import PartitionSpec as P

NRG = 4096
NAZ = 16384
GROUPS = 16
NFILT = 16
TAPS = 8
HALO = 32
LANES = 128
RG1 = NRG // LANES
CHUNKS = 8
PER_CHUNK = LANES // CHUNKS
GROUPED = tuple((c,) for c in range(CHUNKS))
VMEM_LIMIT = 60 << 20
BF16 = jnp.bfloat16
F32 = jnp.float32


def split_np(table):
    table = np.asarray(table, np.float32)
    high = table.astype(ml_dtypes.bfloat16)
    low = (table - high.astype(np.float32)).astype(ml_dtypes.bfloat16)
    return high, low


def unit(angle_num, period, sign):
    angles = (np.asarray(angle_num, np.int64) % period) * (2.0 * np.pi / period)
    return np.cos(angles), sign * np.sin(angles)


def dft_matrix(sign):
    ids = np.arange(LANES)
    return unit(ids[:, None] * ids[None, :], LANES, sign)


def right_tables(sign, scale=1.0):
    c, s = dft_matrix(sign)
    return split_np(np.block([[c, s], [-s, c]]) * scale)


def left_table(sign, scale=1.0, order=np.arange(LANES)):
    c, s = (part[:, order] for part in dft_matrix(sign))
    high, low = split_np(np.block([[c, -s], [s, c]]) * scale)
    return np.concatenate([high, high, low], axis=1)


def split(x):
    high = x.astype(BF16)
    low = (x - high.astype(F32)).astype(BF16)
    return high, low


def dot(a, b):
    return jnp.dot(a, b, preferred_element_type=F32)


def scale_by(value, re, im):
    a, b = value
    eps = 1e-12
    if abs(im) < eps:
        if abs(re - 1.0) < eps:
            return value
        if abs(re + 1.0) < eps:
            return -a, -b
    if abs(re) < eps:
        if abs(im - 1.0) < eps:
            return -b, a
        if abs(im + 1.0) < eps:
            return b, -a
    if abs(abs(re) - abs(im)) < eps:
        sr, si = (1.0 if re > 0 else -1.0), (1.0 if im > 0 else -1.0)
        h = abs(re)
        total, diff = (a + b) * h, (a - b) * h
        if si == sr:
            return (diff, total) if sr > 0 else (-diff, -total)
        return (total, -diff) if sr > 0 else (-total, diff)
    re, im = float(re), float(im)
    return a * re - b * im, a * im + b * re


def dft_list(values, sign):
    count = len(values)
    if count == 1:
        return values
    even, odd = dft_list(values[0::2], sign), dft_list(values[1::2], sign)
    first, second = [], []
    for k in range(count // 2):
        re, im = unit(k, count, sign)
        a, b = even[k], scale_by(odd[k], float(re), float(im))
        first.append((a[0] + b[0], a[1] + b[1]))
        second.append((a[0] - b[0], a[1] - b[1]))
    return first + second


def dft_two_step(load, mid_ref, finish, outer, inner, sign):
    for ib in range(inner):
        column = dft_list([load(ia * inner + ib) for ia in range(outer)], sign)
        for ka in range(outer):
            re, im = unit(ib * ka, outer * inner, sign)
            a, b = scale_by(column[ka], float(re), float(im))
            mid_ref[ka * inner + ib, 0] = a
            mid_ref[ka * inner + ib, 1] = b
    for ka in range(outer):
        row = [(mid_ref[ka * inner + ib, 0], mid_ref[ka * inner + ib, 1]) for ib in range(inner)]
        for kb, value in enumerate(dft_list(row, sign)):
            finish(ka + outer * kb, value)


def pack_kernel(groups, parts, per_part, rows_in, rank_ref, x_ref, *out_refs):
    rank = rank_ref[0]
    for j in range(parts):
        part = jnp.bitwise_xor(rank, j)
        for g, chunks in enumerate(groups):
            for at, c in enumerate(chunks):
                for m in range(per_part):
                    start = CHUNKS * (part * per_part + m) + c
                    to = (at * per_part + m) * rows_in
                    for ri in range(2):
                        out_refs[g * parts + j][ri, 0, to : to + rows_in, :] = x_ref[
                            ri, pl.ds(start, rows_in, stride=LANES), :
                        ]


def pack(raw, rank, parts, groups):
    lines, bins = raw.shape[1], raw.shape[2]
    rows_in, tiles, per_part = lines // LANES, bins // LANES, PER_CHUNK // parts
    heights = [len(chunks) * per_part * rows_in for chunks in groups for _ in range(parts)]
    flat = pl.pallas_call(
        functools.partial(pack_kernel, groups, parts, per_part, rows_in),
        grid=(tiles,),
        in_specs=[
            pl.BlockSpec(memory_space=pltpu.SMEM),
            pl.BlockSpec((2, lines, LANES), lambda i: (0, 0, i)),
        ],
        out_specs=[pl.BlockSpec((2, 1, rows, LANES), lambda i: (0, i, 0, 0)) for rows in heights],
        out_shape=[jax.ShapeDtypeStruct((2, tiles, rows, LANES), F32) for rows in heights],
        compiler_params=pltpu.CompilerParams(vmem_limit_bytes=VMEM_LIMIT),
        cost_estimate=pl.CostEstimate(flops=0, bytes_accessed=16 * lines * bins, transcendentals=0),
        name="pack",
    )(rank, raw)
    return [flat[i * parts : (i + 1) * parts] for i in range(len(groups))]


STEP = 16


def compress_kernel(parts, rows, rank_ref, *refs):
    x_refs = refs[:parts]
    chirp_ref, tw_ref, fwd_ref, fwd_low_ref, inv_ref, inv_low_ref = refs[parts : parts + 6]
    out_ref, buf_ref, lhs_ref, y_ref, mid_ref, sems = refs[parts + 6 :]
    tiles = buf_ref.shape[3]
    rank = rank_ref[0]
    step = pl.program_id(0)
    slot = lax.rem(step, 2)

    def copies(at, to):
        return [
            pltpu.make_async_copy(
                x_refs[j].at[:, :, pl.ds(pl.multiple_of(at * rows, rows), rows), :],
                buf_ref.at[to, jnp.bitwise_xor(rank, j)],
                sems.at[to, j],
            )
            for j in range(parts)
        ]

    @pl.when(step == 0)
    def _():
        for copy in copies(step, slot):
            copy.start()

    @pl.when(step + 1 < pl.num_programs(0))
    def _():
        for copy in copies(step + 1, 1 - slot):
            copy.start()

    for copy in copies(step, slot):
        copy.wait()

    def put(at, re, im):
        for half, part in enumerate((re, im)):
            high, low = split(part)
            lhs_ref[at, half * LANES : (half + 1) * LANES] = high
            lhs_ref[at, (2 + half) * LANES : (3 + half) * LANES] = low

    def forward(i, carry):
        at = pl.ds(pl.multiple_of(i * STEP, STEP), STEP)

        def load(p):
            source = buf_ref.at[slot, p // tiles]
            return source[0, p % tiles, at, :], source[1, p % tiles, at, :]

        def finish(k, value):
            wr, wi = tw_ref[0, k : k + 1, :], tw_ref[1, k : k + 1, :]
            a, b = value
            put(
                pl.ds(pl.multiple_of(k * rows + i * STEP, STEP), STEP),
                a * wr - b * wi,
                a * wi + b * wr,
            )

        dft_two_step(load, mid_ref, finish, 4, RG1 // 4, -1.0)
        return carry

    lax.fori_loop(0, rows // STEP, forward, 0)

    group = max(1, 2 * LANES // rows)

    def middle(i, carry):
        at = pl.ds(pl.multiple_of(i * group * rows, group * rows), group * rows)
        y = dot(lhs_ref[at, :], fwd_ref[...]) + dot(lhs_ref[at, 0 : 2 * LANES], fwd_low_ref[...])
        for s in range(group):
            k = i * group + s
            cr, ci = chirp_ref[0, pl.ds(k, 1), :], chirp_ref[1, pl.ds(k, 1), :]
            a = y[s * rows : (s + 1) * rows, 0:LANES]
            b = y[s * rows : (s + 1) * rows, LANES : 2 * LANES]
            put(pl.ds(pl.multiple_of(k * rows, rows), rows), a * cr - b * ci, a * ci + b * cr)
        z = dot(lhs_ref[at, :], inv_ref[...]) + dot(lhs_ref[at, 0 : 2 * LANES], inv_low_ref[...])
        for s in range(group):
            k = i * group + s
            wr, wi = tw_ref[0, pl.ds(k, 1), :], tw_ref[1, pl.ds(k, 1), :]
            a = z[s * rows : (s + 1) * rows, 0:LANES]
            b = z[s * rows : (s + 1) * rows, LANES : 2 * LANES]
            y_ref[k, 0] = a * wr + b * wi
            y_ref[k, 1] = b * wr - a * wi
        return carry

    lax.fori_loop(0, RG1 // group, middle, 0)

    def backward(i, carry):
        at = pl.ds(pl.multiple_of(i * STEP, STEP), STEP)

        def load(k):
            return y_ref[k, 0, at, :], y_ref[k, 1, at, :]

        def finish(p, value):
            out_ref[p, 0, at, :] = value[0]
            out_ref[p, 1, at, :] = value[1]

        dft_two_step(load, mid_ref, finish, 4, RG1 // 4, 1.0)
        return carry

    lax.fori_loop(0, rows // STEP, backward, 0)


def whole_spec(array):
    zeros = (0,) * array.ndim
    return pl.BlockSpec(array.shape, lambda *_: zeros)


def compress(pieces, rank, chirp):
    parts = len(pieces)
    _, tiles, rows, _ = pieces[0].shape
    block = min(rows, 64)
    ids = np.arange(RG1)[:, None] * np.arange(LANES)[None, :]
    tw = jnp.asarray(np.stack(unit(ids, NRG, -1.0)), F32)
    fwd, fwd_low = right_tables(-1.0)
    inv, inv_low = right_tables(1.0, 1.0 / NRG)
    consts = [
        chirp,
        tw,
        jnp.asarray(np.concatenate([fwd, fwd])),
        jnp.asarray(fwd_low),
        jnp.asarray(np.concatenate([inv, inv])),
        jnp.asarray(inv_low),
    ]
    points = rows * NRG
    return pl.pallas_call(
        functools.partial(compress_kernel, parts, block),
        grid=(rows // block,),
        in_specs=[pl.BlockSpec(memory_space=pltpu.SMEM)]
        + [pl.BlockSpec(memory_space=pl.ANY)] * parts
        + [whole_spec(a) for a in consts],
        out_specs=pl.BlockSpec((RG1, 2, block, LANES), lambda i: (0, 0, i, 0)),
        out_shape=jax.ShapeDtypeStruct((RG1, 2, rows, LANES), F32),
        scratch_shapes=[
            pltpu.VMEM((2, parts, 2, tiles, block, LANES), F32),
            pltpu.VMEM((RG1 * block, 4 * LANES), BF16),
            pltpu.VMEM((RG1, 2, block, LANES), F32),
            pltpu.VMEM((RG1, 2, STEP, LANES), F32),
            pltpu.SemaphoreType.DMA((2, parts)),
        ],
        compiler_params=pltpu.CompilerParams(vmem_limit_bytes=VMEM_LIMIT),
        cost_estimate=pl.CostEstimate(
            flops=points * 8 * LANES * 6, bytes_accessed=16 * points, transcendentals=0
        ),
        name="compress",
    )(rank, *pieces, *consts)


def azimuth_kernel(chunk, x_ref, tw_ref, fwd_ref, fwd_low_ref, out_ref, up_ref, down_ref, t_ref, mid_ref):
    part = pl.program_id(0)
    pieces, per_part, bins = x_ref.shape[1], x_ref.shape[4], x_ref.shape[6]

    def stage(m):
        sides = []
        for ri in range(2):
            column = jnp.concatenate([x_ref[0, a, ri, 0, m] for a in range(pieces)], axis=0)
            sides.append(split(jnp.transpose(column)))
        high = jnp.concatenate([sides[0][0], sides[1][0]], axis=1)
        low = jnp.concatenate([sides[0][1], sides[1][1]], axis=1)
        y = dot(high, fwd_ref[...]) + dot(low, fwd_ref[...]) + dot(high, fwd_low_ref[...])
        index = part * per_part + m
        at = pl.ds(CHUNKS * index + chunk, 1)
        wr, wi = tw_ref[0, at, :], tw_ref[1, at, :]
        a, b = y[:, 0:LANES], y[:, LANES : 2 * LANES]
        t_ref[index, 0] = a * wr - b * wi
        t_ref[index, 1] = a * wi + b * wr

    for m in range(per_part):
        stage(m)

    @pl.when(part == pl.num_programs(0) - 1)
    def _():
        def rest(i, carry):
            at = pl.ds(pl.multiple_of(i * STEP, STEP), STEP)

            def load(m):
                return t_ref[m, 0, at, :], t_ref[m, 1, at, :]

            def finish(k, value):
                re, im = unit(chunk * k, LANES, -1.0)
                a, b = scale_by(value, float(re), float(im))
                out_ref[k, 0, at, :] = a
                out_ref[k, 1, at, :] = b

            dft_two_step(load, mid_ref, finish, 4, PER_CHUNK // 4, -1.0)
            return carry

        lax.fori_loop(0, bins // STEP, rest, 0)

        def edges(k, carry):
            for ri in range(2):
                up_ref[k, ri] = out_ref[k, ri, bins - HALO : bins, :]
                down_ref[k, ri] = out_ref[k, ri, 0:HALO, :]
            return carry

        lax.fori_loop(0, PER_CHUNK, edges, 0)


def azimuth(x, chunk, place):
    parts, pieces, _, _, per_part, rows_in, bins = x.shape
    ids = np.arange(LANES)
    tw = jnp.asarray(np.stack(unit(ids[:, None] * ids[None, :], NAZ, -1.0)), F32)
    fwd, fwd_low = right_tables(-1.0)
    consts = [tw, jnp.asarray(fwd), jnp.asarray(fwd_low)]
    points = PER_CHUNK * LANES * bins
    shape = (PER_CHUNK, 2, bins, LANES)
    edge = (PER_CHUNK, 2, HALO, LANES)
    return pl.pallas_call(
        functools.partial(azimuth_kernel, chunk),
        grid=(parts,),
        in_specs=[
            pl.BlockSpec(
                (1, pieces, 2, 1, per_part, rows_in, bins),
                lambda i: (i, 0, 0, place, 0, 0, 0),
            )
        ]
        + [whole_spec(a) for a in consts],
        out_specs=[pl.BlockSpec(s, lambda i: (0, 0, 0, 0)) for s in (shape, edge, edge)],
        out_shape=[jax.ShapeDtypeStruct(s, F32) for s in (shape, edge, edge)],
        scratch_shapes=[pltpu.VMEM(shape, F32), pltpu.VMEM((PER_CHUNK, 2, STEP, LANES), F32)],
        compiler_params=pltpu.CompilerParams(vmem_limit_bytes=VMEM_LIMIT),
        cost_estimate=pl.CostEstimate(
            flops=points * 8 * LANES * 3, bytes_accessed=16 * points, transcendentals=0
        ),
        name=f"azimuth{chunk}",
    )(x, *consts)


KB = 4
BB = 8
QUAD = 4


def fit(fn, even):
    nodes = np.cos((2 * np.arange(64) + 1) * np.pi / 128) * 0.25
    z2 = (nodes + 0.25) / 2
    z = np.sqrt(z2)
    goal = fn(np.pi * z) if even else fn(np.pi * z) / z
    return [float(v) for v in np.polynomial.polynomial.polyfit(z2, goal, 4)]


SIN_FIT, COS_FIT = fit(np.sin, False), fit(np.cos, True)


def horner(coefficients, x):
    total = coefficients[-1]
    for c in reversed(coefficients[:-1]):
        total = total * x + c
    return total


def square_of(k2):
    f = k2 * LANES + lax.broadcasted_iota(jnp.int32, (1, LANES), 1)
    centred = jnp.where(f >= NAZ // 2, f - NAZ, f).astype(F32) * (1.0 / NAZ)
    return centred * centred


def turn(t):
    z = t - jnp.round(t)
    z2 = z * z
    s = horner(SIN_FIT, z2) * z
    c = horner(COS_FIT, z2)
    twice = s + s
    return 1.0 - twice * s, twice * c


def phase_kernel(part, rate_ref, out_ref):
    k = pl.program_id(0)
    for half in range(2):
        c, s = turn(rate_ref[...] * square_of(k + PER_CHUNK * (2 * part + half)))
        out_ref[half, 0, 0] = c
        out_ref[half, 0, 1] = s


def phase_table(rate, part):
    shape = (2, PER_CHUNK, 2, rate.shape[0], LANES)
    points = 2 * PER_CHUNK * rate.size
    return pl.pallas_call(
        functools.partial(phase_kernel, part),
        grid=(PER_CHUNK,),
        in_specs=[whole_spec(rate)],
        out_specs=pl.BlockSpec((2, 1) + shape[2:], lambda i: (0, i, 0, 0, 0)),
        out_shape=jax.ShapeDtypeStruct(shape, F32),
        compiler_params=pltpu.CompilerParams(vmem_limit_bytes=VMEM_LIMIT),
        cost_estimate=pl.CostEstimate(
            flops=40 * points, bytes_accessed=8 * points, transcendentals=0
        ),
        name="phase",
    )(rate)


def combine(sources, kk, start, put):
    at = slice(start, start + STEP)
    values = [(ref[kk, 0, at, :], ref[kk, 1, at, :]) for ref in sources]
    for q, value in enumerate(dft_list(values, -1.0)):
        for half, part in enumerate(value):
            high, low = split(part)
            put(q, slice(half * LANES, (half + 1) * LANES), high, low)


def final_kernel(steps, joins, wide, *refs):
    refs = list(refs)

    def take(count):
        taken = refs[:count]
        del refs[:count]
        return taken

    sources = take(CHUNKS) if joins else take(1)
    low_refs, high_refs = (take(CHUNKS), take(CHUNKS)) if wide else ((), ())
    phase_refs = take(1 if wide else CHUNKS // 2)
    mover_refs = take(2 if wide else 1)
    inv1_ref, inv2_ref, tw_ref = take(3)
    if not joins or wide:
        out_ref, own_ref, zr_ref, zi_ref, s_ref, swap_ref, half_ref, halo_ref = refs[-8:]
        if not joins:
            own_ref = sources[0]
    else:
        out_ref, joined_ref, own_ref, zr_ref, zi_ref, s_ref, swap_ref, half_ref, sems = refs[-9:]
    step = pl.program_id(0)
    own = own_ref.shape[2] // 2
    rows = zr_ref.shape[0]
    keeps = joins and not wide
    copies = []
    if keeps:
        copies = [
            pltpu.make_async_copy(own_ref.at[q], joined_ref.at[q], sems.at[q])
            for q in range(CHUNKS)
        ]

    def own_at(kk):
        return step * KB + kk if keeps else kk

    def first_half(block):
        base = jnp.minimum(block * BB, rows - BB)
        for j in range(BB // QUAD):
            cols = []
            for t in range(QUAD):
                at = base + QUAD * j + t
                cols.append(jnp.concatenate([zr_ref[at], zi_ref[at]], axis=0))
            hi, lo = split(jnp.concatenate(cols, axis=1))
            w = dot(inv1_ref[...], jnp.concatenate([hi, lo, hi], axis=0))
            turned = []
            for t in range(QUAD):
                a = w[0:LANES, t * LANES : (t + 1) * LANES]
                b = w[LANES : 2 * LANES, t * LANES : (t + 1) * LANES]
                wr, wi = tw_ref[0], tw_ref[1]
                turned.append(jnp.concatenate([a * wr - b * wi, a * wi + b * wr], axis=1))
            hi, lo = split(jnp.concatenate(turned, axis=0))
            half_ref[j] = jnp.concatenate([hi, lo, hi], axis=1)

    @pl.when(step < steps)
    def _():
        def one(kk, buf):
            k = step * KB + kk
            if joins:
                for start in range(0, own, STEP):

                    def put_own(q, cols, high, low, start=start):
                        own_ref[q, own_at(kk), start : start + STEP, cols] = high
                        own_ref[q, own_at(kk), own + start : own + start + STEP, cols] = low

                    combine(sources, kk, start, put_own)
            if wide:
                for side, halo_refs in enumerate((low_refs, high_refs)):
                    for start in range(0, HALO, STEP):

                        def put_halo(q, cols, high, low, at=side * HALO + start):
                            halo_ref[buf, q, at : at + STEP, cols] = high
                            halo_ref[buf, q, 2 * HALO + at : 2 * HALO + at + STEP, cols] = low

                        combine(halo_refs, kk, start, put_halo)
            for q in range(CHUNKS):
                k2 = k + PER_CHUNK * q
                band = lax.div(k2, LANES // GROUPS)
                moved = dot(mover_refs[0][band], own_ref[q, own_at(kk)])
                if wide:
                    moved = moved + dot(mover_refs[1][band], halo_ref[buf, q])
                both = moved[0:rows, :] + moved[rows : 2 * rows, :]
                if wide:
                    c, s = turn(phase_refs[0][...] * square_of(k2))
                else:
                    c, s = phase_refs[q // 2][q % 2, kk, 0], phase_refs[q // 2][q % 2, kk, 1]
                a, b = both[:, 0:LANES], both[:, LANES : 2 * LANES]
                swap_ref[buf, 0, q] = a * c + b * s
                swap_ref[buf, 1, q] = b * c - a * s
            to = pl.ds(pl.multiple_of(k * CHUNKS, CHUNKS), CHUNKS)
            for start in range(0, rows, BB):
                at = slice(start, start + BB)
                zr_ref[at, to, :] = jnp.swapaxes(swap_ref[buf, 0, :, at, :], 0, 1)
                zi_ref[at, to, :] = jnp.swapaxes(swap_ref[buf, 1, :, at, :], 0, 1)

        for kk in range(KB):
            one(kk, kk % 2)

    @pl.when(step > steps)
    def _():
        for j in range(BB // QUAD):
            image = lax.dot_general(
                inv2_ref[...], half_ref[j], (((1,), (1,)), ((), ())), preferred_element_type=F32
            )
            for t in range(QUAD):
                for ri in range(2):
                    s_ref[ri, QUAD * j + t] = image[
                        ri * LANES : (ri + 1) * LANES, t * LANES : (t + 1) * LANES
                    ]
        first_half(step - steps)
        for ri in range(2):
            for start in range(0, LANES, 8):
                lines = jnp.swapaxes(s_ref[ri, :, start : start + 8, :], 0, 1)
                for n in range(8):
                    at = (start + n) * LANES
                    out_ref[ri, :, at : at + LANES] = lines[n]

    @pl.when(step == steps)
    def _():
        for copy in copies:
            copy.start()
        first_half(0)

    @pl.when(step == pl.num_programs(0) - 1)
    def _():
        for copy in copies:
            copy.wait()


def final(bins, places, sources, lows, highs, phases, movers, image=None):
    joins, wide = len(sources) > 1, len(lows) > 0
    rows = len(places) * BB
    steps = PER_CHUNK // KB
    ids = np.arange(LANES)
    tw = jnp.asarray(np.stack(unit(ids[:, None] * ids[None, :], NAZ, 1.0)), F32)
    consts = [
        *movers,
        jnp.asarray(left_table(1.0, 1.0, ids // CHUNKS + PER_CHUNK * (ids % CHUNKS))),
        jnp.asarray(left_table(1.0, 1.0 / NAZ)),
        tw,
    ]
    start, gap_at = places[0], len(places)
    for i, place in enumerate(places):
        if place != start + i:
            gap_at = i
            break
    gap = places[-1] - start - len(places) + 1

    def early(i):
        return (jnp.minimum(i, steps - 1), 0, 0, 0)

    def early_second(i):
        return (0, jnp.minimum(i, steps - 1), 0, 0)

    def late(i):
        at = jnp.maximum(i - steps - 1, 0)
        return (0, start + at + jnp.where(at >= gap_at, gap, 0), 0)

    joined = (CHUNKS, PER_CHUNK, 2 * bins, 2 * LANES)
    joined_spec = pl.BlockSpec((CHUNKS, KB, 2 * bins, 2 * LANES), early_second)
    given = [*sources, *lows, *highs, *phases, *consts]
    specs = [pl.BlockSpec((KB, 2, bins, LANES), early)] * CHUNKS if joins else [joined_spec]
    specs += [pl.BlockSpec((KB, 2, HALO, LANES), early)] * (2 * CHUNKS if wide else 0)
    if wide:
        specs += [whole_spec(a) for a in phases]
    else:
        specs += [
            pl.BlockSpec((2, KB, 2, rows, LANES), lambda i: (0, jnp.minimum(i, steps - 1), 0, 0, 0))
        ] * len(phases)
    specs += [whole_spec(a) for a in consts]
    aliases = {}
    if image is not None:
        aliases = {len(given): 0}
        given.append(image)
        specs.append(pl.BlockSpec(memory_space=pl.ANY))
    shapes = [jax.ShapeDtypeStruct((2, bins, NAZ), F32)]
    out_specs = [pl.BlockSpec((2, BB, NAZ), late)]
    scratch = []
    if joins and wide:
        scratch.append(pltpu.VMEM((CHUNKS, KB, 2 * bins, 2 * LANES), BF16))
    elif joins:
        shapes.append(jax.ShapeDtypeStruct(joined, BF16))
        out_specs.append(pl.BlockSpec(memory_space=pl.ANY))
        scratch.append(pltpu.VMEM(joined, BF16))
    else:
        scratch.append(pltpu.VMEM((16, LANES), BF16))
    scratch += [
        pltpu.VMEM((rows, LANES, LANES), F32),
        pltpu.VMEM((rows, LANES, LANES), F32),
        pltpu.VMEM((2, BB, LANES, LANES), F32),
        pltpu.VMEM((2, 2, CHUNKS, rows, LANES), F32),
        pltpu.VMEM((BB // QUAD, QUAD * LANES, 6 * LANES), BF16),
    ]
    if wide:
        scratch.append(pltpu.VMEM((2, CHUNKS, 4 * HALO, 2 * LANES), BF16))
    else:
        scratch.append(pltpu.SemaphoreType.DMA((CHUNKS,)))
    points = NAZ * rows
    return pl.pallas_call(
        functools.partial(final_kernel, steps, joins, wide),
        grid=(steps + 1 + len(places),),
        in_specs=specs,
        out_specs=out_specs,
        out_shape=shapes,
        scratch_shapes=scratch,
        input_output_aliases=aliases,
        compiler_params=pltpu.CompilerParams(vmem_limit_bytes=VMEM_LIMIT),
        cost_estimate=pl.CostEstimate(
            flops=points * 8 * LANES * 9, bytes_accessed=28 * points, transcendentals=0
        ),
        name="final_wide" if wide else "final_inner",
    )(*given)


def mover_table(rows, columns, shift_table, filter_index, tap_table):
    shift_table, filter_index = shift_table[:, rows], filter_index[:, rows]
    onehot = (filter_index[:, :, None] == jnp.arange(NFILT, dtype=jnp.int32)).astype(F32)
    weights = jnp.einsum("gbf,ft->gbt", onehot, tap_table, precision=lax.Precision.HIGHEST)
    first = rows[None, :].astype(np.int32) + shift_table + (HALO - 4)
    offset = columns.astype(np.int32)[None, None, :] - first[:, :, None]
    table = jnp.zeros(offset.shape, F32)
    for t in range(TAPS):
        table = table + jnp.where(offset == t, weights[:, :, t : t + 1], 0.0)
    high = lax.reduce_precision(table, 8, 7)
    low = table - high
    top = jnp.concatenate([high, high], axis=2)
    bottom = jnp.concatenate([low, jnp.zeros_like(low)], axis=2)
    return jnp.concatenate([top, bottom], axis=1).astype(BF16)


def own_columns(bins):
    return np.arange(HALO, HALO + bins)


def halo_columns(bins):
    return np.concatenate([np.arange(HALO), np.arange(bins + HALO, bins + 2 * HALO)])


def row_sets(bins):
    blocks = np.arange(bins // BB)
    inner = (blocks >= HALO // BB) & (blocks < (bins - HALO) // BB)
    return [blocks[chosen].tolist() for chosen in (inner, ~inner) if chosen.any()]


def bins_of(places):
    return np.concatenate([np.arange(BB) + BB * place for place in places])


def neighbours(axes, size, step):
    return [(i, i + step) for i in range(size) if 0 <= i + step < size]


def local(nrng, naz, raw_echo, chirp_spectrum, azimuth_rate, shift_table, filter_index, tap_table):
    axes = ("rng", "az")
    devices = nrng * naz
    bins = NRG // devices
    rows_in = raw_echo.shape[1] // LANES
    per_part = PER_CHUNK // nrng
    chirp = chirp_spectrum.reshape(2, LANES, RG1).transpose(0, 2, 1)
    rate = jnp.broadcast_to((azimuth_rate * 0.5)[:, None], (bins, LANES))
    rank = lax.axis_index("rng").astype(jnp.int32).reshape(1)
    packed = pack(raw_echo, rank, nrng, GROUPED[:1]) + pack(raw_echo, rank, nrng, GROUPED[1:])
    mains, lows, highs = [None] * CHUNKS, [None] * CHUNKS, [None] * CHUNKS
    turned = []

    def gather(g):
        return [packed[g][0]] + [
            lax.ppermute(packed[g][j], "rng", [(i, i ^ j) for i in range(nrng)])
            for j in range(1, nrng)
        ]

    def transform(g):
        for place, c in enumerate(GROUPED[g]):
            if c > 0:
                turned[g], mains[c - 1] = lax.optimization_barrier((turned[g], mains[c - 1]))
            if 0 < c < CHUNKS - 1:
                held = (turned[g], lows[c - 1], highs[c - 1])
                turned[g], lows[c - 1], highs[c - 1] = lax.optimization_barrier(held)
            main, up, down = azimuth(turned[g], c, place)
            mains[c] = main
            lows[c] = lax.ppermute(up, axes, neighbours(axes, devices, 1))
            highs[c] = lax.ppermute(down, axes, neighbours(axes, devices, -1))

    places = row_sets(bins)
    rates = [rate[bins_of(p)] for p in places]
    inner_rate = rates[0]
    phases = []
    got = [gather(0)]
    packed[1], got[0] = lax.optimization_barrier((packed[1], got[0]))
    got.append(gather(1))
    count = len(GROUPED)
    for g, chunks in enumerate(GROUPED):
        if g >= 2:
            transform(g - 2)
            for c in GROUPED[g - 2]:
                got[g], mains[c] = lax.optimization_barrier((got[g], mains[c]))
        lines = compress(got[g], rank, chirp)
        if g + 1 < count:
            lines, got[g + 1] = lax.optimization_barrier((lines, got[g + 1]))
        if g + 2 < count:
            packed[g + 2], got[g + 1] = lax.optimization_barrier((packed[g + 2], got[g + 1]))
            if g >= 1:
                held = (packed[g + 2], turned[g - 1])
                packed[g + 2], turned[g - 1] = lax.optimization_barrier(held)
            got.append(gather(g + 2))
        if 2 <= g and len(places) > 1 and len(phases) < CHUNKS // 2:
            inner_rate, turned[g - 2] = lax.optimization_barrier((inner_rate, turned[g - 2]))
            table = phase_table(inner_rate, len(phases))
            lines, table = lax.optimization_barrier((lines, table))
            phases.append(table)
        if bins < LANES:
            cut = lines.reshape(RG1, 2, -1, LANES // bins, bins)
            lines = cut.transpose(0, 3, 1, 2, 4).reshape(devices, 2, -1, bins)
        moved = lax.all_to_all(lines, axes, split_axis=0, concat_axis=0, tiled=True)
        turned.append(moved.reshape(nrng, naz, 2, len(chunks), per_part, rows_in, bins))
    transform(count - 2)
    transform(count - 1)
    tables = (shift_table, filter_index, tap_table)
    image, sources = None, mains
    for i, places_of in enumerate(places):
        ids = bins_of(places_of)
        wide = i == len(places) - 1
        halos = (lows, highs) if wide else ([], [])
        columns = [own_columns(bins), halo_columns(bins)] if wide else [own_columns(bins)]
        movers = [mover_table(ids, cols, *tables) for cols in columns]
        result = final(
            bins, places_of, sources, *halos, [rates[i]] if wide else phases, movers, image
        )
        image, sources = result[0], result[1:]
    return image


def solution(mesh):
    return jax.shard_map(
        functools.partial(local, mesh.shape["rng"], mesh.shape["az"]),
        mesh=mesh,
        in_specs=(
            P(None, "az", "rng"),
            P(),
            P(("rng", "az")),
            P(None, ("rng", "az")),
            P(None, ("rng", "az")),
            P(),
        ),
        out_specs=P(None, ("rng", "az"), None),
        check_vma=False,
    )
```

```python
import functools

import jax
import jax.numpy as jnp
import ml_dtypes
import numpy as np
from jax import lax
from jax.experimental import pallas as pl
from jax.experimental.pallas import tpu as pltpu
from jax.sharding import PartitionSpec as P

NRG = 4096
NAZ = 16384
GROUPS = 16
NFILT = 16
TAPS = 8
HALO = 32
LANES = 128
RG1 = NRG // LANES
CHUNKS = 8
PER_CHUNK = LANES // CHUNKS
GROUPED = tuple((c,) for c in range(CHUNKS))
VMEM_LIMIT = 60 << 20
BF16 = jnp.bfloat16
F32 = jnp.float32


def split_np(table):
    table = np.asarray(table, np.float32)
    high = table.astype(ml_dtypes.bfloat16)
    low = (table - high.astype(np.float32)).astype(ml_dtypes.bfloat16)
    return high, low


def unit(angle_num, period, sign):
    angles = (np.asarray(angle_num, np.int64) % period) * (2.0 * np.pi / period)
    return np.cos(angles), sign * np.sin(angles)


def dft_matrix(sign):
    ids = np.arange(LANES)
    return unit(ids[:, None] * ids[None, :], LANES, sign)


def right_tables(sign, scale=1.0):
    c, s = dft_matrix(sign)
    return split_np(np.block([[c, s], [-s, c]]) * scale)


def left_table(sign, scale=1.0, order=np.arange(LANES)):
    c, s = (part[:, order] for part in dft_matrix(sign))
    high, low = split_np(np.block([[c, -s], [s, c]]) * scale)
    return np.concatenate([high, low], axis=0)


def split(x):
    high = x.astype(BF16)
    low = (x - high.astype(F32)).astype(BF16)
    return high, low


def dot(a, b):
    return jnp.dot(a, b, preferred_element_type=F32)


def dot_nt(a, b):
    return lax.dot_general(a, b, (((1,), (1,)), ((), ())), preferred_element_type=F32)


def scale_by(value, re, im):
    a, b = value
    eps = 1e-12
    if abs(im) < eps:
        if abs(re - 1.0) < eps:
            return value
        if abs(re + 1.0) < eps:
            return -a, -b
    if abs(re) < eps:
        if abs(im - 1.0) < eps:
            return -b, a
        if abs(im + 1.0) < eps:
            return b, -a
    if abs(abs(re) - abs(im)) < eps:
        sr, si = (1.0 if re > 0 else -1.0), (1.0 if im > 0 else -1.0)
        h = abs(re)
        total, diff = (a + b) * h, (a - b) * h
        if si == sr:
            return (diff, total) if sr > 0 else (-diff, -total)
        return (total, -diff) if sr > 0 else (-total, diff)
    re, im = float(re), float(im)
    return a * re - b * im, a * im + b * re


def dft_list(values, sign):
    count = len(values)
    if count == 1:
        return values
    even, odd = dft_list(values[0::2], sign), dft_list(values[1::2], sign)
    first, second = [], []
    for k in range(count // 2):
        re, im = unit(k, count, sign)
        a, b = even[k], scale_by(odd[k], float(re), float(im))
        first.append((a[0] + b[0], a[1] + b[1]))
        second.append((a[0] - b[0], a[1] - b[1]))
    return first + second


def dft_two_step(load, mid_ref, finish, outer, inner, sign):
    for ib in range(inner):
        column = dft_list([load(ia * inner + ib) for ia in range(outer)], sign)
        for ka in range(outer):
            re, im = unit(ib * ka, outer * inner, sign)
            a, b = scale_by(column[ka], float(re), float(im))
            mid_ref[ka * inner + ib, 0] = a
            mid_ref[ka * inner + ib, 1] = b
    for ka in range(outer):
        row = [(mid_ref[ka * inner + ib, 0], mid_ref[ka * inner + ib, 1]) for ib in range(inner)]
        for kb, value in enumerate(dft_list(row, sign)):
            finish(ka + outer * kb, value)


def pack_kernel(groups, parts, per_part, rows_in, rank_ref, x_ref, *out_refs):
    rank = rank_ref[0]
    for j in range(parts):
        part = jnp.bitwise_xor(rank, j)
        for g, chunks in enumerate(groups):
            for at, c in enumerate(chunks):
                for m in range(per_part):
                    start = CHUNKS * (part * per_part + m) + c
                    to = (at * per_part + m) * rows_in
                    for ri in range(2):
                        out_refs[g * parts + j][ri, 0, to : to + rows_in, :] = x_ref[
                            ri, pl.ds(start, rows_in, stride=LANES), :
                        ]


def pack(raw, rank, parts, groups):
    lines, bins = raw.shape[1], raw.shape[2]
    rows_in, tiles, per_part = lines // LANES, bins // LANES, PER_CHUNK // parts
    heights = [len(chunks) * per_part * rows_in for chunks in groups for _ in range(parts)]
    flat = pl.pallas_call(
        functools.partial(pack_kernel, groups, parts, per_part, rows_in),
        grid=(tiles,),
        in_specs=[
            pl.BlockSpec(memory_space=pltpu.SMEM),
            pl.BlockSpec((2, lines, LANES), lambda i: (0, 0, i)),
        ],
        out_specs=[pl.BlockSpec((2, 1, rows, LANES), lambda i: (0, i, 0, 0)) for rows in heights],
        out_shape=[jax.ShapeDtypeStruct((2, tiles, rows, LANES), F32) for rows in heights],
        compiler_params=pltpu.CompilerParams(vmem_limit_bytes=VMEM_LIMIT),
        cost_estimate=pl.CostEstimate(flops=0, bytes_accessed=16 * lines * bins, transcendentals=0),
        name="pack",
    )(rank, raw)
    return [flat[i * parts : (i + 1) * parts] for i in range(len(groups))]


STEP = 16


def compress_kernel(parts, rows, rank_ref, *refs):
    x_refs = refs[:parts]
    chirp_ref, tw_ref, fwd_ref, fwd_low_ref, inv_ref, inv_low_ref = refs[parts : parts + 6]
    out_ref, buf_ref, lhs_ref, y_ref, mid_ref, sems = refs[parts + 6 :]
    tiles = buf_ref.shape[3]
    rank = rank_ref[0]
    step = pl.program_id(0)
    slot = lax.rem(step, 2)

    def copies(at, to):
        return [
            pltpu.make_async_copy(
                x_refs[j].at[:, :, pl.ds(pl.multiple_of(at * rows, rows), rows), :],
                buf_ref.at[to, jnp.bitwise_xor(rank, j)],
                sems.at[to, j],
            )
            for j in range(parts)
        ]

    @pl.when(step == 0)
    def _():
        for copy in copies(step, slot):
            copy.start()

    @pl.when(step + 1 < pl.num_programs(0))
    def _():
        for copy in copies(step + 1, 1 - slot):
            copy.start()

    for copy in copies(step, slot):
        copy.wait()

    def put(at, re, im):
        for half, part in enumerate((re, im)):
            high, low = split(part)
            lhs_ref[at, half * LANES : (half + 1) * LANES] = high
            lhs_ref[at, (2 + half) * LANES : (3 + half) * LANES] = low

    def forward(i, carry):
        at = pl.ds(pl.multiple_of(i * STEP, STEP), STEP)

        def load(p):
            source = buf_ref.at[slot, p // tiles]
            return source[0, p % tiles, at, :], source[1, p % tiles, at, :]

        def finish(k, value):
            wr, wi = tw_ref[0, k : k + 1, :], tw_ref[1, k : k + 1, :]
            a, b = value
            put(
                pl.ds(pl.multiple_of(k * rows + i * STEP, STEP), STEP),
                a * wr - b * wi,
                a * wi + b * wr,
            )

        dft_two_step(load, mid_ref, finish, 4, RG1 // 4, -1.0)
        return carry

    lax.fori_loop(0, rows // STEP, forward, 0)

    group = max(1, 2 * LANES // rows)

    def middle(i, carry):
        at = pl.ds(pl.multiple_of(i * group * rows, group * rows), group * rows)
        y = dot(lhs_ref[at, :], fwd_ref[...]) + dot(lhs_ref[at, 0 : 2 * LANES], fwd_low_ref[...])
        for s in range(group):
            k = i * group + s
            cr, ci = chirp_ref[0, pl.ds(k, 1), :], chirp_ref[1, pl.ds(k, 1), :]
            a = y[s * rows : (s + 1) * rows, 0:LANES]
            b = y[s * rows : (s + 1) * rows, LANES : 2 * LANES]
            put(pl.ds(pl.multiple_of(k * rows, rows), rows), a * cr - b * ci, a * ci + b * cr)
        z = dot(lhs_ref[at, :], inv_ref[...]) + dot(lhs_ref[at, 0 : 2 * LANES], inv_low_ref[...])
        for s in range(group):
            k = i * group + s
            wr, wi = tw_ref[0, pl.ds(k, 1), :], tw_ref[1, pl.ds(k, 1), :]
            a = z[s * rows : (s + 1) * rows, 0:LANES]
            b = z[s * rows : (s + 1) * rows, LANES : 2 * LANES]
            y_ref[k, 0] = a * wr + b * wi
            y_ref[k, 1] = b * wr - a * wi
        return carry

    lax.fori_loop(0, RG1 // group, middle, 0)

    def backward(i, carry):
        at = pl.ds(pl.multiple_of(i * STEP, STEP), STEP)

        def load(k):
            return y_ref[k, 0, at, :], y_ref[k, 1, at, :]

        def finish(p, value):
            out_ref[p, 0, at, :] = value[0]
            out_ref[p, 1, at, :] = value[1]

        dft_two_step(load, mid_ref, finish, 4, RG1 // 4, 1.0)
        return carry

    lax.fori_loop(0, rows // STEP, backward, 0)


def whole_spec(array):
    zeros = (0,) * array.ndim
    return pl.BlockSpec(array.shape, lambda *_: zeros)


def compress(pieces, rank, chirp):
    parts = len(pieces)
    _, tiles, rows, _ = pieces[0].shape
    block = min(rows, 64)
    ids = np.arange(RG1)[:, None] * np.arange(LANES)[None, :]
    tw = jnp.asarray(np.stack(unit(ids, NRG, -1.0)), F32)
    fwd, fwd_low = right_tables(-1.0)
    inv, inv_low = right_tables(1.0, 1.0 / NRG)
    consts = [
        chirp,
        tw,
        jnp.asarray(np.concatenate([fwd, fwd])),
        jnp.asarray(fwd_low),
        jnp.asarray(np.concatenate([inv, inv])),
        jnp.asarray(inv_low),
    ]
    points = rows * NRG
    return pl.pallas_call(
        functools.partial(compress_kernel, parts, block),
        grid=(rows // block,),
        in_specs=[pl.BlockSpec(memory_space=pltpu.SMEM)]
        + [pl.BlockSpec(memory_space=pl.ANY)] * parts
        + [whole_spec(a) for a in consts],
        out_specs=pl.BlockSpec((RG1, 2, block, LANES), lambda i: (0, 0, i, 0)),
        out_shape=jax.ShapeDtypeStruct((RG1, 2, rows, LANES), F32),
        scratch_shapes=[
            pltpu.VMEM((2, parts, 2, tiles, block, LANES), F32),
            pltpu.VMEM((RG1 * block, 4 * LANES), BF16),
            pltpu.VMEM((RG1, 2, block, LANES), F32),
            pltpu.VMEM((RG1, 2, STEP, LANES), F32),
            pltpu.SemaphoreType.DMA((2, parts)),
        ],
        compiler_params=pltpu.CompilerParams(vmem_limit_bytes=VMEM_LIMIT),
        cost_estimate=pl.CostEstimate(
            flops=points * 8 * LANES * 6, bytes_accessed=16 * points, transcendentals=0
        ),
        name="compress",
    )(rank, *pieces, *consts)


def azimuth_kernel(chunk, joined, x_ref, *refs):
    edges_before, refs = refs[: 2 * joined], refs[2 * joined :]
    tw_ref, fwd_ref, fwd_low_ref, out_ref, up_ref, down_ref, t_ref, mid_ref = refs
    part = pl.program_id(0)
    pieces, per_part, bins = x_ref.shape[1], x_ref.shape[4], x_ref.shape[6]

    def stage(m):
        sides = []
        for ri in range(2):
            column = jnp.concatenate([x_ref[0, a, ri, 0, m] for a in range(pieces)], axis=0)
            sides.append(split(jnp.transpose(column)))
        high = jnp.concatenate([sides[0][0], sides[1][0]], axis=1)
        low = jnp.concatenate([sides[0][1], sides[1][1]], axis=1)
        y = dot(high, fwd_ref[...]) + dot(low, fwd_ref[...]) + dot(high, fwd_low_ref[...])
        index = part * per_part + m
        at = pl.ds(CHUNKS * index + chunk, 1)
        wr, wi = tw_ref[0, at, :], tw_ref[1, at, :]
        a, b = y[:, 0:LANES], y[:, LANES : 2 * LANES]
        t_ref[index, 0] = a * wr - b * wi
        t_ref[index, 1] = a * wi + b * wr

    for m in range(per_part):
        stage(m)

    @pl.when(part == pl.num_programs(0) - 1)
    def _():
        def rest(i, carry):
            at = pl.ds(pl.multiple_of(i * STEP, STEP), STEP)

            def load(m):
                return t_ref[m, 0, at, :], t_ref[m, 1, at, :]

            def finish(k, value):
                re, im = unit(chunk * k, LANES, -1.0)
                a, b = scale_by(value, float(re), float(im))
                out_ref[k, 0, at, :] = a
                out_ref[k, 1, at, :] = b

            dft_two_step(load, mid_ref, finish, 4, PER_CHUNK // 4, -1.0)
            return carry

        lax.fori_loop(0, bins // STEP, rest, 0)

        def edges(k, carry):
            for ri in range(2):
                at = joined * PER_CHUNK + k
                up_ref[at, ri] = out_ref[k, ri, bins - HALO : bins, :]
                down_ref[at, ri] = out_ref[k, ri, 0:HALO, :]
                for before_ref, edge_ref in zip(edges_before, (up_ref, down_ref)):
                    edge_ref[k, ri] = before_ref[k, ri]
            return carry

        lax.fori_loop(0, PER_CHUNK, edges, 0)


def azimuth(x, chunk, place, before=()):
    parts, pieces, _, _, per_part, rows_in, bins = x.shape
    ids = np.arange(LANES)
    tw = jnp.asarray(np.stack(unit(ids[:, None] * ids[None, :], NAZ, -1.0)), F32)
    fwd, fwd_low = right_tables(-1.0)
    consts = [tw, jnp.asarray(fwd), jnp.asarray(fwd_low)]
    points = PER_CHUNK * LANES * bins
    shape = (PER_CHUNK, 2, bins, LANES)
    joined = len(before) // 2
    edge = ((1 + joined) * PER_CHUNK, 2, HALO, LANES)
    return pl.pallas_call(
        functools.partial(azimuth_kernel, chunk, joined),
        grid=(parts,),
        in_specs=[
            pl.BlockSpec(
                (1, pieces, 2, 1, per_part, rows_in, bins),
                lambda i: (i, 0, 0, place, 0, 0, 0),
            )
        ]
        + [whole_spec(a) for a in (*before, *consts)],
        out_specs=[pl.BlockSpec(s, lambda i: (0, 0, 0, 0)) for s in (shape, edge, edge)],
        out_shape=[jax.ShapeDtypeStruct(s, F32) for s in (shape, edge, edge)],
        scratch_shapes=[pltpu.VMEM(shape, F32), pltpu.VMEM((PER_CHUNK, 2, STEP, LANES), F32)],
        compiler_params=pltpu.CompilerParams(vmem_limit_bytes=VMEM_LIMIT),
        cost_estimate=pl.CostEstimate(
            flops=points * 8 * LANES * 3, bytes_accessed=16 * points, transcendentals=0
        ),
        name=f"azimuth{chunk}",
    )(x, *before, *consts)


KB = 4
BB = 8
QUAD = 4


def fit(fn, even):
    nodes = np.cos((2 * np.arange(64) + 1) * np.pi / 128) * 0.25
    z2 = (nodes + 0.25) / 2
    z = np.sqrt(z2)
    goal = fn(np.pi * z) if even else fn(np.pi * z) / z
    return [float(v) for v in np.polynomial.polynomial.polyfit(z2, goal, 4)]


SIN_FIT, COS_FIT = fit(np.sin, False), fit(np.cos, True)


def horner(coefficients, x):
    total = coefficients[-1]
    for c in reversed(coefficients[:-1]):
        total = total * x + c
    return total


def square_of(k2):
    f = k2 * LANES + lax.broadcasted_iota(jnp.int32, (1, LANES), 1)
    centred = jnp.where(f >= NAZ // 2, f - NAZ, f).astype(F32) * (1.0 / NAZ)
    return centred * centred


def turn(t):
    z = t - jnp.round(t)
    z2 = z * z
    s = horner(SIN_FIT, z2) * z
    c = horner(COS_FIT, z2)
    twice = s + s
    return 1.0 - twice * s, twice * c


def phase_kernel(part, rate_ref, out_ref):
    k = pl.program_id(0)
    for half in range(2):
        c, s = turn(rate_ref[...] * square_of(k + PER_CHUNK * (2 * part + half)))
        out_ref[half, 0, 0] = c
        out_ref[half, 0, 1] = s


def phase_table(rate, part):
    shape = (2, PER_CHUNK, 2, rate.shape[0], LANES)
    points = 2 * PER_CHUNK * rate.size
    return pl.pallas_call(
        functools.partial(phase_kernel, part),
        grid=(PER_CHUNK,),
        in_specs=[whole_spec(rate)],
        out_specs=pl.BlockSpec((2, 1) + shape[2:], lambda i: (0, i, 0, 0, 0)),
        out_shape=jax.ShapeDtypeStruct(shape, F32),
        compiler_params=pltpu.CompilerParams(vmem_limit_bytes=VMEM_LIMIT),
        cost_estimate=pl.CostEstimate(
            flops=40 * points, bytes_accessed=8 * points, transcendentals=0
        ),
        name="phase",
    )(rate)


def combine(sources, kk, start, put):
    at = slice(start, start + STEP)
    values = [(ref[kk, 0, at, :], ref[kk, 1, at, :]) for ref in sources]
    for q, value in enumerate(dft_list(values, -1.0)):
        for half, part in enumerate(value):
            high, low = split(part)
            put(q, slice(half * LANES, (half + 1) * LANES), high, low)


def final_kernel(steps, joins, wide, *refs):
    refs = list(refs)

    def take(count):
        taken = refs[:count]
        del refs[:count]
        return taken

    sources = take(CHUNKS) if joins else take(1)
    low_refs, high_refs = (take(CHUNKS), take(CHUNKS)) if wide else ((), ())
    phase_refs = take(1 if wide else CHUNKS // 2)
    mover_refs = take(2 if wide else 1)
    inv1_ref, inv2_ref, tw_ref = take(3)
    if not joins or wide:
        out_ref, own_ref, zr_ref, zi_ref, s_ref, swap_ref, half_ref, halo_ref = refs[-8:]
        if not joins:
            own_ref = sources[0]
    else:
        out_ref, joined_ref, own_ref, zr_ref, zi_ref, s_ref, swap_ref, half_ref, sems = refs[-9:]
    step = pl.program_id(0)
    own = own_ref.shape[2] // 2
    rows = zr_ref.shape[0]
    keeps = joins and not wide
    copies = []
    if keeps:
        copies = [
            pltpu.make_async_copy(own_ref.at[q], joined_ref.at[q], sems.at[q])
            for q in range(CHUNKS)
        ]

    def own_at(kk):
        return step * KB + kk if keeps else kk

    def first_half(block):
        base = jnp.minimum(block * BB, rows - BB)
        for j in range(BB // QUAD):
            cols = []
            for t in range(QUAD):
                at = base + QUAD * j + t
                cols.append(jnp.concatenate([zr_ref[at], zi_ref[at]], axis=0))
            hi, lo = split(jnp.concatenate(cols, axis=1))
            w = dot(inv1_ref[...], hi)
            w = w[0 : 2 * LANES] + w[2 * LANES :] + dot(inv1_ref[0 : 2 * LANES, :], lo)
            turned = []
            for t in range(QUAD):
                a = w[0:LANES, t * LANES : (t + 1) * LANES]
                b = w[LANES : 2 * LANES, t * LANES : (t + 1) * LANES]
                wr, wi = tw_ref[0], tw_ref[1]
                turned.append(jnp.concatenate([a * wr - b * wi, a * wi + b * wr], axis=1))
            hi, lo = split(jnp.concatenate(turned, axis=0))
            half_ref[j, 0] = hi
            half_ref[j, 1] = lo

    @pl.when(step < steps)
    def _():
        def one(kk, buf):
            k = step * KB + kk
            if joins:
                for start in range(0, own, STEP):

                    def put_own(q, cols, high, low, start=start):
                        own_ref[q, own_at(kk), start : start + STEP, cols] = high
                        own_ref[q, own_at(kk), own + start : own + start + STEP, cols] = low

                    combine(sources, kk, start, put_own)
            if wide:
                for side, halo_refs in enumerate((low_refs, high_refs)):
                    for start in range(0, HALO, STEP):

                        def put_halo(q, cols, high, low, at=side * HALO + start):
                            halo_ref[buf, q, at : at + STEP, cols] = high
                            halo_ref[buf, q, 2 * HALO + at : 2 * HALO + at + STEP, cols] = low

                        combine(halo_refs, kk, start, put_halo)
            for q in range(CHUNKS):
                k2 = k + PER_CHUNK * q
                band = lax.div(k2, LANES // GROUPS)
                moved = dot(mover_refs[0][band], own_ref[q, own_at(kk)])
                if wide:
                    moved = moved + dot(mover_refs[1][band], halo_ref[buf, q])
                both = moved[0:rows, :] + moved[rows : 2 * rows, :]
                if wide:
                    c, s = turn(phase_refs[0][...] * square_of(k2))
                else:
                    c, s = phase_refs[q // 2][q % 2, kk, 0], phase_refs[q // 2][q % 2, kk, 1]
                a, b = both[:, 0:LANES], both[:, LANES : 2 * LANES]
                swap_ref[buf, 0, q] = a * c + b * s
                swap_ref[buf, 1, q] = b * c - a * s
            to = pl.ds(pl.multiple_of(k * CHUNKS, CHUNKS), CHUNKS)
            for start in range(0, rows, BB):
                at = slice(start, start + BB)
                zr_ref[at, to, :] = jnp.swapaxes(swap_ref[buf, 0, :, at, :], 0, 1)
                zi_ref[at, to, :] = jnp.swapaxes(swap_ref[buf, 1, :, at, :], 0, 1)

        for kk in range(KB):
            one(kk, kk % 2)

    @pl.when(step > steps)
    def _():
        for j in range(BB // QUAD):
            image = dot_nt(inv2_ref[...], half_ref[j, 0])
            image = image[0 : 2 * LANES] + image[2 * LANES :]
            image = image + dot_nt(inv2_ref[0 : 2 * LANES, :], half_ref[j, 1])
            for t in range(QUAD):
                for ri in range(2):
                    s_ref[ri, QUAD * j + t] = image[
                        ri * LANES : (ri + 1) * LANES, t * LANES : (t + 1) * LANES
                    ]
        first_half(step - steps)
        for ri in range(2):
            for start in range(0, LANES, 8):
                lines = jnp.swapaxes(s_ref[ri, :, start : start + 8, :], 0, 1)
                for n in range(8):
                    at = (start + n) * LANES
                    out_ref[ri, :, at : at + LANES] = lines[n]

    @pl.when(step == steps)
    def _():
        for copy in copies:
            copy.start()
        first_half(0)

    @pl.when(step == pl.num_programs(0) - 1)
    def _():
        for copy in copies:
            copy.wait()


def final(bins, places, sources, lows, highs, phases, movers, image=None):
    joins, wide = len(sources) > 1, len(lows) > 0
    rows = len(places) * BB
    steps = PER_CHUNK // KB
    ids = np.arange(LANES)
    tw = jnp.asarray(np.stack(unit(ids[:, None] * ids[None, :], NAZ, 1.0)), F32)
    consts = [
        *movers,
        jnp.asarray(left_table(1.0, 1.0, ids // CHUNKS + PER_CHUNK * (ids % CHUNKS))),
        jnp.asarray(left_table(1.0, 1.0 / NAZ)),
        tw,
    ]
    start, gap_at = places[0], len(places)
    for i, place in enumerate(places):
        if place != start + i:
            gap_at = i
            break
    gap = places[-1] - start - len(places) + 1

    def early(i):
        return (jnp.minimum(i, steps - 1), 0, 0, 0)

    def early_second(i):
        return (0, jnp.minimum(i, steps - 1), 0, 0)

    def late(i):
        at = jnp.maximum(i - steps - 1, 0)
        return (0, start + at + jnp.where(at >= gap_at, gap, 0), 0)

    def halo_spec(chunk, held):
        first = (chunk - CHUNKS + held) * steps if held > 1 else 0
        return pl.BlockSpec(
            (KB, 2, HALO, LANES), lambda i: (first + jnp.minimum(i, steps - 1), 0, 0, 0)
        )

    joined = (CHUNKS, PER_CHUNK, 2 * bins, 2 * LANES)
    joined_spec = pl.BlockSpec((CHUNKS, KB, 2 * bins, 2 * LANES), early_second)
    given = [*sources, *lows, *highs, *phases, *consts]
    specs = [pl.BlockSpec((KB, 2, bins, LANES), early)] * CHUNKS if joins else [joined_spec]
    for halos in (lows, highs):
        specs += [halo_spec(i, halo.shape[0] // PER_CHUNK) for i, halo in enumerate(halos)]
    if wide:
        specs += [whole_spec(a) for a in phases]
    else:
        specs += [
            pl.BlockSpec((2, KB, 2, rows, LANES), lambda i: (0, jnp.minimum(i, steps - 1), 0, 0, 0))
        ] * len(phases)
    specs += [whole_spec(a) for a in consts]
    aliases = {}
    if image is not None:
        aliases = {len(given): 0}
        given.append(image)
        specs.append(pl.BlockSpec(memory_space=pl.ANY))
    shapes = [jax.ShapeDtypeStruct((2, bins, NAZ), F32)]
    out_specs = [pl.BlockSpec((2, BB, NAZ), late)]
    scratch = []
    if joins and wide:
        scratch.append(pltpu.VMEM((CHUNKS, KB, 2 * bins, 2 * LANES), BF16))
    elif joins:
        shapes.append(jax.ShapeDtypeStruct(joined, BF16))
        out_specs.append(pl.BlockSpec(memory_space=pl.ANY))
        scratch.append(pltpu.VMEM(joined, BF16))
    else:
        scratch.append(pltpu.VMEM((16, LANES), BF16))
    scratch += [
        pltpu.VMEM((rows, LANES, LANES), F32),
        pltpu.VMEM((rows, LANES, LANES), F32),
        pltpu.VMEM((2, BB, LANES, LANES), F32),
        pltpu.VMEM((2, 2, CHUNKS, rows, LANES), F32),
        pltpu.VMEM((BB // QUAD, 2, QUAD * LANES, 2 * LANES), BF16),
    ]
    if wide:
        scratch.append(pltpu.VMEM((2, CHUNKS, 4 * HALO, 2 * LANES), BF16))
    else:
        scratch.append(pltpu.SemaphoreType.DMA((CHUNKS,)))
    points = NAZ * rows
    return pl.pallas_call(
        functools.partial(final_kernel, steps, joins, wide),
        grid=(steps + 1 + len(places),),
        in_specs=specs,
        out_specs=out_specs,
        out_shape=shapes,
        scratch_shapes=scratch,
        input_output_aliases=aliases,
        compiler_params=pltpu.CompilerParams(vmem_limit_bytes=VMEM_LIMIT),
        cost_estimate=pl.CostEstimate(
            flops=points * 8 * LANES * 9, bytes_accessed=28 * points, transcendentals=0
        ),
        name="final_wide" if wide else "final_inner",
    )(*given)


def mover_table(rows, columns, shift_table, filter_index, tap_table):
    shift_table, filter_index = shift_table[:, rows], filter_index[:, rows]
    onehot = (filter_index[:, :, None] == jnp.arange(NFILT, dtype=jnp.int32)).astype(F32)
    weights = jnp.einsum("gbf,ft->gbt", onehot, tap_table, precision=lax.Precision.HIGHEST)
    first = rows[None, :].astype(np.int32) + shift_table + (HALO - 4)
    offset = columns.astype(np.int32)[None, None, :] - first[:, :, None]
    table = jnp.zeros(offset.shape, F32)
    for t in range(TAPS):
        table = table + jnp.where(offset == t, weights[:, :, t : t + 1], 0.0)
    high = lax.reduce_precision(table, 8, 7)
    low = table - high
    top = jnp.concatenate([high, high], axis=2)
    bottom = jnp.concatenate([low, jnp.zeros_like(low)], axis=2)
    return jnp.concatenate([top, bottom], axis=1).astype(BF16)


def own_columns(bins):
    return np.arange(HALO, HALO + bins)


def halo_columns(bins):
    return np.concatenate([np.arange(HALO), np.arange(bins + HALO, bins + 2 * HALO)])


def row_sets(bins):
    blocks = np.arange(bins // BB)
    inner = (blocks >= HALO // BB) & (blocks < (bins - HALO) // BB)
    return [blocks[chosen].tolist() for chosen in (inner, ~inner) if chosen.any()]


def bins_of(places):
    return np.concatenate([np.arange(BB) + BB * place for place in places])


def neighbours(axes, size, step):
    return [(i, i + step) for i in range(size) if 0 <= i + step < size]


def local(nrng, naz, raw_echo, chirp_spectrum, azimuth_rate, shift_table, filter_index, tap_table):
    axes = ("rng", "az")
    devices = nrng * naz
    bins = NRG // devices
    rows_in = raw_echo.shape[1] // LANES
    per_part = PER_CHUNK // nrng
    chirp = chirp_spectrum.reshape(2, LANES, RG1).transpose(0, 2, 1)
    rate = jnp.broadcast_to((azimuth_rate * 0.5)[:, None], (bins, LANES))
    rank = lax.axis_index("rng").astype(jnp.int32).reshape(1)
    packed = pack(raw_echo, rank, nrng, GROUPED[:1]) + pack(raw_echo, rank, nrng, GROUPED[1:])
    mains, lows, highs = [None] * CHUNKS, [None] * CHUNKS, [None] * CHUNKS
    turned, edges = [], []

    def gather(g):
        return [packed[g][0]] + [
            lax.ppermute(packed[g][j], "rng", [(i, i ^ j) for i in range(nrng)])
            for j in range(1, nrng)
        ]

    def transform(g):
        for place, c in enumerate(GROUPED[g]):
            if c > 0:
                turned[g], mains[c - 1] = lax.optimization_barrier((turned[g], mains[c - 1]))
            mains[c], up, down = azimuth(turned[g], c, place, edges if c == CHUNKS - 1 else ())
            if c == CHUNKS - 2:
                edges.extend([up, down])
                continue
            lows[c] = lax.ppermute(up, axes, neighbours(axes, devices, 1))
            highs[c] = lax.ppermute(down, axes, neighbours(axes, devices, -1))

    places = row_sets(bins)
    rates = [rate[bins_of(p)] for p in places]
    inner_rate = rates[0]
    phases = []
    got = [gather(0)]
    packed[1], got[0] = lax.optimization_barrier((packed[1], got[0]))
    got.append(gather(1))
    count = len(GROUPED)
    for g, chunks in enumerate(GROUPED):
        lines = compress(got[g], rank, chirp)
        if g + 1 < count:
            lines, got[g + 1] = lax.optimization_barrier((lines, got[g + 1]))
        if g + 2 < count:
            packed[g + 2], got[g + 1] = lax.optimization_barrier((packed[g + 2], got[g + 1]))
            if g >= 1:
                held = (packed[g + 2], turned[g - 1])
                packed[g + 2], turned[g - 1] = lax.optimization_barrier(held)
            got.append(gather(g + 2))
        if g >= 2:
            transform(g - 2)
            for c in GROUPED[g - 2]:
                lines, mains[c] = lax.optimization_barrier((lines, mains[c]))
        if g >= 3:
            for c in GROUPED[g - 3]:
                held = (lines, lows[c], highs[c])
                lines, lows[c], highs[c] = lax.optimization_barrier(held)
        if 2 <= g and len(places) > 1 and len(phases) < CHUNKS // 2:
            inner_rate, turned[g - 2] = lax.optimization_barrier((inner_rate, turned[g - 2]))
            table = phase_table(inner_rate, len(phases))
            lines, table = lax.optimization_barrier((lines, table))
            phases.append(table)
        if bins < LANES:
            cut = lines.reshape(RG1, 2, -1, LANES // bins, bins)
            lines = cut.transpose(0, 3, 1, 2, 4).reshape(devices, 2, -1, bins)
        moved = lax.all_to_all(lines, axes, split_axis=0, concat_axis=0, tiled=True)
        turned.append(moved.reshape(nrng, naz, 2, len(chunks), per_part, rows_in, bins))
    transform(count - 2)
    transform(count - 1)
    lows[-2], highs[-2] = lows[-1], highs[-1]
    tables = (shift_table, filter_index, tap_table)
    image, sources = None, mains
    for i, places_of in enumerate(places):
        ids = bins_of(places_of)
        wide = i == len(places) - 1
        halos = (lows, highs) if wide else ([], [])
        columns = [own_columns(bins), halo_columns(bins)] if wide else [own_columns(bins)]
        movers = [mover_table(ids, cols, *tables) for cols in columns]
        result = final(
            bins, places_of, sources, *halos, [rates[i]] if wide else phases, movers, image
        )
        image, sources = result[0], result[1:]
    return image


def solution(mesh):
    return jax.shard_map(
        functools.partial(local, mesh.shape["rng"], mesh.shape["az"]),
        mesh=mesh,
        in_specs=(
            P(None, "az", "rng"),
            P(),
            P(("rng", "az")),
            P(None, ("rng", "az")),
            P(None, ("rng", "az")),
            P(),
        ),
        out_specs=P(None, ("rng", "az"), None),
        check_vma=False,
    )
```

```python
import functools

import jax
import jax.numpy as jnp
import ml_dtypes
import numpy as np
from jax import lax
from jax.experimental import pallas as pl
from jax.experimental.pallas import tpu as pltpu
from jax.sharding import PartitionSpec as P

NRG = 4096
NAZ = 16384
GROUPS = 16
NFILT = 16
TAPS = 8
HALO = 32
LANES = 128
RG1 = NRG // LANES
CHUNKS = 8
PER_CHUNK = LANES // CHUNKS
GROUPED = tuple((c,) for c in range(CHUNKS))
VMEM_LIMIT = 60 << 20
BF16 = jnp.bfloat16
F32 = jnp.float32


def split_np(table):
    table = np.asarray(table, np.float32)
    high = table.astype(ml_dtypes.bfloat16)
    low = (table - high.astype(np.float32)).astype(ml_dtypes.bfloat16)
    return high, low


def unit(angle_num, period, sign):
    angles = (np.asarray(angle_num, np.int64) % period) * (2.0 * np.pi / period)
    return np.cos(angles), sign * np.sin(angles)


def dft_matrix(sign):
    ids = np.arange(LANES)
    return unit(ids[:, None] * ids[None, :], LANES, sign)


def right_tables(sign, scale=1.0):
    c, s = dft_matrix(sign)
    return split_np(np.block([[c, s], [-s, c]]) * scale)


def left_table(sign, scale=1.0, order=np.arange(LANES)):
    c, s = (part[:, order] for part in dft_matrix(sign))
    high, low = split_np(np.block([[c, -s], [s, c]]) * scale)
    return np.concatenate([high, low], axis=0)


def split(x):
    high = x.astype(BF16)
    low = (x - high.astype(F32)).astype(BF16)
    return high, low


def dot(a, b):
    return jnp.dot(a, b, preferred_element_type=F32)


def dot_nt(a, b):
    return lax.dot_general(a, b, (((1,), (1,)), ((), ())), preferred_element_type=F32)


def scale_by(value, re, im):
    a, b = value
    eps = 1e-12
    if abs(im) < eps:
        if abs(re - 1.0) < eps:
            return value
        if abs(re + 1.0) < eps:
            return -a, -b
    if abs(re) < eps:
        if abs(im - 1.0) < eps:
            return -b, a
        if abs(im + 1.0) < eps:
            return b, -a
    if abs(abs(re) - abs(im)) < eps:
        sr, si = (1.0 if re > 0 else -1.0), (1.0 if im > 0 else -1.0)
        h = abs(re)
        total, diff = (a + b) * h, (a - b) * h
        if si == sr:
            return (diff, total) if sr > 0 else (-diff, -total)
        return (total, -diff) if sr > 0 else (-total, diff)
    re, im = float(re), float(im)
    return a * re - b * im, a * im + b * re


def dft_list(values, sign):
    count = len(values)
    if count == 1:
        return values
    even, odd = dft_list(values[0::2], sign), dft_list(values[1::2], sign)
    first, second = [], []
    for k in range(count // 2):
        re, im = unit(k, count, sign)
        a, b = even[k], scale_by(odd[k], float(re), float(im))
        first.append((a[0] + b[0], a[1] + b[1]))
        second.append((a[0] - b[0], a[1] - b[1]))
    return first + second


def dft_two_step(load, mid_ref, finish, outer, inner, sign):
    for ib in range(inner):
        column = dft_list([load(ia * inner + ib) for ia in range(outer)], sign)
        for ka in range(outer):
            re, im = unit(ib * ka, outer * inner, sign)
            a, b = scale_by(column[ka], float(re), float(im))
            mid_ref[ka * inner + ib, 0] = a
            mid_ref[ka * inner + ib, 1] = b
    for ka in range(outer):
        row = [(mid_ref[ka * inner + ib, 0], mid_ref[ka * inner + ib, 1]) for ib in range(inner)]
        for kb, value in enumerate(dft_list(row, sign)):
            finish(ka + outer * kb, value)


def pack_kernel(groups, parts, per_part, rows_in, rank_ref, x_ref, *out_refs):
    rank = rank_ref[0]
    for j in range(parts):
        part = jnp.bitwise_xor(rank, j)
        for g, chunks in enumerate(groups):
            for at, c in enumerate(chunks):
                for m in range(per_part):
                    start = CHUNKS * (part * per_part + m) + c
                    to = (at * per_part + m) * rows_in
                    for ri in range(2):
                        out_refs[g * parts + j][ri, 0, to : to + rows_in, :] = x_ref[
                            ri, pl.ds(start, rows_in, stride=LANES), :
                        ]


def pack(raw, rank, parts, groups):
    lines, bins = raw.shape[1], raw.shape[2]
    rows_in, tiles, per_part = lines // LANES, bins // LANES, PER_CHUNK // parts
    heights = [len(chunks) * per_part * rows_in for chunks in groups for _ in range(parts)]
    flat = pl.pallas_call(
        functools.partial(pack_kernel, groups, parts, per_part, rows_in),
        grid=(tiles,),
        in_specs=[
            pl.BlockSpec(memory_space=pltpu.SMEM),
            pl.BlockSpec((2, lines, LANES), lambda i: (0, 0, i)),
        ],
        out_specs=[pl.BlockSpec((2, 1, rows, LANES), lambda i: (0, i, 0, 0)) for rows in heights],
        out_shape=[jax.ShapeDtypeStruct((2, tiles, rows, LANES), F32) for rows in heights],
        compiler_params=pltpu.CompilerParams(vmem_limit_bytes=VMEM_LIMIT),
        cost_estimate=pl.CostEstimate(flops=0, bytes_accessed=16 * lines * bins, transcendentals=0),
        name="pack",
    )(rank, raw)
    return [flat[i * parts : (i + 1) * parts] for i in range(len(groups))]


STEP = 16


def compress_kernel(parts, rows, rank_ref, *refs):
    x_refs = refs[:parts]
    chirp_ref, tw_ref, fwd_ref, fwd_low_ref, inv_ref, inv_low_ref = refs[parts : parts + 6]
    out_ref, buf_ref, lhs_ref, y_ref, mid_ref, sems = refs[parts + 6 :]
    tiles = buf_ref.shape[3]
    rank = rank_ref[0]
    step = pl.program_id(0)
    slot = lax.rem(step, 2)

    def copies(at, to):
        return [
            pltpu.make_async_copy(
                x_refs[j].at[:, :, pl.ds(pl.multiple_of(at * rows, rows), rows), :],
                buf_ref.at[to, jnp.bitwise_xor(rank, j)],
                sems.at[to, j],
            )
            for j in range(parts)
        ]

    @pl.when(step == 0)
    def _():
        for copy in copies(step, slot):
            copy.start()

    @pl.when(step + 1 < pl.num_programs(0))
    def _():
        for copy in copies(step + 1, 1 - slot):
            copy.start()

    for copy in copies(step, slot):
        copy.wait()

    def put(at, re, im):
        for half, part in enumerate((re, im)):
            high, low = split(part)
            lhs_ref[at, half * LANES : (half + 1) * LANES] = high
            lhs_ref[at, (2 + half) * LANES : (3 + half) * LANES] = low

    def forward(i, carry):
        at = pl.ds(pl.multiple_of(i * STEP, STEP), STEP)

        def load(p):
            source = buf_ref.at[slot, p // tiles]
            return source[0, p % tiles, at, :], source[1, p % tiles, at, :]

        def finish(k, value):
            wr, wi = tw_ref[0, k : k + 1, :], tw_ref[1, k : k + 1, :]
            a, b = value
            put(
                pl.ds(pl.multiple_of(k * rows + i * STEP, STEP), STEP),
                a * wr - b * wi,
                a * wi + b * wr,
            )

        dft_two_step(load, mid_ref, finish, 4, RG1 // 4, -1.0)
        return carry

    lax.fori_loop(0, rows // STEP, forward, 0)

    group = max(1, 2 * LANES // rows)

    def middle(i, carry):
        at = pl.ds(pl.multiple_of(i * group * rows, group * rows), group * rows)
        y = dot(lhs_ref[at, :], fwd_ref[...]) + dot(lhs_ref[at, 0 : 2 * LANES], fwd_low_ref[...])
        for s in range(group):
            k = i * group + s
            cr, ci = chirp_ref[0, pl.ds(k, 1), :], chirp_ref[1, pl.ds(k, 1), :]
            a = y[s * rows : (s + 1) * rows, 0:LANES]
            b = y[s * rows : (s + 1) * rows, LANES : 2 * LANES]
            put(pl.ds(pl.multiple_of(k * rows, rows), rows), a * cr - b * ci, a * ci + b * cr)
        z = dot(lhs_ref[at, :], inv_ref[...]) + dot(lhs_ref[at, 0 : 2 * LANES], inv_low_ref[...])
        for s in range(group):
            k = i * group + s
            wr, wi = tw_ref[0, pl.ds(k, 1), :], tw_ref[1, pl.ds(k, 1), :]
            a = z[s * rows : (s + 1) * rows, 0:LANES]
            b = z[s * rows : (s + 1) * rows, LANES : 2 * LANES]
            y_ref[k, 0] = a * wr + b * wi
            y_ref[k, 1] = b * wr - a * wi
        return carry

    lax.fori_loop(0, RG1 // group, middle, 0)

    def backward(i, carry):
        at = pl.ds(pl.multiple_of(i * STEP, STEP), STEP)

        def load(k):
            return y_ref[k, 0, at, :], y_ref[k, 1, at, :]

        def finish(p, value):
            out_ref[p, 0, at, :] = value[0]
            out_ref[p, 1, at, :] = value[1]

        dft_two_step(load, mid_ref, finish, 4, RG1 // 4, 1.0)
        return carry

    lax.fori_loop(0, rows // STEP, backward, 0)


def whole_spec(array):
    zeros = (0,) * array.ndim
    return pl.BlockSpec(array.shape, lambda *_: zeros)


def compress(pieces, rank, chirp):
    parts = len(pieces)
    _, tiles, rows, _ = pieces[0].shape
    block = min(rows, 64)
    ids = np.arange(RG1)[:, None] * np.arange(LANES)[None, :]
    tw = jnp.asarray(np.stack(unit(ids, NRG, -1.0)), F32)
    fwd, fwd_low = right_tables(-1.0)
    inv, inv_low = right_tables(1.0, 1.0 / NRG)
    consts = [
        chirp,
        tw,
        jnp.asarray(np.concatenate([fwd, fwd])),
        jnp.asarray(fwd_low),
        jnp.asarray(np.concatenate([inv, inv])),
        jnp.asarray(inv_low),
    ]
    points = rows * NRG
    return pl.pallas_call(
        functools.partial(compress_kernel, parts, block),
        grid=(rows // block,),
        in_specs=[pl.BlockSpec(memory_space=pltpu.SMEM)]
        + [pl.BlockSpec(memory_space=pl.ANY)] * parts
        + [whole_spec(a) for a in consts],
        out_specs=pl.BlockSpec((RG1, 2, block, LANES), lambda i: (0, 0, i, 0)),
        out_shape=jax.ShapeDtypeStruct((RG1, 2, rows, LANES), F32),
        scratch_shapes=[
            pltpu.VMEM((2, parts, 2, tiles, block, LANES), F32),
            pltpu.VMEM((RG1 * block, 4 * LANES), BF16),
            pltpu.VMEM((RG1, 2, block, LANES), F32),
            pltpu.VMEM((RG1, 2, STEP, LANES), F32),
            pltpu.SemaphoreType.DMA((2, parts)),
        ],
        compiler_params=pltpu.CompilerParams(vmem_limit_bytes=VMEM_LIMIT),
        cost_estimate=pl.CostEstimate(
            flops=points * 8 * LANES * 6, bytes_accessed=16 * points, transcendentals=0
        ),
        name="compress",
    )(rank, *pieces, *consts)


def azimuth_kernel(chunk, joined, x_ref, *refs):
    edges_before, refs = refs[: 2 * joined], refs[2 * joined :]
    tw_ref, fwd_ref, fwd_low_ref, out_ref, up_ref, down_ref, t_ref, mid_ref = refs
    part = pl.program_id(0)
    pieces, per_part, bins = x_ref.shape[1], x_ref.shape[4], x_ref.shape[6]

    def stage(m):
        sides = []
        for ri in range(2):
            column = jnp.concatenate([x_ref[0, a, ri, 0, m] for a in range(pieces)], axis=0)
            sides.append(split(jnp.transpose(column)))
        high = jnp.concatenate([sides[0][0], sides[1][0]], axis=1)
        low = jnp.concatenate([sides[0][1], sides[1][1]], axis=1)
        y = dot(high, fwd_ref[...]) + dot(low, fwd_ref[...]) + dot(high, fwd_low_ref[...])
        index = part * per_part + m
        at = pl.ds(CHUNKS * index + chunk, 1)
        wr, wi = tw_ref[0, at, :], tw_ref[1, at, :]
        a, b = y[:, 0:LANES], y[:, LANES : 2 * LANES]
        t_ref[index, 0] = a * wr - b * wi
        t_ref[index, 1] = a * wi + b * wr

    for m in range(per_part):
        stage(m)

    @pl.when(part == pl.num_programs(0) - 1)
    def _():
        def rest(i, carry):
            at = pl.ds(pl.multiple_of(i * STEP, STEP), STEP)

            def load(m):
                return t_ref[m, 0, at, :], t_ref[m, 1, at, :]

            def finish(k, value):
                re, im = unit(chunk * k, LANES, -1.0)
                a, b = scale_by(value, float(re), float(im))
                out_ref[k, 0, at, :] = a
                out_ref[k, 1, at, :] = b

            dft_two_step(load, mid_ref, finish, 4, PER_CHUNK // 4, -1.0)
            return carry

        lax.fori_loop(0, bins // STEP, rest, 0)

        def edges(k, carry):
            for ri in range(2):
                at = joined * PER_CHUNK + k
                up_ref[at, ri] = out_ref[k, ri, bins - HALO : bins, :]
                down_ref[at, ri] = out_ref[k, ri, 0:HALO, :]
                for i in range(joined):
                    up_ref[i * PER_CHUNK + k, ri] = edges_before[2 * i][k, ri]
                    down_ref[i * PER_CHUNK + k, ri] = edges_before[2 * i + 1][k, ri]
            return carry

        lax.fori_loop(0, PER_CHUNK, edges, 0)


def azimuth(x, chunk, place, before=()):
    parts, pieces, _, _, per_part, rows_in, bins = x.shape
    ids = np.arange(LANES)
    tw = jnp.asarray(np.stack(unit(ids[:, None] * ids[None, :], NAZ, -1.0)), F32)
    fwd, fwd_low = right_tables(-1.0)
    consts = [tw, jnp.asarray(fwd), jnp.asarray(fwd_low)]
    points = PER_CHUNK * LANES * bins
    shape = (PER_CHUNK, 2, bins, LANES)
    joined = len(before) // 2
    edge = ((1 + joined) * PER_CHUNK, 2, HALO, LANES)
    return pl.pallas_call(
        functools.partial(azimuth_kernel, chunk, joined),
        grid=(parts,),
        in_specs=[
            pl.BlockSpec(
                (1, pieces, 2, 1, per_part, rows_in, bins),
                lambda i: (i, 0, 0, place, 0, 0, 0),
            )
        ]
        + [whole_spec(a) for a in (*before, *consts)],
        out_specs=[pl.BlockSpec(s, lambda i: (0, 0, 0, 0)) for s in (shape, edge, edge)],
        out_shape=[jax.ShapeDtypeStruct(s, F32) for s in (shape, edge, edge)],
        scratch_shapes=[pltpu.VMEM(shape, F32), pltpu.VMEM((PER_CHUNK, 2, STEP, LANES), F32)],
        compiler_params=pltpu.CompilerParams(vmem_limit_bytes=VMEM_LIMIT),
        cost_estimate=pl.CostEstimate(
            flops=points * 8 * LANES * 3, bytes_accessed=16 * points, transcendentals=0
        ),
        name=f"azimuth{chunk}",
    )(x, *before, *consts)


KB = 4
BB = 16
QUAD = 4


def fit(fn, even):
    nodes = np.cos((2 * np.arange(64) + 1) * np.pi / 128) * 0.25
    z2 = (nodes + 0.25) / 2
    z = np.sqrt(z2)
    goal = fn(np.pi * z) if even else fn(np.pi * z) / z
    return [float(v) for v in np.polynomial.polynomial.polyfit(z2, goal, 4)]


SIN_FIT, COS_FIT = fit(np.sin, False), fit(np.cos, True)


def horner(coefficients, x):
    total = coefficients[-1]
    for c in reversed(coefficients[:-1]):
        total = total * x + c
    return total


def square_of(k2):
    f = k2 * LANES + lax.broadcasted_iota(jnp.int32, (1, LANES), 1)
    centred = jnp.where(f >= NAZ // 2, f - NAZ, f).astype(F32) * (1.0 / NAZ)
    return centred * centred


def turn(t):
    z = t - jnp.round(t)
    z2 = z * z
    s = horner(SIN_FIT, z2) * z
    c = horner(COS_FIT, z2)
    twice = s + s
    return 1.0 - twice * s, twice * c


def phase_kernel(part, rate_ref, out_ref):
    k = pl.program_id(0)
    for half in range(2):
        c, s = turn(rate_ref[...] * square_of(k + PER_CHUNK * (2 * part + half)))
        out_ref[half, 0, 0] = c
        out_ref[half, 0, 1] = s


def phase_table(rate, part):
    shape = (2, PER_CHUNK, 2, rate.shape[0], LANES)
    points = 2 * PER_CHUNK * rate.size
    return pl.pallas_call(
        functools.partial(phase_kernel, part),
        grid=(PER_CHUNK,),
        in_specs=[whole_spec(rate)],
        out_specs=pl.BlockSpec((2, 1) + shape[2:], lambda i: (0, i, 0, 0, 0)),
        out_shape=jax.ShapeDtypeStruct(shape, F32),
        compiler_params=pltpu.CompilerParams(vmem_limit_bytes=VMEM_LIMIT),
        cost_estimate=pl.CostEstimate(
            flops=40 * points, bytes_accessed=8 * points, transcendentals=0
        ),
        name="phase",
    )(rate)


def combine(sources, kk, start, put):
    at = slice(start, start + STEP)
    values = [(ref[kk, 0, at, :], ref[kk, 1, at, :]) for ref in sources]
    for q, value in enumerate(dft_list(values, -1.0)):
        for half, part in enumerate(value):
            high, low = split(part)
            put(q, slice(half * LANES, (half + 1) * LANES), high, low)


def final_kernel(steps, joins, wide, *refs):
    refs = list(refs)

    def take(count):
        taken = refs[:count]
        del refs[:count]
        return taken

    sources = take(CHUNKS) if joins else take(1)
    low_refs, high_refs = (take(CHUNKS), take(CHUNKS)) if wide else ((), ())
    phase_refs = take(1 if wide else CHUNKS // 2)
    mover_refs = take(2 if wide else 1)
    inv1_ref, inv2_ref, tw_ref = take(3)
    if not joins or wide:
        out_ref, own_ref, zr_ref, zi_ref, s_ref, swap_ref, half_ref, halo_ref = refs[-8:]
        if not joins:
            own_ref = sources[0]
    else:
        out_ref, joined_ref, own_ref, zr_ref, zi_ref, s_ref, swap_ref, half_ref, sems = refs[-9:]
    step = pl.program_id(0)
    own = own_ref.shape[2] // 2
    rows = zr_ref.shape[0]
    keeps = joins and not wide
    copies = []
    if keeps:
        copies = [
            pltpu.make_async_copy(own_ref.at[q], joined_ref.at[q], sems.at[q])
            for q in range(CHUNKS)
        ]

    def own_at(kk):
        return step * KB + kk if keeps else kk

    def first_half(block):
        base = block * BB
        for j in range(BB // QUAD):
            cols = []
            for t in range(QUAD):
                at = base + QUAD * j + t
                cols.append(jnp.concatenate([zr_ref[at], zi_ref[at]], axis=0))
            hi, lo = split(jnp.concatenate(cols, axis=1))
            w = dot(inv1_ref[...], hi)
            w = w[0 : 2 * LANES] + w[2 * LANES :] + dot(inv1_ref[0 : 2 * LANES, :], lo)
            turned = []
            for t in range(QUAD):
                a = w[0:LANES, t * LANES : (t + 1) * LANES]
                b = w[LANES : 2 * LANES, t * LANES : (t + 1) * LANES]
                wr, wi = tw_ref[0], tw_ref[1]
                turned.append(jnp.concatenate([a * wr - b * wi, a * wi + b * wr], axis=1))
            hi, lo = split(jnp.concatenate(turned, axis=0))
            half_ref[j, 0] = hi
            half_ref[j, 1] = lo

    @pl.when(step < steps)
    def _():
        def one(kk, buf):
            k = step * KB + kk
            if joins:
                for start in range(0, own, STEP):

                    def put_own(q, cols, high, low, start=start):
                        own_ref[q, own_at(kk), start : start + STEP, cols] = high
                        own_ref[q, own_at(kk), own + start : own + start + STEP, cols] = low

                    combine(sources, kk, start, put_own)
            if wide:
                for side, halo_refs in enumerate((low_refs, high_refs)):
                    for start in range(0, HALO, STEP):

                        def put_halo(q, cols, high, low, at=side * HALO + start):
                            halo_ref[buf, q, at : at + STEP, cols] = high
                            halo_ref[buf, q, 2 * HALO + at : 2 * HALO + at + STEP, cols] = low

                        combine(halo_refs, kk, start, put_halo)
            for q in range(CHUNKS):
                k2 = k + PER_CHUNK * q
                band = lax.div(k2, LANES // GROUPS)
                moved = dot(mover_refs[0][band], own_ref[q, own_at(kk)])
                if wide:
                    moved = moved + dot(mover_refs[1][band], halo_ref[buf, q])
                both = moved[0:rows, :] + moved[rows : 2 * rows, :]
                if wide:
                    c, s = turn(phase_refs[0][...] * square_of(k2))
                else:
                    c, s = phase_refs[q // 2][q % 2, kk, 0], phase_refs[q // 2][q % 2, kk, 1]
                a, b = both[:, 0:LANES], both[:, LANES : 2 * LANES]
                swap_ref[buf, 0, q] = a * c + b * s
                swap_ref[buf, 1, q] = b * c - a * s
            to = pl.ds(pl.multiple_of(k * CHUNKS, CHUNKS), CHUNKS)
            for start in range(0, rows, BB):
                at = slice(start, start + BB)
                zr_ref[at, to, :] = jnp.swapaxes(swap_ref[buf, 0, :, at, :], 0, 1)
                zi_ref[at, to, :] = jnp.swapaxes(swap_ref[buf, 1, :, at, :], 0, 1)

        for kk in range(KB):
            one(kk, kk % 2)

    def second_half():
        for j in range(BB // QUAD):
            image = dot_nt(inv2_ref[...], half_ref[j, 0])
            image = image[0 : 2 * LANES] + image[2 * LANES :]
            image = image + dot_nt(inv2_ref[0 : 2 * LANES, :], half_ref[j, 1])
            for t in range(QUAD):
                for ri in range(2):
                    s_ref[ri, QUAD * j + t] = image[
                        ri * LANES : (ri + 1) * LANES, t * LANES : (t + 1) * LANES
                    ]

    def write():
        for ri in range(2):
            for start in range(0, LANES, 8):
                lines = jnp.swapaxes(s_ref[ri, :, start : start + 8, :], 0, 1)
                for n in range(8):
                    at = (start + n) * LANES
                    out_ref[ri, :, at : at + LANES] = lines[n]

    last = pl.num_programs(0) - 1

    @pl.when((step > steps) & (step < last))
    def _():
        second_half()
        first_half(step - steps)
        write()

    @pl.when(step == last)
    def _():
        second_half()
        write()

    @pl.when(step == steps)
    def _():
        for copy in copies:
            copy.start()
        first_half(0)

    @pl.when(step == pl.num_programs(0) - 1)
    def _():
        for copy in copies:
            copy.wait()


def final(bins, places, sources, lows, highs, phases, movers, image=None):
    joins, wide = len(sources) > 1, len(lows) > 0
    rows = len(places) * BB
    steps = PER_CHUNK // KB
    ids = np.arange(LANES)
    tw = jnp.asarray(np.stack(unit(ids[:, None] * ids[None, :], NAZ, 1.0)), F32)
    consts = [
        *movers,
        jnp.asarray(left_table(1.0, 1.0, ids // CHUNKS + PER_CHUNK * (ids % CHUNKS))),
        jnp.asarray(left_table(1.0, 1.0 / NAZ)),
        tw,
    ]
    start, gap_at = places[0], len(places)
    for i, place in enumerate(places):
        if place != start + i:
            gap_at = i
            break
    gap = places[-1] - start - len(places) + 1

    def early(i):
        return (jnp.minimum(i, steps - 1), 0, 0, 0)

    def early_second(i):
        return (0, jnp.minimum(i, steps - 1), 0, 0)

    def late(i):
        at = jnp.maximum(i - steps - 1, 0)
        return (0, start + at + jnp.where(at >= gap_at, gap, 0), 0)

    def halo_spec(chunk, held):
        first = (chunk - CHUNKS + held) * steps if held > 1 else 0
        return pl.BlockSpec(
            (KB, 2, HALO, LANES), lambda i: (first + jnp.minimum(i, steps - 1), 0, 0, 0)
        )

    joined = (CHUNKS, PER_CHUNK, 2 * bins, 2 * LANES)
    joined_spec = pl.BlockSpec((CHUNKS, KB, 2 * bins, 2 * LANES), early_second)
    given = [*sources, *lows, *highs, *phases, *consts]
    specs = [pl.BlockSpec((KB, 2, bins, LANES), early)] * CHUNKS if joins else [joined_spec]
    for halos in (lows, highs):
        specs += [halo_spec(i, halo.shape[0] // PER_CHUNK) for i, halo in enumerate(halos)]
    if wide:
        specs += [whole_spec(a) for a in phases]
    else:
        specs += [
            pl.BlockSpec((2, KB, 2, rows, LANES), lambda i: (0, jnp.minimum(i, steps - 1), 0, 0, 0))
        ] * len(phases)
    specs += [whole_spec(a) for a in consts]
    aliases = {}
    if image is not None:
        aliases = {len(given): 0}
        given.append(image)
        specs.append(pl.BlockSpec(memory_space=pl.ANY))
    shapes = [jax.ShapeDtypeStruct((2, bins, NAZ), F32)]
    out_specs = [pl.BlockSpec((2, BB, NAZ), late)]
    scratch = []
    if joins and wide:
        scratch.append(pltpu.VMEM((CHUNKS, KB, 2 * bins, 2 * LANES), BF16))
    elif joins:
        shapes.append(jax.ShapeDtypeStruct(joined, BF16))
        out_specs.append(pl.BlockSpec(memory_space=pl.ANY))
        scratch.append(pltpu.VMEM(joined, BF16))
    else:
        scratch.append(pltpu.VMEM((16, LANES), BF16))
    scratch += [
        pltpu.VMEM((rows, LANES, LANES), F32),
        pltpu.VMEM((rows, LANES, LANES), F32),
        pltpu.VMEM((2, BB, LANES, LANES), F32),
        pltpu.VMEM((2, 2, CHUNKS, rows, LANES), F32),
        pltpu.VMEM((BB // QUAD, 2, QUAD * LANES, 2 * LANES), BF16),
    ]
    if wide:
        scratch.append(pltpu.VMEM((2, CHUNKS, 4 * HALO, 2 * LANES), BF16))
    else:
        scratch.append(pltpu.SemaphoreType.DMA((CHUNKS,)))
    points = NAZ * rows
    return pl.pallas_call(
        functools.partial(final_kernel, steps, joins, wide),
        grid=(steps + 1 + len(places),),
        in_specs=specs,
        out_specs=out_specs,
        out_shape=shapes,
        scratch_shapes=scratch,
        input_output_aliases=aliases,
        compiler_params=pltpu.CompilerParams(vmem_limit_bytes=VMEM_LIMIT),
        cost_estimate=pl.CostEstimate(
            flops=points * 8 * LANES * 9, bytes_accessed=28 * points, transcendentals=0
        ),
        name="final_wide" if wide else "final_inner",
    )(*given)


def mover_table(rows, columns, shift_table, filter_index, tap_table):
    shift_table, filter_index = shift_table[:, rows], filter_index[:, rows]
    onehot = (filter_index[:, :, None] == jnp.arange(NFILT, dtype=jnp.int32)).astype(F32)
    weights = jnp.einsum("gbf,ft->gbt", onehot, tap_table, precision=lax.Precision.HIGHEST)
    first = rows[None, :].astype(np.int32) + shift_table + (HALO - 4)
    offset = columns.astype(np.int32)[None, None, :] - first[:, :, None]
    table = jnp.zeros(offset.shape, F32)
    for t in range(TAPS):
        table = table + jnp.where(offset == t, weights[:, :, t : t + 1], 0.0)
    high = lax.reduce_precision(table, 8, 7)
    low = table - high
    top = jnp.concatenate([high, high], axis=2)
    bottom = jnp.concatenate([low, jnp.zeros_like(low)], axis=2)
    return jnp.concatenate([top, bottom], axis=1).astype(BF16)


def own_columns(bins):
    return np.arange(HALO, HALO + bins)


def halo_columns(bins):
    return np.concatenate([np.arange(HALO), np.arange(bins + HALO, bins + 2 * HALO)])


def row_sets(bins):
    blocks = np.arange(bins // BB)
    inner = (blocks >= HALO // BB) & (blocks < (bins - HALO) // BB)
    return [blocks[chosen].tolist() for chosen in (inner, ~inner) if chosen.any()]


def bins_of(places):
    return np.concatenate([np.arange(BB) + BB * place for place in places])


def neighbours(axes, size, step):
    return [(i, i + step) for i in range(size) if 0 <= i + step < size]


def local(nrng, naz, raw_echo, chirp_spectrum, azimuth_rate, shift_table, filter_index, tap_table):
    axes = ("rng", "az")
    devices = nrng * naz
    bins = NRG // devices
    rows_in = raw_echo.shape[1] // LANES
    per_part = PER_CHUNK // nrng
    chirp = chirp_spectrum.reshape(2, LANES, RG1).transpose(0, 2, 1)
    rate = jnp.broadcast_to((azimuth_rate * 0.5)[:, None], (bins, LANES))
    rank = lax.axis_index("rng").astype(jnp.int32).reshape(1)
    packed = pack(raw_echo, rank, nrng, GROUPED[:1]) + pack(raw_echo, rank, nrng, GROUPED[1:])
    mains, lows, highs = [None] * CHUNKS, [None] * CHUNKS, [None] * CHUNKS
    turned, edges = [], []

    def gather(g):
        return [packed[g][0]] + [
            lax.ppermute(packed[g][j], "rng", [(i, i ^ j) for i in range(nrng)])
            for j in range(1, nrng)
        ]

    def transform(g):
        for place, c in enumerate(GROUPED[g]):
            if c > 0:
                turned[g], mains[c - 1] = lax.optimization_barrier((turned[g], mains[c - 1]))
            mains[c], up, down = azimuth(turned[g], c, place, edges if c == CHUNKS - 1 else ())
            if CHUNKS - 3 <= c < CHUNKS - 1:
                edges.extend([up, down])
                continue
            lows[c] = lax.ppermute(up, axes, neighbours(axes, devices, 1))
            highs[c] = lax.ppermute(down, axes, neighbours(axes, devices, -1))

    places = row_sets(bins)
    rates = [rate[bins_of(p)] for p in places]
    inner_rate = rates[0]
    phases = []
    got = [gather(0)]
    packed[1], got[0] = lax.optimization_barrier((packed[1], got[0]))
    got.append(gather(1))
    count = len(GROUPED)
    for g, chunks in enumerate(GROUPED):
        lines = compress(got[g], rank, chirp)
        if g + 1 < count:
            lines, got[g + 1] = lax.optimization_barrier((lines, got[g + 1]))
        if g + 2 < count:
            packed[g + 2], got[g + 1] = lax.optimization_barrier((packed[g + 2], got[g + 1]))
            if g >= 1:
                held = (packed[g + 2], turned[g - 1])
                packed[g + 2], turned[g - 1] = lax.optimization_barrier(held)
            got.append(gather(g + 2))
        if g >= 2:
            transform(g - 2)
            for c in GROUPED[g - 2]:
                lines, mains[c] = lax.optimization_barrier((lines, mains[c]))
        if g >= 3:
            for c in GROUPED[g - 3]:
                held = (lines, lows[c], highs[c])
                lines, lows[c], highs[c] = lax.optimization_barrier(held)
        if 2 <= g and len(places) > 1 and len(phases) < CHUNKS // 2:
            inner_rate, turned[g - 2] = lax.optimization_barrier((inner_rate, turned[g - 2]))
            table = phase_table(inner_rate, len(phases))
            lines, table = lax.optimization_barrier((lines, table))
            phases.append(table)
        if bins < LANES:
            cut = lines.reshape(RG1, 2, -1, LANES // bins, bins)
            lines = cut.transpose(0, 3, 1, 2, 4).reshape(devices, 2, -1, bins)
        moved = lax.all_to_all(lines, axes, split_axis=0, concat_axis=0, tiled=True)
        turned.append(moved.reshape(nrng, naz, 2, len(chunks), per_part, rows_in, bins))
    transform(count - 2)
    transform(count - 1)
    lows[-3:], highs[-3:] = lows[-1:] * 3, highs[-1:] * 3
    tables = (shift_table, filter_index, tap_table)
    image, sources = None, mains
    for i, places_of in enumerate(places):
        ids = bins_of(places_of)
        wide = i == len(places) - 1
        halos = (lows, highs) if wide else ([], [])
        columns = [own_columns(bins), halo_columns(bins)] if wide else [own_columns(bins)]
        movers = [mover_table(ids, cols, *tables) for cols in columns]
        result = final(
            bins, places_of, sources, *halos, [rates[i]] if wide else phases, movers, image
        )
        image, sources = result[0], result[1:]
    return image


def solution(mesh):
    return jax.shard_map(
        functools.partial(local, mesh.shape["rng"], mesh.shape["az"]),
        mesh=mesh,
        in_specs=(
            P(None, "az", "rng"),
            P(),
            P(("rng", "az")),
            P(None, ("rng", "az")),
            P(None, ("rng", "az")),
            P(),
        ),
        out_specs=P(None, ("rng", "az"), None),
        check_vma=False,
    )
```
